32 devices in a mesh: dom: 8 (over z, y), sub: 4 (over x, core).
Axes of the slice: x: 2, y: 2, z: 4, core: 2. Of those that a mesh axis runs over, the one named last changes fastest.
Arguments:
- modal_state: float32 [56, 9, 4096], P(None, None, ('dom', 'sub')), may hold values from -6 to 6
- cluster_id: int32 [4096], P(('dom', 'sub')), may hold values 0 or 1
- jacobian_id: int32 [4096], P(('dom', 'sub')), may hold values from 0 to 63
- face_neighbour: int32 [4, 4096], P(None, ('dom', 'sub')), may hold values from 0 to 288, as said below
- flux_index: int32 [4, 4096], P(None, ('dom', 'sub')), may hold values from 0 to 11, as said below
- send_list: int32 [5120], P(('dom', 'sub')), may hold values from 0 to 511, as said below
- derivative: float32 [3, 56, 56], replicated, may hold values from -1.25 to 1.25
- stiffness: float32 [3, 56, 56], replicated, may hold values from -0.75 to 0.75
- restriction: float32 [4, 21, 56], replicated, may hold values from -0.75 to 0.75
- lifting: float32 [4, 56, 21], replicated, may hold values from -1.25 to 1.25
- orientation: float32 [3, 21, 21], replicated, may hold values from -1.25 to 1.25
- star_matrix: float32 [64, 3, 9, 9], replicated, may hold values from -2 to 2
- flux_minus: float32 [64, 4, 9, 9], replicated, may hold values from -2 to 2
- flux_plus: float32 [64, 4, 9, 9], replicated, may hold values from -2 to 2
Outputs:
- new_state: float32 [56, 9, 4096], P(None, None, ('dom', 'sub'))
The draws below stay inside these ranges and needn't reach their ends.
Inputs may be any that keep to these rules, and one draw needn't show every extreme that they name: `face_neighbour`: each device's 4 * 128 faces are all distinct between interior pairs, live ghost slots and faces without neighbour. Slot blocks are symmetric: a live ghost slot of device p for a face F pairs with the peer's slot (as in the reference program) holding the face that neighbours F, and p's own send_list entry at slot g lists F itself. Along dom the devices at both ends have empty outer blocks; some device fills a dom block of 64 slots and every dom group has two sub-blocks sharing 8 faces. For a face whose neighbour is in a ghost slot, flux_index // 3 equals the face number listed in the sender's send_list slot divided by 128. `send_list`: the first 160 faces of a permutation of each device's 4 * 128 faces; slots past a link's count list faces without a neighbour.
All inputs are finite; a program needn't handle non-finite values. No bound on the sum of `cluster_id` on one device may be relied on, other than what follows from the above.
Results may differ from the reference program's by a relative error of at most 0.0003.
Values sent between devices are 32-bit elements; how exact they have to be, the bound alone decides.
No kernel may reach another device: no remote copies, remote signals or barrier semaphores. Data moves between devices by JAX's collectives and lax.ppermute only.
A program may use at most 64 MiB of HBM per device.

```python
import math
import jax
import jax.numpy as jnp
from jax import lax

ORDER = 6
VARS = 9
BASIS = 56
FACE_BASIS = 21
NJ = 64
E_DEV = 128
CAP_DOM = 64
CAP_SUB = 8
ELEMS = 4096
N_DOM = 8
N_SUB = 4


def peer_tables_drawn():
    devices = N_DOM * N_SUB
    ghosts = 2 * CAP_DOM + N_SUB * CAP_SUB
    slot = jnp.arange(ghosts, dtype=jnp.int32)
    in_dom = slot < 2 * CAP_DOM
    upper = jnp.logical_and(slot >= CAP_DOM, in_dom)
    dom_pos = slot % CAP_DOM
    remain = jnp.maximum(slot - 2 * CAP_DOM, 0)
    target = remain // CAP_SUB
    sub_pos = remain % CAP_SUB
    device = jnp.arange(devices, dtype=jnp.int32)
    dom_of = (device // N_SUB)[:, None]
    sub_of = (device % N_SUB)[:, None]
    peer_dom = jnp.where(in_dom[None], dom_of + jnp.where(upper, 1, -1)[None], dom_of)
    peer_dom = jnp.clip(peer_dom, 0, N_DOM - 1)
    peer_sub = jnp.where(in_dom[None], sub_of, target[None])
    peer_slot = jnp.where(in_dom[None], jnp.where(upper, dom_pos, CAP_DOM + dom_pos)[None], 2 * CAP_DOM + sub_of * CAP_SUB + sub_pos[None])
    block = jnp.where(slot < CAP_DOM, 0, jnp.where(in_dom, 1, 2 + target))
    within = jnp.where(in_dom, dom_pos, sub_pos)
    return ((peer_dom * N_SUB + peer_sub).astype(jnp.int32), peer_slot.astype(jnp.int32), block.astype(jnp.int32), within.astype(jnp.int32))


def to_whole(blocked):
    devices = N_DOM * N_SUB
    return jnp.transpose(blocked.reshape(devices, 4, E_DEV), (1, 0, 2)).reshape(4, devices * E_DEV)


def build_mesh(key):
    mesh_key = jax.random.fold_in(key, 17)
    perm_key, dom_key, sub_key, turn_key = jax.random.split(mesh_key, 4)
    devices = N_DOM * N_SUB
    faces = 4 * E_DEV
    ghosts = 2 * CAP_DOM + N_SUB * CAP_SUB
    orders = jax.vmap(lambda single: jax.random.permutation(single, faces))(jax.random.split(perm_key, devices)).astype(jnp.int32)
    dom_links = jax.random.randint(dom_key, (N_DOM - 1, N_SUB), CAP_DOM // 2, CAP_DOM + 1).astype(jnp.int32)
    dom_links = dom_links.at[0, 0].set(CAP_DOM)
    edge_zeros = jnp.zeros((1, N_SUB), jnp.int32)
    padded_links = jnp.concatenate([edge_zeros, dom_links, edge_zeros], axis=0)
    raw_sub = jax.random.randint(sub_key, (N_DOM, N_SUB, N_SUB), 0, CAP_SUB + 1).astype(jnp.int32)
    sub_range = jnp.arange(N_SUB)
    sub_links = jnp.where((sub_range[:, None] < sub_range[None, :])[None], raw_sub, jnp.swapaxes(raw_sub, 1, 2))
    sub_links = jnp.where((sub_range[:, None] == sub_range[None, :])[None], 0, sub_links)
    sub_links = sub_links.at[:, 0, 1].set(CAP_SUB).at[:, 1, 0].set(CAP_SUB)
    device = jnp.arange(devices, dtype=jnp.int32)
    dom_of = device // N_SUB
    sub_of = device % N_SUB
    counts = jnp.concatenate([padded_links[dom_of, sub_of][:, None], padded_links[dom_of + 1, sub_of][:, None], sub_links[dom_of, sub_of]], axis=1)
    peer, peer_slot, block, within = peer_tables_drawn()
    block_counts = jnp.take_along_axis(counts, jnp.broadcast_to(block[None], (devices, ghosts)), axis=1)
    live = within[None, :] < block_counts
    ghost_partner = orders[peer, peer_slot]
    position = jnp.arange(faces, dtype=jnp.int32)
    inner_partner = orders[:, position ^ 1]
    partner = jnp.concatenate([ghost_partner, inner_partner[:, ghosts:]], axis=1)
    live_full = jnp.concatenate([live, jnp.ones((devices, faces - ghosts), bool)], axis=1)
    codes = jnp.where(position[None] < ghosts, jnp.where(live_full, E_DEV + position[None], E_DEV + ghosts), partner % E_DEV)
    turns = jax.random.randint(turn_key, (devices, faces), 0, 3).astype(jnp.int32)
    flux_codes = partner // E_DEV * 3 + turns
    row_ids = jnp.broadcast_to(device[:, None], (devices, faces))
    neighbour = jnp.zeros((devices, faces), jnp.int32).at[row_ids, orders].set(codes.astype(jnp.int32))
    flux_table = jnp.zeros((devices, faces), jnp.int32).at[row_ids, orders].set(flux_codes.astype(jnp.int32))
    return (to_whole(neighbour), to_whole(flux_table), orders[:, :ghosts].reshape(-1))


def draw_face_neighbour(key, part):
    return build_mesh(key)[0]


def draw_flux_index(key, part):
    return build_mesh(key)[1]


def draw_send_list(key, part):
    return build_mesh(key)[2]


def plant(drawn, key, smallest, largest):
    dims = drawn.shape
    place = [jax.random.randint(jax.random.fold_in(key, axis), (), 0, dims[axis]) for axis in range(len(dims))]
    drawn = drawn.at[tuple(place)].set(smallest)
    longest = dims.index(max(dims))
    place[longest] = (place[longest] + 1) % dims[longest]
    return drawn.at[tuple(place)].set(largest)


def block_scale(key, extent, pieces, least, largest):
    def one(dim, blocks):
        steps = jax.random.uniform(jax.random.fold_in(jax.random.fold_in(key, 6), dim), (blocks,), jnp.float32, least / len(pieces), largest / len(pieces))
        return jnp.repeat(jnp.exp(steps), extent[dim] // blocks).reshape((-1,) + (1,) * (len(extent) - dim - 1))

    loudness = one(*pieces[0])
    for cut in pieces[1:]:
        loudness = loudness * one(*cut)
    return loudness


def centred(own_key, extent, width, most, shards=(), held_as=jnp.bfloat16):
    level = block_scale(own_key, extent, shards, -0.22, 0.18) if shards else 1.0
    result = jax.random.normal(own_key, extent, jnp.float32) * width * level
    return jnp.minimum(jnp.maximum(result, -most), most).astype(held_as)


def setup_inputs(seed: int = 0) -> dict:
    arg_keys = jax.random.split(jax.random.key(seed), 15)
    modal_state = centred(arg_keys[0], (BASIS, VARS, ELEMS), 1.0, 6.0, ((2, 32),), jnp.float32)
    cluster_id = plant((jax.random.randint(arg_keys[1], (ELEMS,), 0, 3) < 1).astype(jnp.int32), jax.random.fold_in(arg_keys[1], 1), 0, 1)
    jacobian_id = plant(jax.random.randint(arg_keys[2], (ELEMS,), 0, NJ), jax.random.fold_in(arg_keys[2], 1), 0, NJ - 1).astype(jnp.int32)
    face_neighbour = draw_face_neighbour(jax.random.fold_in(arg_keys[14], 71), 0)
    flux_index = draw_flux_index(jax.random.fold_in(arg_keys[14], 71), 0)
    send_list = draw_send_list(jax.random.fold_in(arg_keys[14], 71), 0)
    derivative = centred(arg_keys[6], (3, BASIS, BASIS), (BASIS * 2 // 5) ** -0.5, 1.25, (), jnp.float32)
    stiffness = centred(arg_keys[7], (3, BASIS, BASIS), BASIS ** -0.5, 0.75, (), jnp.float32)
    restriction = centred(arg_keys[8], (4, FACE_BASIS, BASIS), BASIS ** -0.5, 0.75, (), jnp.float32)
    lifting = centred(arg_keys[9], (4, BASIS, FACE_BASIS), FACE_BASIS ** -0.5, 1.25, (), jnp.float32)
    orientation = centred(arg_keys[10], (3, FACE_BASIS, FACE_BASIS), FACE_BASIS ** -0.5, 1.25, (), jnp.float32)
    star_matrix = centred(arg_keys[11], (NJ, 3, VARS, VARS), VARS ** -0.5, 2.0, (), jnp.float32)
    flux_minus = centred(arg_keys[12], (NJ, 4, VARS, VARS), VARS ** -0.5, 2.0, (), jnp.float32)
    flux_plus = centred(arg_keys[13], (NJ, 4, VARS, VARS), VARS ** -0.5, 2.0, (), jnp.float32)
    return {"modal_state": modal_state, "cluster_id": cluster_id, "jacobian_id": jacobian_id, "face_neighbour": face_neighbour, "flux_index": flux_index, "send_list": send_list, "derivative": derivative, "stiffness": stiffness, "restriction": restriction, "lifting": lifting, "orientation": orientation, "star_matrix": star_matrix, "flux_minus": flux_minus, "flux_plus": flux_plus}


highest = lax.Precision.HIGHEST
step_length = 1.0


def peer_tables():
    devices = N_DOM * N_SUB
    ghosts = 2 * CAP_DOM + N_SUB * CAP_SUB
    slot = jnp.arange(ghosts, dtype=jnp.int32)
    in_dom = slot < 2 * CAP_DOM
    upper = jnp.logical_and(slot >= CAP_DOM, in_dom)
    dom_pos = slot % CAP_DOM
    remain = jnp.maximum(slot - 2 * CAP_DOM, 0)
    target = remain // CAP_SUB
    sub_pos = remain % CAP_SUB
    device = jnp.arange(devices, dtype=jnp.int32)
    dom_of = (device // N_SUB)[:, None]
    sub_of = (device % N_SUB)[:, None]
    peer_dom = jnp.where(in_dom[None], dom_of + jnp.where(upper, 1, -1)[None], dom_of)
    peer_dom = jnp.clip(peer_dom, 0, N_DOM - 1)
    peer_sub = jnp.where(in_dom[None], sub_of, target[None])
    peer_slot = jnp.where(in_dom[None], jnp.where(upper, dom_pos, CAP_DOM + dom_pos)[None], 2 * CAP_DOM + sub_of * CAP_SUB + sub_pos[None])
    return (peer_dom * N_SUB + peer_sub).astype(jnp.int32), peer_slot.astype(jnp.int32)


def lookup(lookup_table, indices):
    onehot = (jnp.arange(lookup_table.shape[0], dtype=jnp.int32)[:, None] == indices[None, :]).astype(lookup_table.dtype)
    return jnp.dot(lookup_table.reshape(lookup_table.shape[0], -1).T, onehot, precision=highest)


def taylor_integrals(values, star_local, derivative, spans):
    taylor_terms = [values]
    current = values
    for degree in range(ORDER - 1):
        following = jnp.zeros_like(values)
        for direction in range(3):
            moved = jnp.einsum('ab,bqe->aqe', derivative[direction], current, precision=highest)
            following = following - jnp.einsum('aqe,qpe->ape', moved, star_local[direction], precision=highest)
        taylor_terms.append(following)
        current = following
    results = []
    for begin_time, end_time in spans:
        summed = jnp.zeros_like(values)
        for degree, taylor_term in enumerate(taylor_terms):
            weight = (end_time ** (degree + 1) - begin_time ** (degree + 1)) / math.factorial(degree + 1)
            summed = summed + weight * taylor_term
        results.append(summed)
    return results


def reference(modal_state, cluster_id, jacobian_id, face_neighbour, flux_index, send_list, derivative, stiffness, restriction, lifting, orientation, star_matrix, flux_minus, flux_plus):
    devices = N_DOM * N_SUB
    elements = E_DEV
    ghosts = 2 * CAP_DOM + N_SUB * CAP_SUB
    basis = modal_state.shape[0]
    variables = modal_state.shape[1]
    peer, peer_slot = peer_tables()
    send_table = send_list.reshape(devices, ghosts)
    ghost_global = peer * elements + send_table[peer, peer_slot] % elements
    codes = face_neighbour.reshape(4, devices, elements)
    dev_index = jnp.broadcast_to(jnp.arange(devices, dtype=jnp.int32)[None, :, None], codes.shape)
    slot = jnp.clip(codes - elements, 0, ghosts - 1)
    global_nbr = jnp.where(codes < elements, dev_index * elements + codes, ghost_global[dev_index, slot])
    valid_face = codes < elements + ghosts
    global_nbr = jnp.where(valid_face, global_nbr, 0).astype(jnp.int32)
    nbr_blocks = jnp.transpose(global_nbr, (1, 0, 2))
    valid_blocks = jnp.transpose(valid_face, (1, 0, 2)).astype(modal_state.dtype)
    flux_blocks = jnp.transpose(flux_index.reshape(4, devices, elements), (1, 0, 2))
    state_blocks = jnp.transpose(modal_state.reshape(basis, variables, devices, elements), (2, 0, 1, 3))
    jac_blocks = jacobian_id.reshape(devices, elements)
    cluster_blocks = cluster_id.reshape(devices, elements)
    half = step_length / 2

    def predict_both(inputs):
        values, jac_part = inputs
        star_local = lookup(star_matrix, jac_part).reshape(3, variables, variables, elements)
        early, later = taylor_integrals(values, star_local, derivative, ((0.0, half), (half, step_length)))
        return early, later

    def predict_half(inputs):
        values, jac_part = inputs
        star_local = lookup(star_matrix, jac_part).reshape(3, variables, variables, elements)
        return taylor_integrals(values, star_local, derivative, ((0.0, half),))[0]

    def make_update(integral_all):
        def update_block(inputs):
            values, jac_part, flux_part, nbr_part, valid_part = inputs
            star_local = lookup(star_matrix, jac_part).reshape(3, variables, variables, elements)
            minus_local = lookup(flux_minus, jac_part).reshape(4, variables, variables, elements)
            plus_local = lookup(flux_plus, jac_part).reshape(4, variables, variables, elements)
            neigh = integral_all[nbr_part // elements, :, :, nbr_part % elements]
            own_face = jnp.einsum('frb,bqe->frqe', restriction, values, precision=highest)
            restrict_sel = restriction[flux_part // 3]
            nbr_face = jnp.einsum('ferb,febq->frqe', restrict_sel, neigh, precision=highest)
            nbr_face = nbr_face * valid_part[:, None, None, :]
            turn_sel = orientation[flux_part % 3]
            oriented = jnp.einsum('ferc,fcqe->frqe', turn_sel, nbr_face, precision=highest)
            combined = jnp.einsum('frqe,fqpe->frpe', own_face, minus_local, precision=highest) + jnp.einsum('frqe,fqpe->frpe', oriented, plus_local, precision=highest)
            lifted = jnp.einsum('fbr,frpe->bpe', lifting, combined, precision=highest)
            weighted = jnp.einsum('cqe,dqpe->dcpe', values, star_local, precision=highest)
            volume = jnp.einsum('dbc,dcpe->bpe', stiffness, weighted, precision=highest)
            return volume + lifted
        return update_block

    first, late = lax.map(predict_both, (state_blocks, jac_blocks))
    middle = state_blocks + lax.map(make_update(first), (first, jac_blocks, flux_blocks, nbr_blocks, valid_blocks))
    fine_half = lax.map(predict_half, (middle, jac_blocks))
    second = jnp.where((cluster_blocks == 1)[:, None, None, :], fine_half, late)
    new_blocks = middle + lax.map(make_update(second), (second, jac_blocks, flux_blocks, nbr_blocks, valid_blocks))
    return jnp.transpose(new_blocks, (1, 2, 0, 3)).reshape(basis, variables, devices * elements)
```

```python
import functools

import jax
import jax.numpy as jnp
from jax import lax
from jax.experimental import pallas as pl
from jax.experimental.pallas import tpu as pltpu
from jax.sharding import PartitionSpec as P

ORDER = 6
CAP_DOM = 64
HALF = 0.5
PAD = 24
SEC = 64

F32 = jnp.float32
BF16 = jnp.bfloat16


def split(x):
    high = x.astype(BF16)
    low = (x - high.astype(F32)).astype(BF16)
    return high, low


def dot(a, b):
    return lax.dot_general(a, b, (((1,), (0,)), ((), ())), preferred_element_type=F32)


def dot_nt(a, b):
    return lax.dot_general(a, b, (((1,), (1,)), ((), ())), preferred_element_type=F32)


def stack_left(matrix):
    m, k = matrix.shape
    wide = jnp.concatenate([matrix, jnp.zeros((m, 128 - k), F32)], axis=1)
    high = wide.astype(BF16).astype(F32)
    low = wide - high
    both = high + pltpu.roll(high, SEC, 1)
    return jnp.concatenate([both.astype(BF16), low.astype(BF16)], axis=1)[:, : 3 * SEC]


def stack_right(get, out_ref, variables):
    for q in range(variables):
        x = get(q)
        pad = jnp.zeros((SEC - x.shape[0], x.shape[1]), F32)
        high, low = split(jnp.concatenate([x, pad], axis=0))
        lanes = slice(q * 128, (q + 1) * 128)
        out_ref[0:SEC, lanes] = high
        out_ref[SEC : 2 * SEC, lanes] = low
        out_ref[2 * SEC : 3 * SEC, lanes] = high


def mix_directions(moved_ref, star_ref, basis, variables, emit):
    group = 3
    for first_p in range(0, variables, group):
        acc = [None] * group
        for q in range(variables):
            for d in range(3):
                block = moved_ref[d * basis : (d + 1) * basis, q * 128 : (q + 1) * 128]
                for i in range(group):
                    row = (q * variables + first_p + i) * 4 + d
                    term = block * star_ref[row : row + 1, :]
                    acc[i] = term if acc[i] is None else acc[i] + term
        for i in range(group):
            emit(first_p + i, acc[i])


def lookup(table_ref, stage_ref, class_row, out_ref):
    nq, np_, parts, classes = table_ref.shape
    for q in range(nq):
        for p in range(np_):
            row = (q * np_ + p) * 4
            stage_ref[row : row + parts, :classes] = table_ref[q, p]
    rows = nq * np_ * 4
    table = stage_ref[:rows, :classes]
    high, low = split(table)
    onehot = (lax.broadcasted_iota(jnp.int32, (classes, 128), 0) == class_row).astype(F32).astype(BF16)
    out_ref[:rows, :] = dot(high, onehot) + dot(low, onehot)


def predictor(x_ref, star_ref, left, xs_ref, moved_ref, first_ref, late_ref, variables):
    basis = x_ref.shape[1]
    for p in range(variables):
        x = x_ref[p]
        first_ref[p] = x * HALF
        if late_ref is not None:
            late_ref[p] = x * (1.0 - HALF)

    def step(degree, weights):
        w_half, w_full = weights
        scale = -1.0 / (degree + 2).astype(F32)
        w_half = w_half * (scale * HALF)
        w_full = w_full * scale
        stack_right(lambda q: x_ref[q], xs_ref, variables)
        moved_ref[...] = dot(left, xs_ref[...])

        def emit(p, value):
            x_ref[p] = value
            first_ref[p] += w_half * value
            if late_ref is not None:
                late_ref[p] += (w_full - w_half) * value

        mix_directions(moved_ref, star_ref, basis, variables, emit)
        return w_half, w_full

    lax.fori_loop(0, ORDER - 1, step, (jnp.float32(HALF), jnp.float32(1.0)))


def project(values_ref, restrict_ref, stage_ref, xs_ref, proj_ref, variables):
    faces, face_basis, basis = restrict_ref.shape
    stage_ref[...] = jnp.zeros_like(stage_ref)
    for f in range(faces):
        stage_ref[f * PAD : f * PAD + face_basis, :basis] = restrict_ref[f]
    left = stack_left(stage_ref[:, :basis])
    stack_right(lambda q: values_ref[q], xs_ref, variables)
    proj_ref[...] = dot(left, xs_ref[...])


def by_face(proj_ref, f, variables):
    pieces = [proj_ref[f * PAD : (f + 1) * PAD, q * 128 : (q + 1) * 128] for q in range(variables)]
    rows = variables * PAD
    extra = -rows % 16
    if extra:
        pieces.append(jnp.zeros((extra, 128), F32))
    return jnp.concatenate(pieces, axis=0)


def payloads(proj_ref, send_ref, slot_ref, outs, variables, sub_count, cap_sub):
    pa_ref, pb_ref, sub_refs = outs
    ghosts = send_ref.shape[1]
    rows = slot_ref.shape[0]
    lanes = slot_ref.shape[1]
    wide = jnp.concatenate([send_ref[...], jnp.zeros((1, -ghosts % 128), jnp.int32)], axis=1)
    column = jnp.transpose(jnp.broadcast_to(wide.astype(F32), (128, wide.shape[1])), (1, 0))[:ghosts]
    lane = lax.broadcasted_iota(jnp.int32, (ghosts, 128), 1).astype(F32)
    total = None
    for f in range(4):
        onehot = (column == lane + f * 128).astype(F32).astype(BF16)
        high, low = split(by_face(proj_ref, f, variables))
        term = dot_nt(onehot, high) + dot_nt(onehot, low)
        total = term if total is None else total + term
    used = total.shape[1]
    full = jnp.concatenate([total, jnp.zeros((ghosts, lanes - used), F32)], axis=1) if used < lanes else total
    slot_ref[0:ghosts, :] = full
    lower = slot_ref[0:CAP_DOM, :]
    upper = slot_ref[CAP_DOM : 2 * CAP_DOM, :]
    even = lax.rem(lax.axis_index("dom"), 2) == 0
    pa_ref[...] = jnp.where(even, upper, lower)
    pb_ref[...] = jnp.where(even, lower, upper)
    me = lax.axis_index("sub")
    for k in range(1, sub_count):
        start = pl.multiple_of(2 * CAP_DOM + jnp.bitwise_xor(me, k) * cap_sub, 8)
        sub_refs[k - 1][...] = slot_ref[pl.ds(start, cap_sub), :]


def ghosts_by_slot(ins, slot_ref, sub_count, cap_sub):
    ra_ref, rb_ref, sub_refs = ins
    even = lax.rem(lax.axis_index("dom"), 2) == 0
    ra, rb = ra_ref[...], rb_ref[...]
    slot_ref[0:CAP_DOM, :] = jnp.where(even, rb, ra)
    slot_ref[CAP_DOM : 2 * CAP_DOM, :] = jnp.where(even, ra, rb)
    slot_ref[2 * CAP_DOM :, :] = jnp.zeros((slot_ref.shape[0] - 2 * CAP_DOM, slot_ref.shape[1]), F32)
    me = lax.axis_index("sub")
    for k in range(1, sub_count):
        start = pl.multiple_of(2 * CAP_DOM + jnp.bitwise_xor(me, k) * cap_sub, 8)
        slot_ref[pl.ds(start, cap_sub), :] = sub_refs[k - 1][...]


def face_terms(values, mats_ref, f, variables):
    acc = [None] * variables
    for q in range(variables):
        block = values(q)
        for p in range(variables):
            row = (q * variables + p) * 4 + f
            term = block * mats_ref[row : row + 1, :]
            acc[p] = term if acc[p] is None else acc[p] + term
    return acc


def lift(comb_ref, lift_ref, stage_ref, variables):
    faces, basis, face_basis = lift_ref.shape
    rows = comb_ref.shape[0]
    stage = [jnp.concatenate([lift_ref[f], jnp.zeros((basis, PAD - face_basis), F32)], axis=1) for f in range(faces)]
    left = jnp.concatenate(stage, axis=1)
    left_high, left_low = split(left)
    high, low = split(comb_ref[...])
    return dot(left_high, high) + (dot(left_high, low) + dot(left_low, high))


def kernel_predict(variables, sub_count, cap_sub, *refs):
    (state_ref, class_ref, table_ref, deriv_ref, restrict_ref, send_ref,
     first_ref, late_ref, proj_ref, star_ref, pa_ref, pb_ref, *rest) = refs
    sub_refs, (x_ref, xs_ref, moved_ref, stage_ref, rstage_ref, slot_ref) = rest[: sub_count - 1], rest[sub_count - 1 :]
    basis = state_ref.shape[1]
    lookup(table_ref, stage_ref, class_ref[...], star_ref)
    left = stack_left(jnp.reshape(deriv_ref[...], (3 * basis, basis)))
    x_ref[...] = state_ref[...]
    predictor(x_ref, star_ref, left, xs_ref, moved_ref, first_ref, late_ref, variables)
    project(first_ref, restrict_ref, rstage_ref, xs_ref, proj_ref, variables)
    payloads(proj_ref, send_ref, slot_ref, (pa_ref, pb_ref, sub_refs), variables, sub_count, cap_sub)


def local_part(values_ref, base_ref, proj_ref, star_ref, minus_ref, code_ref, flux_ref, stiff_ref, lift_ref,
               partial_ref, gath_ref, xs_ref, moved_ref, comb_ref, stage_ref, variables):
    basis = values_ref.shape[1]
    left = stack_left(jnp.reshape(stiff_ref[...], (3 * basis, basis)))
    stack_right(lambda q: values_ref[q], xs_ref, variables)
    moved_ref[...] = dot(left, xs_ref[...])
    for f in range(4):
        rows = slice(f * PAD, (f + 1) * PAD)
        acc = face_terms(lambda q: proj_ref[rows, q * 128 : (q + 1) * 128], minus_ref, f, variables)
        for p in range(variables):
            comb_ref[rows, p * 128 : (p + 1) * 128] = acc[p]
    lifted = lift(comb_ref, lift_ref, stage_ref, variables)

    def emit(p, value):
        partial_ref[p] = base_ref[p] + (value + lifted[:, p * 128 : (p + 1) * 128])

    mix_directions(moved_ref, star_ref, basis, variables, emit)
    rows = variables * PAD
    total = None
    code = code_ref[...]
    flux = flux_ref[...]
    face = (flux >= 3).astype(jnp.int32) + (flux >= 6).astype(jnp.int32) + (flux >= 9).astype(jnp.int32)
    target = jnp.where(code < 128, face * 128 + code, -1)
    place = lax.broadcasted_iota(jnp.int32, (128, 128), 0)
    for j in range(4):
        pick = jnp.concatenate(
            [(place + j * 128 == target[f : f + 1, :]).astype(F32).astype(BF16) for f in range(4)], axis=1
        )
        high, low = split(by_face(proj_ref, j, variables))
        term = dot(high, pick) + dot(low, pick)
        total = term if total is None else total + term
    gath_ref[...] = total[:rows]


def kernel_local(variables, with_lookup, *refs):
    if with_lookup:
        (class_ref, minus_table, plus_table, values_ref, base_ref, proj_ref, star_ref, code_ref, flux_ref, stiff_ref,
         lift_ref, partial_ref, gath_ref, minus_ref, plus_ref, xs_ref, moved_ref, comb_ref, stage_ref) = refs
        lookup(minus_table, stage_ref, class_ref[...], minus_ref)
        lookup(plus_table, stage_ref, class_ref[...], plus_ref)
    else:
        (values_ref, base_ref, proj_ref, star_ref, minus_ref, code_ref, flux_ref, stiff_ref, lift_ref,
         partial_ref, gath_ref, xs_ref, moved_ref, comb_ref, stage_ref) = refs
    local_part(values_ref, base_ref, proj_ref, star_ref, minus_ref, code_ref, flux_ref, stiff_ref, lift_ref,
               partial_ref, gath_ref, xs_ref, moved_ref, comb_ref, stage_ref, variables)


def neighbour_part(ins, code_ref, flux_ref, gath_ref, partial_ref, plus_ref, orient_ref, lift_ref, out_ref,
                   slot_ref, turned_ref, comb_ref, stage_ref, variables, sub_count, cap_sub):
    ghosts_by_slot(ins, slot_ref, sub_count, cap_sub)
    by_value = jnp.transpose(slot_ref[...], (1, 0))
    rows = variables * PAD
    high, low = split(by_value[:rows])
    code = code_ref[...]
    flux = flux_ref[...]
    slots = slot_ref.shape[0]
    place = lax.broadcasted_iota(jnp.int32, (slots, 128), 0) + 128
    pick = jnp.concatenate([(place == code[f : f + 1, :]).astype(F32).astype(BF16) for f in range(4)], axis=1)
    gathered = gath_ref[...] + (dot(high, pick) + dot(low, pick))
    face_basis = orient_ref.shape[1]
    orient = []
    for h in range(3):
        orient.append(jnp.concatenate([orient_ref[h], jnp.zeros((PAD - face_basis, face_basis), F32)], axis=0))
    orient = jnp.concatenate(orient, axis=0)
    orient = jnp.concatenate([orient, jnp.zeros((3 * PAD, PAD - face_basis), F32)], axis=1)
    o_high, o_low = split(orient)
    turn = flux - 3 * (
        (flux >= 3).astype(jnp.int32) + (flux >= 6).astype(jnp.int32) + (flux >= 9).astype(jnp.int32)
    )
    for q in range(variables):
        g_high, g_low = split(gathered[q * PAD : (q + 1) * PAD])
        turned = dot(o_high, g_high) + (dot(o_high, g_low) + dot(o_low, g_high))
        for f in range(4):
            lanes = slice(f * 128, (f + 1) * 128)
            pick_turn = turn[f : f + 1, :]
            value = jnp.where(
                pick_turn == 0,
                turned[0:PAD, lanes],
                jnp.where(pick_turn == 1, turned[PAD : 2 * PAD, lanes], turned[2 * PAD :, lanes]),
            )
            turned_ref[f * PAD : (f + 1) * PAD, q * 128 : (q + 1) * 128] = value
    for f in range(4):
        frows = slice(f * PAD, (f + 1) * PAD)
        acc = face_terms(lambda q: turned_ref[frows, q * 128 : (q + 1) * 128], plus_ref, f, variables)
        for p in range(variables):
            comb_ref[frows, p * 128 : (p + 1) * 128] = acc[p]
    lifted = lift(comb_ref, lift_ref, stage_ref, variables)
    for p in range(variables):
        out_ref[p] = partial_ref[p] + lifted[:, p * 128 : (p + 1) * 128]


def kernel_second(variables, sub_count, cap_sub, *refs):
    ra_ref, rb_ref, *rest = refs
    rsub, rest = rest[: sub_count - 1], rest[sub_count - 1 :]
    (code_ref, flux_ref, gath_ref, partial_ref, plus_ref, star_ref, late_ref, cluster_ref, orient_ref, lift_ref,
     deriv_ref, restrict_ref, send_ref, middle_ref, second_ref, proj_ref, pa_ref, pb_ref, *rest) = rest
    sub_refs, rest = rest[: sub_count - 1], rest[sub_count - 1 :]
    x_ref, xs_ref, moved_ref, stage_ref, rstage_ref, slot_ref, pslot_ref, turned_ref, comb_ref = rest
    neighbour_part((ra_ref, rb_ref, rsub), code_ref, flux_ref, gath_ref, partial_ref, plus_ref, orient_ref, lift_ref,
                   middle_ref, slot_ref, turned_ref, comb_ref, stage_ref, variables, sub_count, cap_sub)
    basis = middle_ref.shape[1]
    left = stack_left(jnp.reshape(deriv_ref[...], (3 * basis, basis)))
    x_ref[...] = middle_ref[...]
    predictor(x_ref, star_ref, left, xs_ref, moved_ref, second_ref, None, variables)
    fine = cluster_ref[...] == 1
    for p in range(variables):
        second_ref[p] = jnp.where(fine, second_ref[p], late_ref[p])
    project(second_ref, restrict_ref, rstage_ref, xs_ref, proj_ref, variables)
    payloads(proj_ref, send_ref, pslot_ref, (pa_ref, pb_ref, sub_refs), variables, sub_count, cap_sub)


def kernel_last(variables, sub_count, cap_sub, *refs):
    ra_ref, rb_ref, *rest = refs
    rsub, rest = rest[: sub_count - 1], rest[sub_count - 1 :]
    (code_ref, flux_ref, gath_ref, partial_ref, plus_ref, orient_ref, lift_ref, out_ref,
     slot_ref, turned_ref, comb_ref, stage_ref) = rest
    neighbour_part((ra_ref, rb_ref, rsub), code_ref, flux_ref, gath_ref, partial_ref, plus_ref, orient_ref, lift_ref,
                   out_ref, slot_ref, turned_ref, comb_ref, stage_ref, variables, sub_count, cap_sub)


def body(
    dom_count,
    sub_count,
    modal_state,
    cluster_id,
    jacobian_id,
    face_neighbour,
    flux_index,
    send_list,
    derivative,
    stiffness,
    restriction,
    lifting,
    orientation,
    star_matrix,
    flux_minus,
    flux_plus,
):
    basis, variables, elements = modal_state.shape
    ghosts = send_list.shape[0]
    cap_sub = (ghosts - 2 * CAP_DOM) // sub_count
    lanes = variables * elements
    payload_lanes = -(-variables * PAD // 128) * 128
    mat_rows = variables * variables * 4 + 4
    slots = -(-(ghosts + 1) // 128) * 128

    state = jnp.transpose(modal_state, (1, 0, 2))
    star_table = jnp.transpose(star_matrix, (2, 3, 1, 0))
    minus_table = jnp.transpose(flux_minus, (2, 3, 1, 0))
    plus_table = jnp.transpose(flux_plus, (2, 3, 1, 0))
    classes = jacobian_id.reshape(1, elements)
    clusters = cluster_id.reshape(1, elements)
    sends = send_list.reshape(1, ghosts)

    def sds(*shape, dtype=F32):
        return jax.ShapeDtypeStruct(shape, dtype)

    whole = sds(variables, basis, elements)
    proj_t = sds(4 * PAD, lanes)
    mat_t = sds(mat_rows, 128)
    pay_t = [sds(CAP_DOM, payload_lanes)] * 2 + [sds(cap_sub, payload_lanes)] * (sub_count - 1)
    gath_t = sds(variables * PAD, 4 * elements)
    x_s = pltpu.VMEM((variables, basis, elements), F32)
    xs_s = pltpu.VMEM((3 * SEC, lanes), BF16)
    moved_s = pltpu.VMEM((3 * basis, lanes), F32)
    stage_s = pltpu.VMEM((mat_rows, 128), F32)
    rstage_s = pltpu.VMEM((4 * PAD, 128), F32)
    slot_s = pltpu.VMEM((slots, payload_lanes), F32)
    pslot_s = pltpu.VMEM((ghosts, payload_lanes), F32)
    face_s = pltpu.VMEM((4 * PAD, lanes), F32)

    def call(fn, outs, scratch, operands, flops):
        vmem = pl.BlockSpec(memory_space=pltpu.VMEM)
        return pl.pallas_call(
            fn,
            out_shape=outs,
            in_specs=[vmem] * len(operands),
            out_specs=jax.tree.map(lambda _: vmem, outs),
            scratch_shapes=scratch,
            cost_estimate=pl.CostEstimate(flops=flops, bytes_accessed=2_000_000, transcendentals=0),
            compiler_params=pltpu.CompilerParams(vmem_limit_bytes=24 * 1024 * 1024),
        )(*operands)

    combined = ("dom", "sub")

    def device(d, s):
        return d * sub_count + s

    def pairs(target):
        return [
            (device(d, s), device(*target(d, s))) for d in range(dom_count) for s in range(sub_count)
        ]

    even_pairs = pairs(lambda d, s: (d ^ 1, s))
    odd_pairs = pairs(lambda d, s: (((d + 1) ^ 1) - 1, s) if 0 < d < dom_count - 1 else (d, s ^ 1))

    def trade(payload):
        pa, pb, *subs = payload
        ra = lax.ppermute(pa, combined, even_pairs)
        rb = lax.ppermute(pb, combined, odd_pairs)
        rs = [
            lax.ppermute(part, combined, pairs(lambda d, s: (d, s ^ k)))
            for k, part in zip(range(1, sub_count), subs)
        ]
        return [ra, rb, *rs]

    first, late, proj, star, *payload = call(
        functools.partial(kernel_predict, variables, sub_count, cap_sub),
        [whole, whole, proj_t, mat_t] + pay_t,
        [x_s, xs_s, moved_s, stage_s, rstage_s, pslot_s],
        [state, classes, star_table, derivative, restriction, sends],
        60_000_000,
    )
    received = trade(payload)
    partial, gath, minus, plus = call(
        functools.partial(kernel_local, variables, True),
        [whole, gath_t, mat_t, mat_t],
        [xs_s, moved_s, face_s, stage_s],
        [classes, minus_table, plus_table, first, state, proj, star, face_neighbour, flux_index, stiffness, lifting],
        30_000_000,
    )
    middle, second, proj, *payload = call(
        functools.partial(kernel_second, variables, sub_count, cap_sub),
        [whole, whole, proj_t] + pay_t,
        [x_s, xs_s, moved_s, stage_s, rstage_s, slot_s, pslot_s, face_s, face_s],
        received
        + [face_neighbour, flux_index, gath, partial, plus, star, late, clusters, orientation, lifting]
        + [derivative, restriction, sends],
        70_000_000,
    )
    received = trade(payload)
    partial, gath = call(
        functools.partial(kernel_local, variables, False),
        [whole, gath_t],
        [xs_s, moved_s, face_s, stage_s],
        [second, middle, proj, star, minus, face_neighbour, flux_index, stiffness, lifting],
        30_000_000,
    )
    result = call(
        functools.partial(kernel_last, variables, sub_count, cap_sub),
        whole,
        [slot_s, face_s, face_s, stage_s],
        received + [face_neighbour, flux_index, gath, partial, plus, orientation, lifting],
        10_000_000,
    )
    return jnp.transpose(result, (1, 0, 2))


def solution(mesh):
    placed = (
        P(None, None, ("dom", "sub")),
        P(("dom", "sub")),
        P(("dom", "sub")),
        P(None, ("dom", "sub")),
        P(None, ("dom", "sub")),
        P(("dom", "sub")),
        P(),
        P(),
        P(),
        P(),
        P(),
        P(),
        P(),
        P(),
    )
    return jax.shard_map(
        functools.partial(body, mesh.shape["dom"], mesh.shape["sub"]),
        mesh=mesh,
        in_specs=placed,
        out_specs=P(None, None, ("dom", "sub")),
        check_vma=False,
    )
```

```python
import collections
import functools

import jax
import jax.numpy as jnp
from jax import lax
from jax.experimental import pallas as pl
from jax.experimental.pallas import tpu as pltpu
from jax.sharding import PartitionSpec as P

ORDER = 6
CAP_DOM = 64
HALF = 0.5
PAD = 24
SEC = 64
OSEC = 32
GROUP = 3

F32 = jnp.float32
BF16 = jnp.bfloat16
I32 = jnp.int32

Sizes = collections.namedtuple(
    "Sizes", ["variables", "basis", "sub_count", "cap_sub", "rows", "half_rows"]
)


def split(x):
    high = x.astype(BF16)
    low = (x - high.astype(F32)).astype(BF16)
    return high, low


def dot(a, b):
    return lax.dot_general(a, b, (((1,), (0,)), ((), ())), preferred_element_type=F32)


def dot_nt(a, b):
    return lax.dot_general(a, b, (((1,), (1,)), ((), ())), preferred_element_type=F32)


def pad_to(x, rows, lanes):
    m, k = x.shape
    if lanes > k:
        x = jnp.concatenate([x, jnp.zeros((m, lanes - k), x.dtype)], axis=1)
    if rows > m:
        x = jnp.concatenate([x, jnp.zeros((rows - m, lanes), x.dtype)], axis=0)
    return x


def stack_left(matrix):
    m = -(-matrix.shape[0] // 16) * 16
    wide = pad_to(matrix, m, 128)
    high = wide.astype(BF16).astype(F32)
    low = wide - high
    both = high + pltpu.roll(high, SEC, 1)
    return jnp.concatenate([both.astype(BF16), low.astype(BF16)], axis=1)[:, : 3 * SEC]


def stack_right(blocks):
    out = []
    for x in blocks:
        high, low = split(pad_to(x, SEC, x.shape[1]))
        out.append(jnp.concatenate([high, low, high], axis=0))
    return jnp.concatenate(out, axis=1) if len(out) > 1 else out[0]


def mix_group(moved_ref, star_ref, sizes, g):
    basis, variables = sizes.basis, sizes.variables
    acc = [None] * GROUP
    for q in range(variables):
        for d in range(3):
            block = moved_ref[d * basis : (d + 1) * basis, q * 128 : (q + 1) * 128]
            for i in range(GROUP):
                row = (q * variables + g * GROUP + i) * 4 + d
                term = block * star_ref[row : row + 1, :]
                acc[i] = term if acc[i] is None else acc[i] + term
    return acc


def lookup(table_ref, stage_ref, class_row, out_ref):
    nq, np_, parts, classes = table_ref.shape
    for q in range(nq):
        for p in range(np_):
            row = (q * np_ + p) * 4
            stage_ref[row : row + parts, :classes] = table_ref[q, p]
    rows = stage_ref.shape[0]
    high, low = split(stage_ref[:, :classes])
    onehot = (lax.broadcasted_iota(I32, (classes, 128), 0) == class_row).astype(F32).astype(BF16)
    out_ref[0:rows, :] = dot(high, onehot) + dot(low, onehot)


def groups(sizes):
    return range(sizes.variables // GROUP)


def group_lanes(g):
    return slice(g * GROUP * 128, (g + 1) * GROUP * 128)


def advance(src_ref, dst_ref, star_ref, left, sizes, emit):
    for g in groups(sizes):
        acc = mix_group(src_ref, star_ref, sizes, g)
        for i in range(GROUP):
            emit(g * GROUP + i, acc[i])
        dst_ref[:, group_lanes(g)] = dot(left, stack_right(acc))[: dst_ref.shape[0]]


def predictor(moved_ref, other_ref, star_ref, left, first_ref, late_ref, sizes, finish):
    def weigh(weights, degree):
        w_half, w_full = weights
        scale = -1.0 / (degree + 1).astype(F32)
        return w_half * (scale * HALF), w_full * scale

    def emitter(weights):
        w_half, w_full = weights

        def emit(p, value):
            first_ref[p] += w_half * value
            if late_ref is not None:
                late_ref[p] += (w_full - w_half) * value

        return emit

    def two(i, weights):
        weights = weigh(weights, 2 * i + 1)
        advance(moved_ref, other_ref, star_ref, left, sizes, emitter(weights))
        weights = weigh(weights, 2 * i + 2)
        advance(other_ref, moved_ref, star_ref, left, sizes, emitter(weights))
        return weights

    steps = ORDER - 1
    weights = lax.fori_loop(0, steps // 2, two, (jnp.float32(HALF), jnp.float32(1.0)))
    w_half, w_full = weigh(weights, jnp.int32(steps))
    for g in groups(sizes):
        acc = mix_group(moved_ref, star_ref, sizes, g)
        values = []
        for i in range(GROUP):
            p = g * GROUP + i
            first = first_ref[p] + w_half * acc[i]
            if late_ref is not None:
                late_ref[p] += (w_full - w_half) * acc[i]
            values.append(finish(p, first))
        yield g, values


def project(g, values, left, proj_ref):
    proj_ref[:, group_lanes(g)] = dot(left, stack_right(values))


def by_face(proj_ref, faces_ref, sizes):
    rows = sizes.rows
    for f in range(4):
        pieces = [
            proj_ref[f * PAD : (f + 1) * PAD, q * 128 : (q + 1) * 128] for q in range(sizes.variables)
        ]
        high, low = split(pad_to(jnp.concatenate(pieces, axis=0), rows, 128))
        faces_ref[0:rows, f * 128 : (f + 1) * 128] = high
        faces_ref[rows : 2 * rows, f * 128 : (f + 1) * 128] = low


def is_even():
    return lax.rem(lax.axis_index("dom"), 2) == 0


def low_lanes(shape):
    return lax.broadcasted_iota(I32, shape, 1) < CAP_DOM


def picks_of_sends(send_ref, pick_ref, pick_sub_ref):
    ghosts = send_ref.shape[1]
    row = send_ref[...].astype(F32)
    dom_row = row[:, 0:128]
    dom_row = jnp.where(is_even(), pltpu.roll(dom_row, CAP_DOM, 1), dom_row)
    place = lax.broadcasted_iota(I32, (128, 128), 0).astype(F32)
    for f in range(4):
        pick_ref[f * 128 : (f + 1) * 128, :] = (place + f * 128 == dom_row).astype(F32).astype(BF16)
    subs = ghosts - 128
    sub_row = pad_to(row[:, 128:], 1, 128)
    column = jnp.transpose(jnp.broadcast_to(sub_row, (128, 128)), (1, 0))[:subs]
    lane = lax.broadcasted_iota(I32, (subs, 128), 1).astype(F32)
    for f in range(4):
        pick_sub_ref[:, f * 128 : (f + 1) * 128] = (column == lane + f * 128).astype(F32).astype(BF16)


def payloads(faces_ref, pick_ref, pick_sub_ref, slot_ref, outs, sizes):
    pa_ref, pb_ref, p1_ref, pk_refs = outs
    rows, half = sizes.rows, sizes.half_rows
    sub = dot_nt(pick_sub_ref[...], faces_ref[0:rows, :]) + dot_nt(pick_sub_ref[...], faces_ref[rows : 2 * rows, :])
    slot_ref[...] = pad_to(sub, sub.shape[0], slot_ref.shape[1])
    both = dot(faces_ref[...], pick_ref[...])
    both = both[0:rows] + both[rows : 2 * rows]
    top, bottom = both[0:half], both[half:]
    low = low_lanes((half, 128))
    pa_ref[...] = jnp.where(low, top, pltpu.roll(bottom, CAP_DOM, 1))
    pb_ref[...] = jnp.where(low, pltpu.roll(top, CAP_DOM, 1), bottom)
    me = lax.axis_index("sub")
    cap = sizes.cap_sub

    def block(k):
        return slot_ref[pl.ds(pl.multiple_of(jnp.bitwise_xor(me, k) * cap, 8), cap), :]

    p1_ref[0:cap, :] = block(1)
    for i, k in enumerate(range(2, sizes.sub_count, 2)):
        p1_ref[(i + 1) * cap : (i + 2) * cap, :] = block(k + 1)
        pk_refs[i][...] = block(k)


def unpack(ins, slot_ref, sizes):
    ra_ref, rb_ref, r1_ref, rk_refs = ins
    ra, rb = ra_ref[...], rb_ref[...]
    low = low_lanes(ra.shape)
    top = jnp.where(low, ra, pltpu.roll(rb, CAP_DOM, 1))
    bottom = jnp.where(low, pltpu.roll(ra, CAP_DOM, 1), rb)
    dom = jnp.concatenate([top, bottom], axis=0)
    me = lax.axis_index("sub")
    cap = sizes.cap_sub
    slot_ref[...] = jnp.zeros_like(slot_ref)

    def put(k, value):
        slot_ref[pl.ds(pl.multiple_of(jnp.bitwise_xor(me, k) * cap, 8), cap), :] = value

    put(1, r1_ref[0:cap, :])
    for i, k in enumerate(range(2, sizes.sub_count, 2)):
        put(k, rk_refs[i][0:cap, :])
        put(k + 1, rk_refs[i][cap : 2 * cap, :])
    sub = jnp.transpose(slot_ref[...], (1, 0))[: dom.shape[0]]
    return jnp.concatenate([dom, sub], axis=1)


def turn_blocks(values, left, turns):
    out = []
    for value in values:
        high, low = split(pad_to(value, OSEC, value.shape[1]))
        turned = dot(left, jnp.concatenate([high, low, high], axis=0))
        out.append(
            jnp.where(
                turns == 0,
                turned[0:PAD],
                jnp.where(turns == 1, turned[PAD : 2 * PAD], turned[2 * PAD : 3 * PAD]),
            )
        )
    return out


def orient_left(orient_ref):
    blocks = [pad_to(orient_ref[h], PAD, 128) for h in range(3)]
    wide = pad_to(jnp.concatenate(blocks, axis=0), 80, 128)
    high = wide.astype(BF16).astype(F32)
    low = wide - high
    stacked = high + pltpu.roll(high, OSEC, 1) + pltpu.roll(low, 2 * OSEC, 1)
    return stacked.astype(BF16)[:, : 3 * OSEC]


def face_of(flux):
    return (flux >= 3).astype(I32) + (flux >= 6).astype(I32) + (flux >= 9).astype(I32)


def kernel_predict(sizes, *refs):
    xs = sizes.sub_count // 2 - 1
    (state_hbm, class_hbm, table_hbm, deriv_hbm, restrict_hbm, send_hbm, *later_hbm) = refs[:14]
    refs = refs[14:]
    class_ref, refs = refs[0], refs[1:]
    later_refs, refs = refs[:8], refs[8:]
    (state_ref, first_ref, late_ref, proj_ref, faces_ref, star_ref, dleft_ref, rleft_ref, pick_ref, pick_sub_ref,
     pa_ref, pb_ref, p1_ref, *rest) = refs
    pk_refs, rest = rest[:xs], rest[xs:]
    (table_ref, deriv_ref, restrict_ref, send_ref, moved_ref, other_ref, stage_ref, rstage_ref, slot_ref,
     sems) = rest
    sources = [class_hbm, table_hbm, deriv_hbm, state_hbm, send_hbm, restrict_hbm, *later_hbm]
    targets = [class_ref, table_ref, deriv_ref, state_ref, send_ref, restrict_ref, *later_refs]
    copies = [pltpu.make_async_copy(s, t, sems.at[i]) for i, (s, t) in enumerate(zip(sources, targets))]
    for copy in copies:
        copy.start()
    variables, basis = sizes.variables, sizes.basis
    copies[0].wait()
    copies[1].wait()
    lookup(table_ref, stage_ref, class_ref[...], star_ref)
    copies[2].wait()
    dleft_ref[...] = stack_left(jnp.reshape(deriv_ref[...], (3 * basis, basis)))
    left = dleft_ref[...]
    copies[3].wait()
    for g in groups(sizes):
        values = [state_ref[g * GROUP + i] for i in range(GROUP)]
        moved_ref[:, group_lanes(g)] = dot(left, stack_right(values))[: moved_ref.shape[0]]
        for i in range(GROUP):
            first_ref[g * GROUP + i] = values[i] * HALF
            late_ref[g * GROUP + i] = values[i] * (1.0 - HALF)
    copies[4].wait()
    picks_of_sends(send_ref, pick_ref, pick_sub_ref)
    copies[5].wait()
    faces, face_basis = 4, restrict_ref.shape[0]
    rstage_ref[...] = jnp.zeros_like(rstage_ref)
    for f in range(faces):
        rstage_ref[f * PAD : f * PAD + face_basis, :basis] = restrict_ref[:, f, :]
    rleft_ref[...] = stack_left(rstage_ref[:, :basis])

    def finish(p, first):
        first_ref[p] = first
        return first

    for g, values in predictor(moved_ref, other_ref, star_ref, left, first_ref, late_ref, sizes, finish):
        project(g, values, rleft_ref[...], proj_ref)
    by_face(proj_ref, faces_ref, sizes)
    payloads(faces_ref, pick_ref, pick_sub_ref, slot_ref, (pa_ref, pb_ref, p1_ref, pk_refs), sizes)
    for copy in copies[6:]:
        copy.wait()


def volume_part(values_ref, base_ref, star_ref, kleft, moved_ref, partial_ref, sizes):
    for g in groups(sizes):
        values = [values_ref[g * GROUP + i] for i in range(GROUP)]
        moved_ref[:, group_lanes(g)] = dot(kleft, stack_right(values))[: moved_ref.shape[0]]
    for g in groups(sizes):
        acc = mix_group(moved_ref, star_ref, sizes, g)
        for i in range(GROUP):
            partial_ref[g * GROUP + i] = base_ref[g * GROUP + i] + acc[i]


def interior_part(faces_ref, pick_ref, oleft, turn, gath_ref, sizes):
    rows = sizes.rows
    both = dot(faces_ref[...], pick_ref[...])
    both = both[0:rows] + both[rows : 2 * rows]
    blocks = [both[q * PAD : (q + 1) * PAD] for q in range(sizes.variables)]
    for q, block in enumerate(turn_blocks(blocks, oleft, turn)):
        gath_ref[q * PAD : (q + 1) * PAD, :] = block


def own_part(proj_ref, minus_ref, comb_ref, sizes):
    variables = sizes.variables
    for f in range(4):
        rows = slice(f * PAD, (f + 1) * PAD)
        acc = [None] * variables
        for q in range(variables):
            block = proj_ref[rows, q * 128 : (q + 1) * 128]
            for p in range(variables):
                row = (q * variables + p) * 4 + f
                term = block * minus_ref[row : row + 1, :]
                acc[p] = term if acc[p] is None else acc[p] + term
        for p in range(variables):
            comb_ref[rows, p * 128 : (p + 1) * 128] = acc[p]


def kernel_local_first(sizes, *refs):
    (class_ref, minus_table, plus_table, code_ref, flux_ref, stiff_ref, lift_ref, orient_ref,
     first_ref, state_ref, star_ref, proj_ref, faces_ref,
     partial_ref, gath_ref, comb_ref, minus_ref, plus_ref, kleft_ref, oleft_ref, lleft_ref, llow_ref,
     pick_ref, ghost_pick_ref, turn_ref, ghost_turn_ref, moved_ref, stage_ref, lstage_ref) = refs
    basis = sizes.basis
    kleft_ref[...] = stack_left(jnp.reshape(stiff_ref[...], (3 * basis, basis)))
    volume_part(first_ref, state_ref, star_ref, kleft_ref[...], moved_ref, partial_ref, sizes)
    lookup(minus_table, stage_ref, class_ref[...], minus_ref)
    oleft_ref[...] = orient_left(orient_ref)
    code = code_ref[...]
    flux = flux_ref[...]
    face = face_of(flux)
    turn = flux - 3 * face
    turn_row = jnp.concatenate([turn[f : f + 1, :] for f in range(4)], axis=1)
    turn_ref[...] = turn_row
    place = lax.broadcasted_iota(I32, (128, 128), 0)
    target = jnp.where(code < 128, face * 128 + code, -1)
    for f in range(4):
        for j in range(4):
            pick_ref[j * 128 : (j + 1) * 128, f * 128 : (f + 1) * 128] = (
                (place + j * 128 == target[f : f + 1, :]).astype(F32).astype(BF16)
            )
    slot = code - 128
    swapped = jnp.where(slot < CAP_DOM, slot + CAP_DOM, jnp.where(slot < 2 * CAP_DOM, slot - CAP_DOM, slot))
    slot = jnp.where(is_even(), swapped, slot)
    slot = jnp.where(code < 128, -1, slot)
    for f in range(4):
        for j in range(2):
            ghost_pick_ref[j * 128 : (j + 1) * 128, f * 128 : (f + 1) * 128] = (
                (place + j * 128 == slot[f : f + 1, :]).astype(F32).astype(BF16)
            )
    rows = jnp.broadcast_to(turn_row.astype(F32), (16, 512)).astype(BF16)
    ghost_turn_ref[...] = dot_nt(rows, ghost_pick_ref[...])[0:1].astype(I32)
    interior_part(faces_ref, pick_ref, oleft_ref[...], turn_row, gath_ref, sizes)
    own_part(proj_ref, minus_ref, comb_ref, sizes)
    lookup(plus_table, stage_ref, class_ref[...], plus_ref)
    lstage_ref[...] = jnp.zeros_like(lstage_ref)
    for f in range(4):
        lstage_ref[f * PAD : f * PAD + lift_ref.shape[0], :basis] = lift_ref[:, f, :]
    wide = jnp.transpose(lstage_ref[...], (1, 0))[:64]
    high = wide.astype(BF16).astype(F32)
    low = wide - high
    rolled = pltpu.roll(high, 4 * PAD, 1)
    lane = lax.broadcasted_iota(I32, (64, 128), 1)
    lleft_ref[:, 0:128] = jnp.where(lane < 4 * PAD, high, rolled).astype(BF16)
    lleft_ref[:, 128:256] = jnp.where(lane < 8 * PAD - 128, rolled, 0.0).astype(BF16)
    llow_ref[...] = low.astype(BF16)


def kernel_local_second(sizes, *refs):
    (second_ref, middle_ref, star_ref, kleft_ref, proj_ref, faces_ref, minus_ref, oleft_ref, pick_ref, turn_ref,
     partial_ref, gath_ref, comb_ref, moved_ref) = refs
    volume_part(second_ref, middle_ref, star_ref, kleft_ref[...], moved_ref, partial_ref, sizes)
    interior_part(faces_ref, pick_ref, oleft_ref[...], turn_ref[...], gath_ref, sizes)
    own_part(proj_ref, minus_ref, comb_ref, sizes)


def neighbour_part(ins, oleft_ref, ghost_turn_ref, ghost_pick_ref, gath_ref, comb_ref, plus_ref, lleft_ref, llow_ref,
                   partial_ref, slot_ref, ghost_ref, gsum_ref, sizes):
    variables, basis, rows = sizes.variables, sizes.basis, sizes.rows
    received = unpack(ins, slot_ref, sizes)
    blocks = [received[q * PAD : (q + 1) * PAD] for q in range(variables)]
    turned = turn_blocks(blocks, oleft_ref[...], ghost_turn_ref[...])
    high, low = split(pad_to(jnp.concatenate(turned, axis=0), rows, turned[0].shape[1]))
    ghost_ref[0:rows, :] = high
    ghost_ref[rows : 2 * rows, :] = low
    both = dot(ghost_ref[...], ghost_pick_ref[...])
    used = variables * PAD
    gsum_ref[...] = gath_ref[...] + (both[0:used] + both[rows : rows + used])
    for g in groups(sizes):
        highs, stacks = [], []
        faces = [[], [], []]
        for f in range(4):
            frows = slice(f * PAD, (f + 1) * PAD)
            acc = []
            for i in range(GROUP):
                p = g * GROUP + i
                acc.append(comb_ref[frows, p * 128 : (p + 1) * 128])
            for q in range(variables):
                block = gsum_ref[q * PAD : (q + 1) * PAD, f * 128 : (f + 1) * 128]
                for i in range(GROUP):
                    row = (q * variables + g * GROUP + i) * 4 + f
                    acc[i] = acc[i] + block * plus_ref[row : row + 1, :]
            for i in range(GROUP):
                faces[i].append(acc[i])
        for i in range(GROUP):
            high, low = split(jnp.concatenate(faces[i], axis=0))
            highs.append(high)
            stacks.append(jnp.concatenate([high, low], axis=0))
        lifted = dot(lleft_ref[:, : 8 * PAD], jnp.concatenate(stacks, axis=1)) + dot(
            llow_ref[:, : 4 * PAD], jnp.concatenate(highs, axis=1)
        )
        yield g, [
            partial_ref[g * GROUP + i] + lifted[:basis, i * 128 : (i + 1) * 128] for i in range(GROUP)
        ]


def kernel_second(sizes, *refs):
    xs = sizes.sub_count // 2 - 1
    ra_ref, rb_ref, r1_ref, *refs = refs
    rk_refs, refs = refs[:xs], refs[xs:]
    (oleft_ref, ghost_turn_ref, ghost_pick_ref, gath_ref, comb_ref, plus_ref, lleft_ref, llow_ref, partial_ref,
     star_ref, late_ref, cluster_ref, dleft_ref, rleft_ref, pick_ref, pick_sub_ref,
     middle_ref, second_ref, proj_ref, faces_ref, pa_ref, pb_ref, p1_ref, *rest) = refs
    pk_refs, rest = rest[:xs], rest[xs:]
    moved_ref, other_ref, slot_ref, pslot_ref, ghost_ref, gsum_ref = rest
    left = dleft_ref[...]
    for g, values in neighbour_part((ra_ref, rb_ref, r1_ref, rk_refs), oleft_ref, ghost_turn_ref, ghost_pick_ref,
                                    gath_ref, comb_ref, plus_ref, lleft_ref, llow_ref, partial_ref, slot_ref,
                                    ghost_ref, gsum_ref, sizes):
        moved_ref[:, group_lanes(g)] = dot(left, stack_right(values))[: moved_ref.shape[0]]
        for i in range(GROUP):
            middle_ref[g * GROUP + i] = values[i]
            second_ref[g * GROUP + i] = values[i] * HALF
    fine = cluster_ref[...] == 1

    def finish(p, first):
        value = jnp.where(fine, first, late_ref[p])
        second_ref[p] = value
        return value

    for g, values in predictor(moved_ref, other_ref, star_ref, left, second_ref, None, sizes, finish):
        project(g, values, rleft_ref[...], proj_ref)
    by_face(proj_ref, faces_ref, sizes)
    payloads(faces_ref, pick_ref, pick_sub_ref, pslot_ref, (pa_ref, pb_ref, p1_ref, pk_refs), sizes)


def kernel_last(sizes, *refs):
    xs = sizes.sub_count // 2 - 1
    ra_ref, rb_ref, r1_ref, *refs = refs
    rk_refs, refs = refs[:xs], refs[xs:]
    (oleft_ref, ghost_turn_ref, ghost_pick_ref, gath_ref, comb_ref, plus_ref, lleft_ref, llow_ref, partial_ref,
     out_ref, slot_ref, ghost_ref, gsum_ref) = refs
    for g, values in neighbour_part((ra_ref, rb_ref, r1_ref, rk_refs), oleft_ref, ghost_turn_ref, ghost_pick_ref,
                                    gath_ref, comb_ref, plus_ref, lleft_ref, llow_ref, partial_ref, slot_ref,
                                    ghost_ref, gsum_ref, sizes):
        for i in range(GROUP):
            out_ref[g * GROUP + i] = values[i]


def body(
    dom_count,
    sub_count,
    modal_state,
    cluster_id,
    jacobian_id,
    face_neighbour,
    flux_index,
    send_list,
    derivative,
    stiffness,
    restriction,
    lifting,
    orientation,
    star_matrix,
    flux_minus,
    flux_plus,
):
    basis, variables, elements = modal_state.shape
    ghosts = send_list.shape[0]
    cap_sub = (ghosts - 2 * CAP_DOM) // sub_count
    lanes = variables * elements
    half_rows = -(-variables * PAD // 32) * 16
    rows = 2 * half_rows
    sizes = Sizes(variables, basis, sub_count, cap_sub, rows, half_rows)
    sub_lanes = -(-rows // 128) * 128
    mat_rows = variables * variables * 4 + 4
    xs = sub_count // 2 - 1

    state = jnp.transpose(modal_state, (1, 0, 2))
    star_table = jnp.transpose(star_matrix, (2, 3, 1, 0))
    minus_table = jnp.transpose(flux_minus, (2, 3, 1, 0))
    plus_table = jnp.transpose(flux_plus, (2, 3, 1, 0))
    restrict = jnp.transpose(restriction, (1, 0, 2))
    lift = jnp.transpose(lifting, (2, 0, 1))
    classes = jacobian_id.reshape(1, elements)
    clusters = cluster_id.reshape(1, elements)
    sends = send_list.reshape(1, ghosts)

    def sds(*shape, dtype=F32):
        return jax.ShapeDtypeStruct(shape, dtype)

    def like(x):
        return sds(*x.shape, dtype=x.dtype)

    whole = sds(variables, basis, elements)
    face_t = sds(4 * PAD, lanes)
    faces_t = sds(2 * rows, 4 * elements, dtype=BF16)
    mat_t = sds(mat_rows, 128)
    gath_t = sds(variables * PAD, 4 * elements)
    left_t = sds(-(-3 * basis // 16) * 16, 3 * SEC, dtype=BF16)
    pay_t = [sds(half_rows, 128)] * 2 + [sds(cap_sub * (xs + 1), sub_lanes)] + [sds(cap_sub, sub_lanes)] * xs

    def scratch(t):
        return pltpu.VMEM(t.shape, t.dtype)

    moved_s = pltpu.VMEM((3 * basis, lanes), F32)
    stage_s = pltpu.VMEM((mat_rows, 128), F32)
    slot_s = pltpu.VMEM((128, sub_lanes), F32)
    pslot_s = pltpu.VMEM((ghosts - 2 * CAP_DOM, sub_lanes), F32)
    ghost_s = pltpu.VMEM((2 * rows, 256), BF16)

    def call(fn, outs, scratches, operands, flops, space=pltpu.VMEM):
        vmem = pl.BlockSpec(memory_space=pltpu.VMEM)
        if space is pltpu.HBM:
            operands = [pltpu.with_memory_space_constraint(x, pltpu.HBM) for x in operands]
        return pl.pallas_call(
            functools.partial(fn, sizes),
            out_shape=outs,
            in_specs=[pl.BlockSpec(memory_space=space)] * len(operands),
            out_specs=jax.tree.map(lambda _: vmem, outs),
            scratch_shapes=scratches,
            cost_estimate=pl.CostEstimate(flops=flops, bytes_accessed=2_000_000, transcendentals=0),
            compiler_params=pltpu.CompilerParams(vmem_limit_bytes=24 * 1024 * 1024),
        )(*operands)

    combined = ("dom", "sub")

    def device(d, s):
        return d * sub_count + s

    def pairs(target):
        return [(device(d, s), device(*target(d, s))) for d in range(dom_count) for s in range(sub_count)]

    even_pairs = pairs(lambda d, s: (d ^ 1, s))
    odd_pairs = pairs(lambda d, s: (((d + 1) ^ 1) - 1, s) if 0 < d < dom_count - 1 else (d, s ^ 1))

    def sub_pairs(k):
        return pairs(lambda d, s: (d, s ^ k))

    def trade(payload):
        pa, pb, p1, *pk = payload
        r1 = lax.ppermute(p1, combined, sub_pairs(1))
        rb = lax.ppermute(pb, combined, odd_pairs)
        ra = lax.ppermute(pa, combined, even_pairs)
        rk = []
        for i, part in enumerate(pk):
            passed = r1[(i + 1) * cap_sub : (i + 2) * cap_sub]
            rk.append(lax.ppermute(jnp.concatenate([part, passed], axis=0), combined, sub_pairs(2 * i + 2)))
        return [ra, rb, r1, *rk]

    later = [clusters, minus_table, plus_table, face_neighbour, flux_index, stiffness, lift, orientation]
    outs = call(
        kernel_predict,
        [like(x) for x in [classes, *later]]
        + [whole, whole, whole, face_t, faces_t, mat_t, left_t, sds(4 * PAD, 3 * SEC, dtype=BF16)]
        + [sds(4 * elements, 128, dtype=BF16), sds(ghosts - 2 * CAP_DOM, 4 * elements, dtype=BF16)]
        + pay_t,
        [
            scratch(star_table), scratch(derivative), scratch(restrict), scratch(sends),
            moved_s, moved_s, stage_s, pltpu.VMEM((4 * PAD, 128), F32), pslot_s, pltpu.SemaphoreType.DMA((14,)),
        ],
        [state, classes, star_table, derivative, restrict, sends, *later],
        60_000_000,
        pltpu.HBM,
    )
    clusters, minus_table, plus_table, code, flux, stiff, lift, orient = outs[1:9]
    classes = outs[0]
    state, first, late, proj, faces, star, dleft, rleft, pick_send, pick_sub, *payload = outs[9:]
    received = trade(payload)
    (partial, gath, comb, minus, plus, kleft, oleft, lleft, llow, pick, ghost_pick, turn, ghost_turn) = call(
        kernel_local_first,
        [whole, gath_t, face_t, mat_t, mat_t, left_t, sds(80, 3 * OSEC, dtype=BF16)]
        + [sds(64, 256, dtype=BF16), sds(64, 128, dtype=BF16)]
        + [sds(4 * elements, 4 * elements, dtype=BF16), sds(256, 4 * elements, dtype=BF16)]
        + [sds(1, 4 * elements, dtype=I32), sds(1, 256, dtype=I32)],
        [moved_s, stage_s, pltpu.VMEM((128, 128), F32)],
        [classes, minus_table, plus_table, code, flux, stiff, lift, orient, first, state, star, proj, faces],
        30_000_000,
    )
    common = [oleft, ghost_turn, ghost_pick]
    middle, second, proj, faces, *payload = call(
        kernel_second,
        [whole, whole, face_t, faces_t] + pay_t,
        [moved_s, moved_s, slot_s, pslot_s, ghost_s, scratch(gath_t)],
        received
        + common
        + [gath, comb, plus, lleft, llow, partial, star, late, clusters, dleft, rleft, pick_send, pick_sub],
        70_000_000,
    )
    received = trade(payload)
    partial, gath, comb = call(
        kernel_local_second,
        [whole, gath_t, face_t],
        [moved_s],
        [second, middle, star, kleft, proj, faces, minus, oleft, pick, turn],
        30_000_000,
    )
    result = call(
        kernel_last,
        whole,
        [slot_s, ghost_s, scratch(gath_t)],
        received + common + [gath, comb, plus, lleft, llow, partial],
        10_000_000,
    )
    return jnp.transpose(result, (1, 0, 2))


def solution(mesh):
    placed = (
        P(None, None, ("dom", "sub")),
        P(("dom", "sub")),
        P(("dom", "sub")),
        P(None, ("dom", "sub")),
        P(None, ("dom", "sub")),
        P(("dom", "sub")),
        P(),
        P(),
        P(),
        P(),
        P(),
        P(),
        P(),
        P(),
    )
    return jax.shard_map(
        functools.partial(body, mesh.shape["dom"], mesh.shape["sub"]),
        mesh=mesh,
        in_specs=placed,
        out_specs=P(None, None, ("dom", "sub")),
        check_vma=False,
    )
```

```python
import collections
import functools

import jax
import jax.numpy as jnp
from jax import lax
from jax.experimental import pallas as pl
from jax.experimental.pallas import tpu as pltpu
from jax.sharding import PartitionSpec as P

ORDER = 6
CAP_DOM = 64
HALF = 0.5
PAD = 24
SEC = 64
OSEC = 32
GROUP = 3

F32 = jnp.float32
BF16 = jnp.bfloat16
I32 = jnp.int32

Sizes = collections.namedtuple(
    "Sizes", ["variables", "basis", "sub_count", "cap_sub", "rows", "half_rows"]
)


def split(x):
    high = x.astype(BF16)
    low = (x - high.astype(F32)).astype(BF16)
    return high, low


def dot(a, b):
    return lax.dot_general(a, b, (((1,), (0,)), ((), ())), preferred_element_type=F32)


def dot_nt(a, b):
    return lax.dot_general(a, b, (((1,), (1,)), ((), ())), preferred_element_type=F32)


def pad_to(x, rows, lanes):
    m, k = x.shape
    if lanes > k:
        x = jnp.concatenate([x, jnp.zeros((m, lanes - k), x.dtype)], axis=1)
    if rows > m:
        x = jnp.concatenate([x, jnp.zeros((rows - m, lanes), x.dtype)], axis=0)
    return x


def stack_left(matrix):
    m = -(-matrix.shape[0] // 16) * 16
    wide = pad_to(matrix, m, 128)
    high = wide.astype(BF16).astype(F32)
    low = wide - high
    both = high + pltpu.roll(high, SEC, 1)
    return jnp.concatenate([both.astype(BF16), low.astype(BF16)], axis=1)[:, : 3 * SEC]


def stack_right(blocks):
    out = []
    for x in blocks:
        high, low = split(pad_to(x, SEC, x.shape[1]))
        out.append(jnp.concatenate([high, low, high], axis=0))
    return jnp.concatenate(out, axis=1) if len(out) > 1 else out[0]


def mix_group(moved_ref, star_ref, sizes, g):
    basis, variables = sizes.basis, sizes.variables
    acc = [None] * GROUP
    for q in range(variables):
        for d in range(3):
            block = moved_ref[d * basis : (d + 1) * basis, q * 128 : (q + 1) * 128]
            for i in range(GROUP):
                row = (q * variables + g * GROUP + i) * 4 + d
                term = block * star_ref[row : row + 1, :]
                acc[i] = term if acc[i] is None else acc[i] + term
    return acc


def lookup(table_ref, stage_ref, class_row, out_ref):
    nq, np_, parts, classes = table_ref.shape
    for q in range(nq):
        for p in range(np_):
            row = (q * np_ + p) * 4
            stage_ref[row : row + parts, :classes] = table_ref[q, p]
    rows = stage_ref.shape[0]
    high, low = split(stage_ref[:, :classes])
    onehot = (lax.broadcasted_iota(I32, (classes, 128), 0) == class_row).astype(F32).astype(BF16)
    out_ref[0:rows, :] = dot(high, onehot) + dot(low, onehot)


def groups(sizes):
    return range(sizes.variables // GROUP)


def group_lanes(g):
    return slice(g * GROUP * 128, (g + 1) * GROUP * 128)


def advance(src_ref, dst_ref, star_ref, left, sizes, emit):
    for g in groups(sizes):
        acc = mix_group(src_ref, star_ref, sizes, g)
        for i in range(GROUP):
            emit(g * GROUP + i, acc[i])
        dst_ref[:, group_lanes(g)] = dot(left, stack_right(acc))[: dst_ref.shape[0]]


def predictor(moved_ref, other_ref, star_ref, left, first_ref, late_ref, sizes, finish):
    def weigh(weights, degree):
        w_half, w_full = weights
        scale = -1.0 / (degree + 1)
        return w_half * (scale * HALF), w_full * scale

    def emitter(weights):
        w_half, w_full = weights

        def emit(p, value):
            first_ref[p] += w_half * value
            if late_ref is not None:
                late_ref[p] += (w_full - w_half) * value

        return emit

    def two(i, weights):
        weights = weigh(weights, 2 * i + 1)
        advance(moved_ref, other_ref, star_ref, left, sizes, emitter(weights))
        weights = weigh(weights, 2 * i + 2)
        advance(other_ref, moved_ref, star_ref, left, sizes, emitter(weights))
        return weights

    steps = ORDER - 1
    weights = (HALF, 1.0)
    for i in range(steps // 2):
        weights = two(i, weights)
    w_half, w_full = weigh(weights, steps)
    for g in groups(sizes):
        acc = mix_group(moved_ref, star_ref, sizes, g)
        values = []
        for i in range(GROUP):
            p = g * GROUP + i
            first = first_ref[p] + w_half * acc[i]
            if late_ref is not None:
                late_ref[p] += (w_full - w_half) * acc[i]
            values.append(finish(p, first))
        yield g, values


def project(g, values, left, proj_ref):
    proj_ref[:, group_lanes(g)] = dot(left, stack_right(values))


def by_face(proj_ref, faces_ref, sizes):
    rows = sizes.rows
    for f in range(4):
        pieces = [
            proj_ref[f * PAD : (f + 1) * PAD, q * 128 : (q + 1) * 128] for q in range(sizes.variables)
        ]
        high, low = split(pad_to(jnp.concatenate(pieces, axis=0), rows, 128))
        faces_ref[0:rows, f * 128 : (f + 1) * 128] = high
        faces_ref[rows : 2 * rows, f * 128 : (f + 1) * 128] = low


def is_even():
    return lax.rem(lax.axis_index("dom"), 2) == 0


def low_lanes(shape):
    return lax.broadcasted_iota(I32, shape, 1) < CAP_DOM


def picks_of_sends(send_ref, pick_ref, pick_sub_ref):
    ghosts = send_ref.shape[1]
    row = send_ref[...].astype(F32)
    dom_row = row[:, 0:128]
    dom_row = jnp.where(is_even(), pltpu.roll(dom_row, CAP_DOM, 1), dom_row)
    place = lax.broadcasted_iota(I32, (128, 128), 0).astype(F32)
    for f in range(4):
        pick_ref[f * 128 : (f + 1) * 128, :] = (place + f * 128 == dom_row).astype(F32).astype(BF16)
    subs = ghosts - 128
    sub_row = pad_to(row[:, 128:], 1, 128)
    column = jnp.transpose(jnp.broadcast_to(sub_row, (128, 128)), (1, 0))[:subs]
    lane = lax.broadcasted_iota(I32, (subs, 128), 1).astype(F32)
    for f in range(4):
        pick_sub_ref[:, f * 128 : (f + 1) * 128] = (column == lane + f * 128).astype(F32).astype(BF16)


def payloads(faces_ref, pick_ref, pick_sub_ref, slot_ref, outs, sizes):
    pa_ref, pb_ref, p1_ref, pk_refs = outs
    rows, half = sizes.rows, sizes.half_rows
    sub = dot_nt(pick_sub_ref[...], faces_ref[0:rows, :]) + dot_nt(pick_sub_ref[...], faces_ref[rows : 2 * rows, :])
    slot_ref[...] = pad_to(sub, sub.shape[0], slot_ref.shape[1])
    both = dot(faces_ref[...], pick_ref[...])
    both = both[0:rows] + both[rows : 2 * rows]
    top, bottom = both[0:half], both[half:]
    low = low_lanes((half, 128))
    pa_ref[...] = jnp.where(low, top, pltpu.roll(bottom, CAP_DOM, 1))
    pb_ref[...] = jnp.where(low, pltpu.roll(top, CAP_DOM, 1), bottom)
    me = lax.axis_index("sub")
    cap = sizes.cap_sub

    def block(k):
        return slot_ref[pl.ds(pl.multiple_of(jnp.bitwise_xor(me, k) * cap, 8), cap), :]

    p1_ref[0:cap, :] = block(1)
    for i, k in enumerate(range(2, sizes.sub_count, 2)):
        p1_ref[(i + 1) * cap : (i + 2) * cap, :] = block(k + 1)
        pk_refs[i][...] = block(k)


def unpack(ins, slot_ref, sizes):
    ra_ref, rb_ref, r1_ref, rk_refs = ins
    ra, rb = ra_ref[...], rb_ref[...]
    low = low_lanes(ra.shape)
    top = jnp.where(low, ra, pltpu.roll(rb, CAP_DOM, 1))
    bottom = jnp.where(low, pltpu.roll(ra, CAP_DOM, 1), rb)
    dom = jnp.concatenate([top, bottom], axis=0)
    me = lax.axis_index("sub")
    cap = sizes.cap_sub
    slot_ref[...] = jnp.zeros_like(slot_ref)

    def put(k, value):
        slot_ref[pl.ds(pl.multiple_of(jnp.bitwise_xor(me, k) * cap, 8), cap), :] = value

    put(1, r1_ref[0:cap, :])
    for i, k in enumerate(range(2, sizes.sub_count, 2)):
        put(k, rk_refs[i][0:cap, :])
        put(k + 1, rk_refs[i][cap : 2 * cap, :])
    sub = jnp.transpose(slot_ref[...], (1, 0))[: dom.shape[0]]
    return jnp.concatenate([dom, sub], axis=1)


def turn_blocks(values, left, turns):
    out = []
    for value in values:
        high, low = split(pad_to(value, OSEC, value.shape[1]))
        turned = dot(left, jnp.concatenate([high, low, high], axis=0))
        out.append(
            jnp.where(
                turns == 0,
                turned[0:PAD],
                jnp.where(turns == 1, turned[PAD : 2 * PAD], turned[2 * PAD : 3 * PAD]),
            )
        )
    return out


def orient_left(orient_ref):
    blocks = [pad_to(orient_ref[h], PAD, 128) for h in range(3)]
    wide = pad_to(jnp.concatenate(blocks, axis=0), 80, 128)
    high = wide.astype(BF16).astype(F32)
    low = wide - high
    stacked = high + pltpu.roll(high, OSEC, 1) + pltpu.roll(low, 2 * OSEC, 1)
    return stacked.astype(BF16)[:, : 3 * OSEC]


def face_of(flux):
    return (flux >= 3).astype(I32) + (flux >= 6).astype(I32) + (flux >= 9).astype(I32)


def kernel_predict(sizes, *refs):
    xs = sizes.sub_count // 2 - 1
    (state_hbm, class_hbm, table_hbm, deriv_hbm, restrict_hbm, send_hbm, *later_hbm) = refs[:14]
    refs = refs[14:]
    class_ref, refs = refs[0], refs[1:]
    later_refs, refs = refs[:8], refs[8:]
    (state_ref, first_ref, late_ref, proj_ref, faces_ref, star_ref, dleft_ref, rleft_ref, pick_ref, pick_sub_ref,
     pa_ref, pb_ref, p1_ref, *rest) = refs
    pk_refs, rest = rest[:xs], rest[xs:]
    (table_ref, deriv_ref, restrict_ref, send_ref, moved_ref, other_ref, stage_ref, rstage_ref, slot_ref,
     sems) = rest
    sources = [class_hbm, table_hbm, deriv_hbm, state_hbm, send_hbm, restrict_hbm, *later_hbm]
    targets = [class_ref, table_ref, deriv_ref, state_ref, send_ref, restrict_ref, *later_refs]
    copies = [pltpu.make_async_copy(s, t, sems.at[i]) for i, (s, t) in enumerate(zip(sources, targets))]
    for copy in copies:
        copy.start()
    variables, basis = sizes.variables, sizes.basis
    copies[0].wait()
    copies[1].wait()
    lookup(table_ref, stage_ref, class_ref[...], star_ref)
    copies[2].wait()
    dleft_ref[...] = stack_left(jnp.reshape(deriv_ref[...], (3 * basis, basis)))
    left = dleft_ref[...]
    copies[3].wait()
    for g in groups(sizes):
        values = [state_ref[g * GROUP + i] for i in range(GROUP)]
        moved_ref[:, group_lanes(g)] = dot(left, stack_right(values))[: moved_ref.shape[0]]
        for i in range(GROUP):
            first_ref[g * GROUP + i] = values[i] * HALF
            late_ref[g * GROUP + i] = values[i] * (1.0 - HALF)
    copies[4].wait()
    picks_of_sends(send_ref, pick_ref, pick_sub_ref)
    copies[5].wait()
    faces, face_basis = 4, restrict_ref.shape[0]
    rstage_ref[...] = jnp.zeros_like(rstage_ref)
    for f in range(faces):
        rstage_ref[f * PAD : f * PAD + face_basis, :basis] = restrict_ref[:, f, :]
    rleft_ref[...] = stack_left(rstage_ref[:, :basis])

    def finish(p, first):
        first_ref[p] = first
        return first

    for g, values in predictor(moved_ref, other_ref, star_ref, left, first_ref, late_ref, sizes, finish):
        project(g, values, rleft_ref[...], proj_ref)
    by_face(proj_ref, faces_ref, sizes)
    payloads(faces_ref, pick_ref, pick_sub_ref, slot_ref, (pa_ref, pb_ref, p1_ref, pk_refs), sizes)
    for copy in copies[6:]:
        copy.wait()


def volume_part(values_ref, base_ref, star_ref, kleft, moved_ref, partial_ref, sizes):
    for g in groups(sizes):
        values = [values_ref[g * GROUP + i] for i in range(GROUP)]
        moved_ref[:, group_lanes(g)] = dot(kleft, stack_right(values))[: moved_ref.shape[0]]
    for g in groups(sizes):
        acc = mix_group(moved_ref, star_ref, sizes, g)
        for i in range(GROUP):
            partial_ref[g * GROUP + i] = base_ref[g * GROUP + i] + acc[i]


def interior_part(faces_ref, pick_ref, oleft, turn, gath_ref, sizes):
    rows = sizes.rows
    both = dot(faces_ref[...], pick_ref[...])
    both = both[0:rows] + both[rows : 2 * rows]
    blocks = [both[q * PAD : (q + 1) * PAD] for q in range(sizes.variables)]
    for q, block in enumerate(turn_blocks(blocks, oleft, turn)):
        gath_ref[q * PAD : (q + 1) * PAD, :] = block


def own_part(proj_ref, minus_ref, comb_ref, sizes):
    variables = sizes.variables
    for f in range(4):
        rows = slice(f * PAD, (f + 1) * PAD)
        acc = [None] * variables
        for q in range(variables):
            block = proj_ref[rows, q * 128 : (q + 1) * 128]
            for p in range(variables):
                row = (q * variables + p) * 4 + f
                term = block * minus_ref[row : row + 1, :]
                acc[p] = term if acc[p] is None else acc[p] + term
        for p in range(variables):
            comb_ref[rows, p * 128 : (p + 1) * 128] = acc[p]


def kernel_local_first(sizes, *refs):
    (class_ref, minus_table, plus_table, code_ref, flux_ref, stiff_ref, lift_ref, orient_ref,
     first_ref, state_ref, star_ref, proj_ref, faces_ref,
     partial_ref, gath_ref, comb_ref, minus_ref, plus_ref, kleft_ref, oleft_ref, lleft_ref, llow_ref,
     pick_ref, ghost_pick_ref, turn_ref, ghost_turn_ref, moved_ref, stage_ref, lstage_ref) = refs
    basis = sizes.basis
    kleft_ref[...] = stack_left(jnp.reshape(stiff_ref[...], (3 * basis, basis)))
    volume_part(first_ref, state_ref, star_ref, kleft_ref[...], moved_ref, partial_ref, sizes)
    lookup(minus_table, stage_ref, class_ref[...], minus_ref)
    oleft_ref[...] = orient_left(orient_ref)
    code = code_ref[...]
    flux = flux_ref[...]
    face = face_of(flux)
    turn = flux - 3 * face
    turn_row = jnp.concatenate([turn[f : f + 1, :] for f in range(4)], axis=1)
    turn_ref[...] = turn_row
    place = lax.broadcasted_iota(I32, (128, 128), 0)
    target = jnp.where(code < 128, face * 128 + code, -1)
    for f in range(4):
        for j in range(4):
            pick_ref[j * 128 : (j + 1) * 128, f * 128 : (f + 1) * 128] = (
                (place + j * 128 == target[f : f + 1, :]).astype(F32).astype(BF16)
            )
    slot = code - 128
    swapped = jnp.where(slot < CAP_DOM, slot + CAP_DOM, jnp.where(slot < 2 * CAP_DOM, slot - CAP_DOM, slot))
    slot = jnp.where(is_even(), swapped, slot)
    slot = jnp.where(code < 128, -1, slot)
    for f in range(4):
        for j in range(2):
            ghost_pick_ref[j * 128 : (j + 1) * 128, f * 128 : (f + 1) * 128] = (
                (place + j * 128 == slot[f : f + 1, :]).astype(F32).astype(BF16)
            )
    rows = jnp.broadcast_to(turn_row.astype(F32), (16, 512)).astype(BF16)
    ghost_turn_ref[...] = dot_nt(rows, ghost_pick_ref[...])[0:1].astype(I32)
    interior_part(faces_ref, pick_ref, oleft_ref[...], turn_row, gath_ref, sizes)
    own_part(proj_ref, minus_ref, comb_ref, sizes)
    lookup(plus_table, stage_ref, class_ref[...], plus_ref)
    lstage_ref[...] = jnp.zeros_like(lstage_ref)
    for f in range(4):
        lstage_ref[f * PAD : f * PAD + lift_ref.shape[0], :basis] = lift_ref[:, f, :]
    wide = jnp.transpose(lstage_ref[...], (1, 0))[:64]
    high = wide.astype(BF16).astype(F32)
    low = wide - high
    rolled = pltpu.roll(high, 4 * PAD, 1)
    lane = lax.broadcasted_iota(I32, (64, 128), 1)
    lleft_ref[:, 0:128] = jnp.where(lane < 4 * PAD, high, rolled).astype(BF16)
    lleft_ref[:, 128:256] = jnp.where(lane < 8 * PAD - 128, rolled, 0.0).astype(BF16)
    llow_ref[...] = low.astype(BF16)


def kernel_local_second(sizes, *refs):
    (second_ref, middle_ref, star_ref, kleft_ref, proj_ref, faces_ref, minus_ref, oleft_ref, pick_ref, turn_ref,
     partial_ref, gath_ref, comb_ref, moved_ref) = refs
    volume_part(second_ref, middle_ref, star_ref, kleft_ref[...], moved_ref, partial_ref, sizes)
    interior_part(faces_ref, pick_ref, oleft_ref[...], turn_ref[...], gath_ref, sizes)
    own_part(proj_ref, minus_ref, comb_ref, sizes)


def neighbour_part(ins, oleft_ref, ghost_turn_ref, ghost_pick_ref, gath_ref, comb_ref, plus_ref, lleft_ref, llow_ref,
                   partial_ref, slot_ref, ghost_ref, gsum_ref, sizes):
    variables, basis, rows = sizes.variables, sizes.basis, sizes.rows
    received = unpack(ins, slot_ref, sizes)
    blocks = [received[q * PAD : (q + 1) * PAD] for q in range(variables)]
    turned = turn_blocks(blocks, oleft_ref[...], ghost_turn_ref[...])
    high, low = split(pad_to(jnp.concatenate(turned, axis=0), rows, turned[0].shape[1]))
    ghost_ref[0:rows, :] = high
    ghost_ref[rows : 2 * rows, :] = low
    both = dot(ghost_ref[...], ghost_pick_ref[...])
    used = variables * PAD
    gsum_ref[...] = gath_ref[...] + (both[0:used] + both[rows : rows + used])
    for g in groups(sizes):
        highs, stacks = [], []
        faces = [[], [], []]
        for f in range(4):
            frows = slice(f * PAD, (f + 1) * PAD)
            acc = []
            for i in range(GROUP):
                p = g * GROUP + i
                acc.append(comb_ref[frows, p * 128 : (p + 1) * 128])
            for q in range(variables):
                block = gsum_ref[q * PAD : (q + 1) * PAD, f * 128 : (f + 1) * 128]
                for i in range(GROUP):
                    row = (q * variables + g * GROUP + i) * 4 + f
                    acc[i] = acc[i] + block * plus_ref[row : row + 1, :]
            for i in range(GROUP):
                faces[i].append(acc[i])
        for i in range(GROUP):
            high, low = split(jnp.concatenate(faces[i], axis=0))
            highs.append(high)
            stacks.append(jnp.concatenate([high, low], axis=0))
        lifted = dot(lleft_ref[:, : 8 * PAD], jnp.concatenate(stacks, axis=1)) + dot(
            llow_ref[:, : 4 * PAD], jnp.concatenate(highs, axis=1)
        )
        yield g, [
            partial_ref[g * GROUP + i] + lifted[:basis, i * 128 : (i + 1) * 128] for i in range(GROUP)
        ]


def kernel_second(sizes, *refs):
    xs = sizes.sub_count // 2 - 1
    ra_ref, rb_ref, r1_ref, *refs = refs
    rk_refs, refs = refs[:xs], refs[xs:]
    (oleft_ref, ghost_turn_ref, ghost_pick_ref, gath_ref, comb_ref, plus_ref, lleft_ref, llow_ref, partial_ref,
     star_ref, late_ref, cluster_ref, dleft_ref, rleft_ref, pick_ref, pick_sub_ref,
     middle_ref, second_ref, proj_ref, faces_ref, pa_ref, pb_ref, p1_ref, *rest) = refs
    pk_refs, rest = rest[:xs], rest[xs:]
    moved_ref, other_ref, slot_ref, pslot_ref, ghost_ref, gsum_ref = rest
    left = dleft_ref[...]
    for g, values in neighbour_part((ra_ref, rb_ref, r1_ref, rk_refs), oleft_ref, ghost_turn_ref, ghost_pick_ref,
                                    gath_ref, comb_ref, plus_ref, lleft_ref, llow_ref, partial_ref, slot_ref,
                                    ghost_ref, gsum_ref, sizes):
        moved_ref[:, group_lanes(g)] = dot(left, stack_right(values))[: moved_ref.shape[0]]
        for i in range(GROUP):
            middle_ref[g * GROUP + i] = values[i]
            second_ref[g * GROUP + i] = values[i] * HALF
    fine = cluster_ref[...] == 1

    def finish(p, first):
        value = jnp.where(fine, first, late_ref[p])
        second_ref[p] = value
        return value

    for g, values in predictor(moved_ref, other_ref, star_ref, left, second_ref, None, sizes, finish):
        project(g, values, rleft_ref[...], proj_ref)
    by_face(proj_ref, faces_ref, sizes)
    payloads(faces_ref, pick_ref, pick_sub_ref, pslot_ref, (pa_ref, pb_ref, p1_ref, pk_refs), sizes)


def kernel_last(sizes, *refs):
    xs = sizes.sub_count // 2 - 1
    ra_ref, rb_ref, r1_ref, *refs = refs
    rk_refs, refs = refs[:xs], refs[xs:]
    (oleft_ref, ghost_turn_ref, ghost_pick_ref, gath_ref, comb_ref, plus_ref, lleft_ref, llow_ref, partial_ref,
     out_ref, slot_ref, ghost_ref, gsum_ref) = refs
    for g, values in neighbour_part((ra_ref, rb_ref, r1_ref, rk_refs), oleft_ref, ghost_turn_ref, ghost_pick_ref,
                                    gath_ref, comb_ref, plus_ref, lleft_ref, llow_ref, partial_ref, slot_ref,
                                    ghost_ref, gsum_ref, sizes):
        for i in range(GROUP):
            out_ref[g * GROUP + i] = values[i]


def body(
    dom_count,
    sub_count,
    modal_state,
    cluster_id,
    jacobian_id,
    face_neighbour,
    flux_index,
    send_list,
    derivative,
    stiffness,
    restriction,
    lifting,
    orientation,
    star_matrix,
    flux_minus,
    flux_plus,
):
    basis, variables, elements = modal_state.shape
    ghosts = send_list.shape[0]
    cap_sub = (ghosts - 2 * CAP_DOM) // sub_count
    lanes = variables * elements
    half_rows = -(-variables * PAD // 32) * 16
    rows = 2 * half_rows
    sizes = Sizes(variables, basis, sub_count, cap_sub, rows, half_rows)
    sub_lanes = -(-rows // 128) * 128
    mat_rows = variables * variables * 4 + 4
    xs = sub_count // 2 - 1

    state = jnp.transpose(modal_state, (1, 0, 2))
    star_table = jnp.transpose(star_matrix, (2, 3, 1, 0))
    minus_table = jnp.transpose(flux_minus, (2, 3, 1, 0))
    plus_table = jnp.transpose(flux_plus, (2, 3, 1, 0))
    restrict = jnp.transpose(restriction, (1, 0, 2))
    lift = jnp.transpose(lifting, (2, 0, 1))
    classes = jacobian_id.reshape(1, elements)
    clusters = cluster_id.reshape(1, elements)
    sends = send_list.reshape(1, ghosts)

    def sds(*shape, dtype=F32):
        return jax.ShapeDtypeStruct(shape, dtype)

    def like(x):
        return sds(*x.shape, dtype=x.dtype)

    whole = sds(variables, basis, elements)
    face_t = sds(4 * PAD, lanes)
    faces_t = sds(2 * rows, 4 * elements, dtype=BF16)
    mat_t = sds(mat_rows, 128)
    gath_t = sds(variables * PAD, 4 * elements)
    left_t = sds(-(-3 * basis // 16) * 16, 3 * SEC, dtype=BF16)
    pay_t = [sds(half_rows, 128)] * 2 + [sds(cap_sub * (xs + 1), sub_lanes)] + [sds(cap_sub, sub_lanes)] * xs

    def scratch(t):
        return pltpu.VMEM(t.shape, t.dtype)

    moved_s = pltpu.VMEM((3 * basis, lanes), F32)
    stage_s = pltpu.VMEM((mat_rows, 128), F32)
    slot_s = pltpu.VMEM((128, sub_lanes), F32)
    pslot_s = pltpu.VMEM((ghosts - 2 * CAP_DOM, sub_lanes), F32)
    ghost_s = pltpu.VMEM((2 * rows, 256), BF16)

    def call(fn, outs, scratches, operands, flops, space=pltpu.VMEM):
        vmem = pl.BlockSpec(memory_space=pltpu.VMEM)
        if space is pltpu.HBM:
            operands = [pltpu.with_memory_space_constraint(x, pltpu.HBM) for x in operands]
        return pl.pallas_call(
            functools.partial(fn, sizes),
            out_shape=outs,
            in_specs=[pl.BlockSpec(memory_space=space)] * len(operands),
            out_specs=jax.tree.map(lambda _: vmem, outs),
            scratch_shapes=scratches,
            cost_estimate=pl.CostEstimate(flops=flops, bytes_accessed=2_000_000, transcendentals=0),
            compiler_params=pltpu.CompilerParams(vmem_limit_bytes=24 * 1024 * 1024),
        )(*operands)

    combined = ("dom", "sub")

    def device(d, s):
        return d * sub_count + s

    def pairs(target):
        return [(device(d, s), device(*target(d, s))) for d in range(dom_count) for s in range(sub_count)]

    even_pairs = pairs(lambda d, s: (d ^ 1, s))
    odd_pairs = pairs(lambda d, s: (((d + 1) ^ 1) - 1, s) if 0 < d < dom_count - 1 else (d, s ^ 1))

    def sub_pairs(k):
        return pairs(lambda d, s: (d, s ^ k))

    def trade(payload):
        pa, pb, p1, *pk = payload
        r1 = lax.ppermute(p1, combined, sub_pairs(1))
        rb = lax.ppermute(pb, combined, odd_pairs)
        ra = lax.ppermute(pa, combined, even_pairs)
        rk = []
        for i, part in enumerate(pk):
            passed = r1[(i + 1) * cap_sub : (i + 2) * cap_sub]
            rk.append(lax.ppermute(jnp.concatenate([part, passed], axis=0), combined, sub_pairs(2 * i + 2)))
        return [ra, rb, r1, *rk]

    later = [clusters, minus_table, plus_table, face_neighbour, flux_index, stiffness, lift, orientation]
    outs = call(
        kernel_predict,
        [like(x) for x in [classes, *later]]
        + [whole, whole, whole, face_t, faces_t, mat_t, left_t, sds(4 * PAD, 3 * SEC, dtype=BF16)]
        + [sds(4 * elements, 128, dtype=BF16), sds(ghosts - 2 * CAP_DOM, 4 * elements, dtype=BF16)]
        + pay_t,
        [
            scratch(star_table), scratch(derivative), scratch(restrict), scratch(sends),
            moved_s, moved_s, stage_s, pltpu.VMEM((4 * PAD, 128), F32), pslot_s, pltpu.SemaphoreType.DMA((14,)),
        ],
        [state, classes, star_table, derivative, restrict, sends, *later],
        60_000_000,
        pltpu.HBM,
    )
    clusters, minus_table, plus_table, code, flux, stiff, lift, orient = outs[1:9]
    classes = outs[0]
    state, first, late, proj, faces, star, dleft, rleft, pick_send, pick_sub, *payload = outs[9:]
    received = trade(payload)
    (partial, gath, comb, minus, plus, kleft, oleft, lleft, llow, pick, ghost_pick, turn, ghost_turn) = call(
        kernel_local_first,
        [whole, gath_t, face_t, mat_t, mat_t, left_t, sds(80, 3 * OSEC, dtype=BF16)]
        + [sds(64, 256, dtype=BF16), sds(64, 128, dtype=BF16)]
        + [sds(4 * elements, 4 * elements, dtype=BF16), sds(256, 4 * elements, dtype=BF16)]
        + [sds(1, 4 * elements, dtype=I32), sds(1, 256, dtype=I32)],
        [moved_s, stage_s, pltpu.VMEM((128, 128), F32)],
        [classes, minus_table, plus_table, code, flux, stiff, lift, orient, first, state, star, proj, faces],
        30_000_000,
    )
    common = [oleft, ghost_turn, ghost_pick]
    middle, second, proj, faces, *payload = call(
        kernel_second,
        [whole, whole, face_t, faces_t] + pay_t,
        [moved_s, moved_s, slot_s, pslot_s, ghost_s, scratch(gath_t)],
        received
        + common
        + [gath, comb, plus, lleft, llow, partial, star, late, clusters, dleft, rleft, pick_send, pick_sub],
        70_000_000,
    )
    received = trade(payload)
    partial, gath, comb = call(
        kernel_local_second,
        [whole, gath_t, face_t],
        [moved_s],
        [second, middle, star, kleft, proj, faces, minus, oleft, pick, turn],
        30_000_000,
    )
    result = call(
        kernel_last,
        whole,
        [slot_s, ghost_s, scratch(gath_t)],
        received + common + [gath, comb, plus, lleft, llow, partial],
        10_000_000,
    )
    return jnp.transpose(result, (1, 0, 2))


def solution(mesh):
    placed = (
        P(None, None, ("dom", "sub")),
        P(("dom", "sub")),
        P(("dom", "sub")),
        P(None, ("dom", "sub")),
        P(None, ("dom", "sub")),
        P(("dom", "sub")),
        P(),
        P(),
        P(),
        P(),
        P(),
        P(),
        P(),
        P(),
    )
    return jax.shard_map(
        functools.partial(body, mesh.shape["dom"], mesh.shape["sub"]),
        mesh=mesh,
        in_specs=placed,
        out_specs=P(None, None, ("dom", "sub")),
        check_vma=False,
    )
```

```python
import collections
import functools

import jax
import jax.numpy as jnp
from jax import lax
from jax.experimental import pallas as pl
from jax.experimental.pallas import tpu as pltpu
from jax.sharding import PartitionSpec as P

ORDER = 6
CAP_DOM = 64
HALF = 0.5
PAD = 24
SEC = 64
OSEC = 32
GROUP = 3

F32 = jnp.float32
BF16 = jnp.bfloat16
I32 = jnp.int32

Sizes = collections.namedtuple(
    "Sizes", ["variables", "basis", "sub_count", "cap_sub", "rows", "half_rows"]
)


def split(x):
    high = x.astype(BF16)
    low = (x - high.astype(F32)).astype(BF16)
    return high, low


def dot(a, b):
    return lax.dot_general(a, b, (((1,), (0,)), ((), ())), preferred_element_type=F32)


def dot_nt(a, b):
    return lax.dot_general(a, b, (((1,), (1,)), ((), ())), preferred_element_type=F32)


def pad_to(x, rows, lanes):
    m, k = x.shape
    if lanes > k:
        x = jnp.concatenate([x, jnp.zeros((m, lanes - k), x.dtype)], axis=1)
    if rows > m:
        x = jnp.concatenate([x, jnp.zeros((rows - m, lanes), x.dtype)], axis=0)
    return x


def stack_left(matrix):
    m = -(-matrix.shape[0] // 16) * 16
    wide = pad_to(matrix, m, 128)
    high = wide.astype(BF16).astype(F32)
    low = wide - high
    both = high + pltpu.roll(high, SEC, 1)
    return jnp.concatenate([both.astype(BF16), low.astype(BF16)], axis=1)[:, : 3 * SEC]


def stack_right(blocks):
    out = []
    for x in blocks:
        high, low = split(pad_to(x, SEC, x.shape[1]))
        out.append(jnp.concatenate([high, low, high], axis=0))
    return jnp.concatenate(out, axis=1) if len(out) > 1 else out[0]


def mix_group(moved_ref, star_ref, sizes, g):
    basis, variables = sizes.basis, sizes.variables
    acc = [None] * GROUP
    for q in range(variables):
        for d in range(3):
            block = moved_ref[d * basis : (d + 1) * basis, q * 128 : (q + 1) * 128]
            for i in range(GROUP):
                row = (q * variables + g * GROUP + i) * 4 + d
                term = block * star_ref[row : row + 1, :]
                acc[i] = term if acc[i] is None else acc[i] + term
    return acc


def lookup(table_ref, stage_ref, class_row, out_ref):
    nq, np_, parts, classes = table_ref.shape
    for q in range(nq):
        for p in range(np_):
            row = (q * np_ + p) * 4
            stage_ref[row : row + parts, :classes] = table_ref[q, p]
    rows = stage_ref.shape[0]
    high, low = split(stage_ref[:, :classes])
    onehot = (lax.broadcasted_iota(I32, (classes, 128), 0) == class_row).astype(F32).astype(BF16)
    out_ref[0:rows, :] = dot(high, onehot) + dot(low, onehot)


def groups(sizes):
    return range(sizes.variables // GROUP)


def group_lanes(g):
    return slice(g * GROUP * 128, (g + 1) * GROUP * 128)


def advance(src_ref, dst_ref, star_ref, left, sizes, emit, between):
    for g in groups(sizes):
        acc = mix_group(src_ref, star_ref, sizes, g)
        for i in range(GROUP):
            emit(g * GROUP + i, acc[i])
        dst_ref[:, group_lanes(g)] = dot(left, stack_right(acc))[: dst_ref.shape[0]]
        between()


def predictor(moved_ref, other_ref, star_ref, left, first_ref, late_ref, sizes, finish, extra=()):
    extra = list(extra)

    def between():
        if extra:
            extra.pop(0)()

    def weigh(weights, degree):
        w_half, w_full = weights
        scale = -1.0 / (degree + 1)
        return w_half * (scale * HALF), w_full * scale

    def emitter(weights):
        w_half, w_full = weights

        def emit(p, value):
            first_ref[p] += w_half * value
            if late_ref is not None:
                late_ref[p] += (w_full - w_half) * value

        return emit

    def two(i, weights):
        weights = weigh(weights, 2 * i + 1)
        advance(moved_ref, other_ref, star_ref, left, sizes, emitter(weights), between)
        weights = weigh(weights, 2 * i + 2)
        advance(other_ref, moved_ref, star_ref, left, sizes, emitter(weights), between)
        return weights

    steps = ORDER - 1
    weights = (HALF, 1.0)
    for i in range(steps // 2):
        weights = two(i, weights)
    w_half, w_full = weigh(weights, steps)
    for g in groups(sizes):
        acc = mix_group(moved_ref, star_ref, sizes, g)
        values = []
        for i in range(GROUP):
            p = g * GROUP + i
            first = first_ref[p] + w_half * acc[i]
            if late_ref is not None:
                late_ref[p] += (w_full - w_half) * acc[i]
            values.append(finish(p, first))
        yield g, values


def project(g, values, left, proj_ref):
    proj_ref[:, group_lanes(g)] = dot(left, stack_right(values))


def by_face(proj_ref, faces_ref, sizes):
    rows = sizes.rows
    for f in range(4):
        pieces = [
            proj_ref[f * PAD : (f + 1) * PAD, q * 128 : (q + 1) * 128] for q in range(sizes.variables)
        ]
        high, low = split(pad_to(jnp.concatenate(pieces, axis=0), rows, 128))
        faces_ref[0:rows, f * 128 : (f + 1) * 128] = high
        faces_ref[rows : 2 * rows, f * 128 : (f + 1) * 128] = low


def is_even():
    return lax.rem(lax.axis_index("dom"), 2) == 0


def low_lanes(shape):
    return lax.broadcasted_iota(I32, shape, 1) < CAP_DOM


def picks_of_sends(send_ref, pick_ref, pick_sub_ref):
    ghosts = send_ref.shape[1]
    row = send_ref[...].astype(F32)
    dom_row = row[:, 0:128]
    dom_row = jnp.where(is_even(), pltpu.roll(dom_row, CAP_DOM, 1), dom_row)
    place = lax.broadcasted_iota(I32, (128, 128), 0).astype(F32)
    for f in range(4):
        pick_ref[f * 128 : (f + 1) * 128, :] = (place + f * 128 == dom_row).astype(F32).astype(BF16)
    subs = ghosts - 128
    sub_row = pad_to(row[:, 128:], 1, 128)
    column = jnp.transpose(jnp.broadcast_to(sub_row, (128, 128)), (1, 0))[:subs]
    lane = lax.broadcasted_iota(I32, (subs, 128), 1).astype(F32)
    for f in range(4):
        pick_sub_ref[:, f * 128 : (f + 1) * 128] = (column == lane + f * 128).astype(F32).astype(BF16)


def payloads(faces_ref, pick_ref, pick_sub_ref, slot_ref, outs, sizes):
    pa_ref, pb_ref, p1_ref, pk_refs = outs
    rows, half = sizes.rows, sizes.half_rows
    sub = dot_nt(pick_sub_ref[...], faces_ref[0:rows, :]) + dot_nt(pick_sub_ref[...], faces_ref[rows : 2 * rows, :])
    slot_ref[...] = pad_to(sub, sub.shape[0], slot_ref.shape[1])
    both = dot(faces_ref[...], pick_ref[...])
    both = both[0:rows] + both[rows : 2 * rows]
    top, bottom = both[0:half], both[half:]
    low = low_lanes((half, 128))
    pa_ref[...] = jnp.where(low, top, pltpu.roll(bottom, CAP_DOM, 1))
    pb_ref[...] = jnp.where(low, pltpu.roll(top, CAP_DOM, 1), bottom)
    me = lax.axis_index("sub")
    cap = sizes.cap_sub

    def block(k):
        return slot_ref[pl.ds(pl.multiple_of(jnp.bitwise_xor(me, k) * cap, 8), cap), :]

    p1_ref[0:cap, :] = block(1)
    for i, k in enumerate(range(2, sizes.sub_count, 2)):
        p1_ref[(i + 1) * cap : (i + 2) * cap, :] = block(k + 1)
        pk_refs[i][...] = block(k)


def unpack(ins, slot_ref, sizes):
    ra_ref, rb_ref, r1_ref, rk_refs = ins
    ra, rb = ra_ref[...], rb_ref[...]
    low = low_lanes(ra.shape)
    top = jnp.where(low, ra, pltpu.roll(rb, CAP_DOM, 1))
    bottom = jnp.where(low, pltpu.roll(ra, CAP_DOM, 1), rb)
    dom = jnp.concatenate([top, bottom], axis=0)
    me = lax.axis_index("sub")
    cap = sizes.cap_sub
    slot_ref[...] = jnp.zeros_like(slot_ref)

    def put(k, value):
        slot_ref[pl.ds(pl.multiple_of(jnp.bitwise_xor(me, k) * cap, 8), cap), :] = value

    put(1, r1_ref[0:cap, :])
    for i, k in enumerate(range(2, sizes.sub_count, 2)):
        put(k, rk_refs[i][0:cap, :])
        put(k + 1, rk_refs[i][cap : 2 * cap, :])
    sub = jnp.transpose(slot_ref[...], (1, 0))[: dom.shape[0]]
    return jnp.concatenate([dom, sub], axis=1)


def turn_blocks(values, left, turns):
    out = []
    for value in values:
        high, low = split(pad_to(value, OSEC, value.shape[1]))
        turned = dot(left, jnp.concatenate([high, low, high], axis=0))
        out.append(
            jnp.where(
                turns == 0,
                turned[0:PAD],
                jnp.where(turns == 1, turned[PAD : 2 * PAD], turned[2 * PAD : 3 * PAD]),
            )
        )
    return out


def orient_left(orient_ref):
    blocks = [pad_to(orient_ref[h], PAD, 128) for h in range(3)]
    wide = pad_to(jnp.concatenate(blocks, axis=0), 80, 128)
    high = wide.astype(BF16).astype(F32)
    low = wide - high
    stacked = high + pltpu.roll(high, OSEC, 1) + pltpu.roll(low, 2 * OSEC, 1)
    return stacked.astype(BF16)[:, : 3 * OSEC]


def face_of(flux):
    return (flux >= 3).astype(I32) + (flux >= 6).astype(I32) + (flux >= 9).astype(I32)


def kernel_predict(sizes, *refs):
    xs = sizes.sub_count // 2 - 1
    (state_hbm, class_hbm, table_hbm, deriv_hbm, restrict_hbm, send_hbm, *later_hbm) = refs[:14]
    refs = refs[14:]
    class_ref, refs = refs[0], refs[1:]
    later_refs, refs = refs[:8], refs[8:]
    (state_ref, first_ref, late_ref, proj_ref, faces_ref, star_ref, dleft_ref, rleft_ref, pick_ref, pick_sub_ref,
     pa_ref, pb_ref, p1_ref, *rest) = refs
    pk_refs, rest = rest[:xs], rest[xs:]
    (table_ref, deriv_ref, restrict_ref, send_ref, moved_ref, other_ref, stage_ref, rstage_ref, slot_ref,
     sems) = rest
    sources = [class_hbm, table_hbm, deriv_hbm, state_hbm, send_hbm, restrict_hbm, *later_hbm]
    targets = [class_ref, table_ref, deriv_ref, state_ref, send_ref, restrict_ref, *later_refs]
    copies = [pltpu.make_async_copy(s, t, sems.at[i]) for i, (s, t) in enumerate(zip(sources, targets))]
    for copy in copies:
        copy.start()
    variables, basis = sizes.variables, sizes.basis
    copies[0].wait()
    copies[1].wait()
    lookup(table_ref, stage_ref, class_ref[...], star_ref)
    copies[2].wait()
    dleft_ref[...] = stack_left(jnp.reshape(deriv_ref[...], (3 * basis, basis)))
    left = dleft_ref[...]
    copies[3].wait()
    for g in groups(sizes):
        values = [state_ref[g * GROUP + i] for i in range(GROUP)]
        moved_ref[:, group_lanes(g)] = dot(left, stack_right(values))[: moved_ref.shape[0]]
        for i in range(GROUP):
            first_ref[g * GROUP + i] = values[i] * HALF
            late_ref[g * GROUP + i] = values[i] * (1.0 - HALF)
    for copy in copies[4:6]:
        copy.wait()
    def send_picks():
        picks_of_sends(send_ref, pick_ref, pick_sub_ref)

    def restrict_left():
        rstage_ref[...] = jnp.zeros_like(rstage_ref)
        for f in range(4):
            rstage_ref[f * PAD : f * PAD + restrict_ref.shape[0], :basis] = restrict_ref[:, f, :]
        rleft_ref[...] = stack_left(rstage_ref[:, :basis])

    send_picks()
    restrict_left()

    def finish(p, first):
        first_ref[p] = first
        return first

    for g, values in predictor(moved_ref, other_ref, star_ref, left, first_ref, late_ref, sizes, finish,
                               []):
        project(g, values, rleft_ref[...], proj_ref)
    by_face(proj_ref, faces_ref, sizes)
    payloads(faces_ref, pick_ref, pick_sub_ref, slot_ref, (pa_ref, pb_ref, p1_ref, pk_refs), sizes)
    for copy in copies[6:]:
        copy.wait()


def volume_part(values_ref, base_ref, star_ref, kleft, moved_ref, partial_ref, sizes):
    for g in groups(sizes):
        values = [values_ref[g * GROUP + i] for i in range(GROUP)]
        moved_ref[:, group_lanes(g)] = dot(kleft, stack_right(values))[: moved_ref.shape[0]]
    for g in groups(sizes):
        acc = mix_group(moved_ref, star_ref, sizes, g)
        for i in range(GROUP):
            partial_ref[g * GROUP + i] = base_ref[g * GROUP + i] + acc[i]


def interior_part(faces_ref, pick_ref, oleft, turn, gath_ref, sizes):
    rows = sizes.rows
    both = dot(faces_ref[...], pick_ref[...])
    both = both[0:rows] + both[rows : 2 * rows]
    blocks = [both[q * PAD : (q + 1) * PAD] for q in range(sizes.variables)]
    for q, block in enumerate(turn_blocks(blocks, oleft, turn)):
        gath_ref[q * PAD : (q + 1) * PAD, :] = block


def own_part(proj_ref, minus_ref, comb_ref, sizes):
    variables = sizes.variables
    for f in range(4):
        rows = slice(f * PAD, (f + 1) * PAD)
        acc = [None] * variables
        for q in range(variables):
            block = proj_ref[rows, q * 128 : (q + 1) * 128]
            for p in range(variables):
                row = (q * variables + p) * 4 + f
                term = block * minus_ref[row : row + 1, :]
                acc[p] = term if acc[p] is None else acc[p] + term
        for p in range(variables):
            comb_ref[rows, p * 128 : (p + 1) * 128] = acc[p]


def kernel_local_first(sizes, *refs):
    (class_ref, minus_table, plus_table, code_ref, flux_ref, stiff_ref, lift_ref, orient_ref,
     first_ref, state_ref, star_ref, proj_ref, faces_ref,
     partial_ref, gath_ref, comb_ref, minus_ref, plus_ref, kleft_ref, oleft_ref, lleft_ref, llow_ref,
     pick_ref, ghost_pick_ref, turn_ref, ghost_turn_ref, moved_ref, stage_ref, lstage_ref) = refs
    basis = sizes.basis
    kleft_ref[...] = stack_left(jnp.reshape(stiff_ref[...], (3 * basis, basis)))
    volume_part(first_ref, state_ref, star_ref, kleft_ref[...], moved_ref, partial_ref, sizes)
    lookup(minus_table, stage_ref, class_ref[...], minus_ref)
    oleft_ref[...] = orient_left(orient_ref)
    code = code_ref[...]
    flux = flux_ref[...]
    face = face_of(flux)
    turn = flux - 3 * face
    turn_row = jnp.concatenate([turn[f : f + 1, :] for f in range(4)], axis=1)
    turn_ref[...] = turn_row
    place = lax.broadcasted_iota(I32, (128, 128), 0)
    target = jnp.where(code < 128, face * 128 + code, -1)
    for f in range(4):
        for j in range(4):
            pick_ref[j * 128 : (j + 1) * 128, f * 128 : (f + 1) * 128] = (
                (place + j * 128 == target[f : f + 1, :]).astype(F32).astype(BF16)
            )
    slot = code - 128
    swapped = jnp.where(slot < CAP_DOM, slot + CAP_DOM, jnp.where(slot < 2 * CAP_DOM, slot - CAP_DOM, slot))
    slot = jnp.where(is_even(), swapped, slot)
    slot = jnp.where(code < 128, -1, slot)
    for f in range(4):
        for j in range(2):
            ghost_pick_ref[j * 128 : (j + 1) * 128, f * 128 : (f + 1) * 128] = (
                (place + j * 128 == slot[f : f + 1, :]).astype(F32).astype(BF16)
            )
    rows = jnp.broadcast_to(turn_row.astype(F32), (16, 512)).astype(BF16)
    ghost_turn_ref[...] = dot_nt(rows, ghost_pick_ref[...])[0:1].astype(I32)
    interior_part(faces_ref, pick_ref, oleft_ref[...], turn_row, gath_ref, sizes)
    own_part(proj_ref, minus_ref, comb_ref, sizes)
    lookup(plus_table, stage_ref, class_ref[...], plus_ref)
    lstage_ref[...] = jnp.zeros_like(lstage_ref)
    for f in range(4):
        lstage_ref[f * PAD : f * PAD + lift_ref.shape[0], :basis] = lift_ref[:, f, :]
    wide = jnp.transpose(lstage_ref[...], (1, 0))[:64]
    high = wide.astype(BF16).astype(F32)
    low = wide - high
    rolled = pltpu.roll(high, 4 * PAD, 1)
    lane = lax.broadcasted_iota(I32, (64, 128), 1)
    lleft_ref[:, 0:128] = jnp.where(lane < 4 * PAD, high, rolled).astype(BF16)
    lleft_ref[:, 128:256] = jnp.where(lane < 8 * PAD - 128, rolled, 0.0).astype(BF16)
    llow_ref[...] = low.astype(BF16)


def kernel_local_second(sizes, *refs):
    (second_ref, middle_ref, star_ref, kleft_ref, proj_ref, faces_ref, minus_ref, oleft_ref, pick_ref, turn_ref,
     partial_ref, gath_ref, comb_ref, moved_ref) = refs
    volume_part(second_ref, middle_ref, star_ref, kleft_ref[...], moved_ref, partial_ref, sizes)
    interior_part(faces_ref, pick_ref, oleft_ref[...], turn_ref[...], gath_ref, sizes)
    own_part(proj_ref, minus_ref, comb_ref, sizes)


def neighbour_part(ins, oleft_ref, ghost_turn_ref, ghost_pick_ref, gath_ref, comb_ref, plus_ref, lleft_ref, llow_ref,
                   partial_ref, slot_ref, ghost_ref, gsum_ref, sizes):
    variables, basis, rows = sizes.variables, sizes.basis, sizes.rows
    received = unpack(ins, slot_ref, sizes)
    blocks = [received[q * PAD : (q + 1) * PAD] for q in range(variables)]
    turned = turn_blocks(blocks, oleft_ref[...], ghost_turn_ref[...])
    high, low = split(pad_to(jnp.concatenate(turned, axis=0), rows, turned[0].shape[1]))
    ghost_ref[0:rows, :] = high
    ghost_ref[rows : 2 * rows, :] = low
    both = dot(ghost_ref[...], ghost_pick_ref[...])
    used = variables * PAD
    gsum_ref[...] = gath_ref[...] + (both[0:used] + both[rows : rows + used])
    for g in groups(sizes):
        highs, stacks = [], []
        faces = [[], [], []]
        for f in range(4):
            frows = slice(f * PAD, (f + 1) * PAD)
            acc = []
            for i in range(GROUP):
                p = g * GROUP + i
                acc.append(comb_ref[frows, p * 128 : (p + 1) * 128])
            for q in range(variables):
                block = gsum_ref[q * PAD : (q + 1) * PAD, f * 128 : (f + 1) * 128]
                for i in range(GROUP):
                    row = (q * variables + g * GROUP + i) * 4 + f
                    acc[i] = acc[i] + block * plus_ref[row : row + 1, :]
            for i in range(GROUP):
                faces[i].append(acc[i])
        for i in range(GROUP):
            high, low = split(jnp.concatenate(faces[i], axis=0))
            highs.append(high)
            stacks.append(jnp.concatenate([high, low], axis=0))
        lifted = dot(lleft_ref[:, : 8 * PAD], jnp.concatenate(stacks, axis=1)) + dot(
            llow_ref[:, : 4 * PAD], jnp.concatenate(highs, axis=1)
        )
        yield g, [
            partial_ref[g * GROUP + i] + lifted[:basis, i * 128 : (i + 1) * 128] for i in range(GROUP)
        ]


def kernel_second(sizes, *refs):
    xs = sizes.sub_count // 2 - 1
    ra_ref, rb_ref, r1_ref, *refs = refs
    rk_refs, refs = refs[:xs], refs[xs:]
    (oleft_ref, ghost_turn_ref, ghost_pick_ref, gath_ref, comb_ref, plus_ref, lleft_ref, llow_ref, partial_ref,
     star_ref, late_ref, cluster_ref, dleft_ref, rleft_ref, pick_ref, pick_sub_ref,
     middle_ref, second_ref, proj_ref, faces_ref, pa_ref, pb_ref, p1_ref, *rest) = refs
    pk_refs, rest = rest[:xs], rest[xs:]
    moved_ref, other_ref, slot_ref, pslot_ref, ghost_ref, gsum_ref = rest
    left = dleft_ref[...]
    for g, values in neighbour_part((ra_ref, rb_ref, r1_ref, rk_refs), oleft_ref, ghost_turn_ref, ghost_pick_ref,
                                    gath_ref, comb_ref, plus_ref, lleft_ref, llow_ref, partial_ref, slot_ref,
                                    ghost_ref, gsum_ref, sizes):
        moved_ref[:, group_lanes(g)] = dot(left, stack_right(values))[: moved_ref.shape[0]]
        for i in range(GROUP):
            middle_ref[g * GROUP + i] = values[i]
            second_ref[g * GROUP + i] = values[i] * HALF
    fine = cluster_ref[...] == 1

    def finish(p, first):
        value = jnp.where(fine, first, late_ref[p])
        second_ref[p] = value
        return value

    for g, values in predictor(moved_ref, other_ref, star_ref, left, second_ref, None, sizes, finish):
        project(g, values, rleft_ref[...], proj_ref)
    by_face(proj_ref, faces_ref, sizes)
    payloads(faces_ref, pick_ref, pick_sub_ref, pslot_ref, (pa_ref, pb_ref, p1_ref, pk_refs), sizes)


def kernel_last(sizes, *refs):
    xs = sizes.sub_count // 2 - 1
    ra_ref, rb_ref, r1_ref, *refs = refs
    rk_refs, refs = refs[:xs], refs[xs:]
    (oleft_ref, ghost_turn_ref, ghost_pick_ref, gath_ref, comb_ref, plus_ref, lleft_ref, llow_ref, partial_ref,
     out_hbm, slot_ref, ghost_ref, gsum_ref, out_ref, sems) = refs
    copies = []
    for g, values in neighbour_part((ra_ref, rb_ref, r1_ref, rk_refs), oleft_ref, ghost_turn_ref, ghost_pick_ref,
                                    gath_ref, comb_ref, plus_ref, lleft_ref, llow_ref, partial_ref, slot_ref,
                                    ghost_ref, gsum_ref, sizes):
        for i in range(GROUP):
            out_ref[g * GROUP + i] = values[i]
        part = pl.ds(g * GROUP, GROUP)
        copies.append(pltpu.make_async_copy(out_ref.at[part], out_hbm.at[part], sems.at[g]))
        copies[-1].start()
    for copy in copies:
        copy.wait()


def body(
    dom_count,
    sub_count,
    modal_state,
    cluster_id,
    jacobian_id,
    face_neighbour,
    flux_index,
    send_list,
    derivative,
    stiffness,
    restriction,
    lifting,
    orientation,
    star_matrix,
    flux_minus,
    flux_plus,
):
    basis, variables, elements = modal_state.shape
    ghosts = send_list.shape[0]
    cap_sub = (ghosts - 2 * CAP_DOM) // sub_count
    lanes = variables * elements
    half_rows = -(-variables * PAD // 32) * 16
    rows = 2 * half_rows
    sizes = Sizes(variables, basis, sub_count, cap_sub, rows, half_rows)
    sub_lanes = -(-rows // 128) * 128
    mat_rows = variables * variables * 4 + 4
    xs = sub_count // 2 - 1

    state = jnp.transpose(modal_state, (1, 0, 2))
    star_table = jnp.transpose(star_matrix, (2, 3, 1, 0))
    minus_table = jnp.transpose(flux_minus, (2, 3, 1, 0))
    plus_table = jnp.transpose(flux_plus, (2, 3, 1, 0))
    restrict = jnp.transpose(restriction, (1, 0, 2))
    lift = jnp.transpose(lifting, (2, 0, 1))
    classes = jacobian_id.reshape(1, elements)
    clusters = cluster_id.reshape(1, elements)
    sends = send_list.reshape(1, ghosts)

    def sds(*shape, dtype=F32):
        return jax.ShapeDtypeStruct(shape, dtype)

    def like(x):
        return sds(*x.shape, dtype=x.dtype)

    whole = sds(variables, basis, elements)
    face_t = sds(4 * PAD, lanes)
    faces_t = sds(2 * rows, 4 * elements, dtype=BF16)
    mat_t = sds(mat_rows, 128)
    gath_t = sds(variables * PAD, 4 * elements)
    left_t = sds(-(-3 * basis // 16) * 16, 3 * SEC, dtype=BF16)
    pay_t = [sds(half_rows, 128)] * 2 + [sds(cap_sub * (xs + 1), sub_lanes)] + [sds(cap_sub, sub_lanes)] * xs

    def scratch(t):
        return pltpu.VMEM(t.shape, t.dtype)

    moved_s = pltpu.VMEM((3 * basis, lanes), F32)
    stage_s = pltpu.VMEM((mat_rows, 128), F32)
    slot_s = pltpu.VMEM((128, sub_lanes), F32)
    pslot_s = pltpu.VMEM((ghosts - 2 * CAP_DOM, sub_lanes), F32)
    ghost_s = pltpu.VMEM((2 * rows, 256), BF16)

    def call(fn, outs, scratches, operands, flops, space=pltpu.VMEM, out_space=pltpu.VMEM):
        vmem = pl.BlockSpec(memory_space=out_space)
        if space is pltpu.HBM:
            operands = [pltpu.with_memory_space_constraint(x, pltpu.HBM) for x in operands]
        return pl.pallas_call(
            functools.partial(fn, sizes),
            out_shape=outs,
            in_specs=[pl.BlockSpec(memory_space=space)] * len(operands),
            out_specs=jax.tree.map(lambda _: vmem, outs),
            scratch_shapes=scratches,
            cost_estimate=pl.CostEstimate(flops=flops, bytes_accessed=2_000_000, transcendentals=0),
            compiler_params=pltpu.CompilerParams(vmem_limit_bytes=24 * 1024 * 1024),
        )(*operands)

    combined = ("dom", "sub")

    def device(d, s):
        return d * sub_count + s

    def pairs(target):
        return [(device(d, s), device(*target(d, s))) for d in range(dom_count) for s in range(sub_count)]

    even_pairs = pairs(lambda d, s: (d ^ 1, s))
    odd_pairs = pairs(lambda d, s: (((d + 1) ^ 1) - 1, s) if 0 < d < dom_count - 1 else (d, s ^ 1))

    def sub_pairs(k):
        return pairs(lambda d, s: (d, s ^ k))

    def trade(payload):
        pa, pb, p1, *pk = payload
        r1 = lax.ppermute(p1, combined, sub_pairs(1))
        rb = lax.ppermute(pb, combined, odd_pairs)
        ra = lax.ppermute(pa, combined, even_pairs)
        rk = []
        for i, part in enumerate(pk):
            passed = r1[(i + 1) * cap_sub : (i + 2) * cap_sub]
            rk.append(lax.ppermute(jnp.concatenate([part, passed], axis=0), combined, sub_pairs(2 * i + 2)))
        return [ra, rb, r1, *rk]

    later = [clusters, minus_table, plus_table, face_neighbour, flux_index, stiffness, lift, orientation]
    outs = call(
        kernel_predict,
        [like(x) for x in [classes, *later]]
        + [whole, whole, whole, face_t, faces_t, mat_t, left_t, sds(4 * PAD, 3 * SEC, dtype=BF16)]
        + [sds(4 * elements, 128, dtype=BF16), sds(ghosts - 2 * CAP_DOM, 4 * elements, dtype=BF16)]
        + pay_t,
        [
            scratch(star_table), scratch(derivative), scratch(restrict), scratch(sends),
            moved_s, moved_s, stage_s, pltpu.VMEM((4 * PAD, 128), F32), pslot_s, pltpu.SemaphoreType.DMA((14,)),
        ],
        [state, classes, star_table, derivative, restrict, sends, *later],
        60_000_000,
        pltpu.HBM,
    )
    clusters, minus_table, plus_table, code, flux, stiff, lift, orient = outs[1:9]
    classes = outs[0]
    state, first, late, proj, faces, star, dleft, rleft, pick_send, pick_sub, *payload = outs[9:]
    received = trade(payload)
    (partial, gath, comb, minus, plus, kleft, oleft, lleft, llow, pick, ghost_pick, turn, ghost_turn) = call(
        kernel_local_first,
        [whole, gath_t, face_t, mat_t, mat_t, left_t, sds(80, 3 * OSEC, dtype=BF16)]
        + [sds(64, 256, dtype=BF16), sds(64, 128, dtype=BF16)]
        + [sds(4 * elements, 4 * elements, dtype=BF16), sds(256, 4 * elements, dtype=BF16)]
        + [sds(1, 4 * elements, dtype=I32), sds(1, 256, dtype=I32)],
        [moved_s, stage_s, pltpu.VMEM((128, 128), F32)],
        [classes, minus_table, plus_table, code, flux, stiff, lift, orient, first, state, star, proj, faces],
        30_000_000,
    )
    common = [oleft, ghost_turn, ghost_pick]
    middle, second, proj, faces, *payload = call(
        kernel_second,
        [whole, whole, face_t, faces_t] + pay_t,
        [moved_s, moved_s, slot_s, pslot_s, ghost_s, scratch(gath_t)],
        received
        + common
        + [gath, comb, plus, lleft, llow, partial, star, late, clusters, dleft, rleft, pick_send, pick_sub],
        70_000_000,
    )
    received = trade(payload)
    partial, gath, comb = call(
        kernel_local_second,
        [whole, gath_t, face_t],
        [moved_s],
        [second, middle, star, kleft, proj, faces, minus, oleft, pick, turn],
        30_000_000,
    )
    result = call(
        kernel_last,
        whole,
        [slot_s, ghost_s, scratch(gath_t), scratch(whole), pltpu.SemaphoreType.DMA((variables // GROUP,))],
        received + common + [gath, comb, plus, lleft, llow, partial],
        10_000_000,
        out_space=pltpu.HBM,
    )
    return jnp.transpose(result, (1, 0, 2))


def solution(mesh):
    placed = (
        P(None, None, ("dom", "sub")),
        P(("dom", "sub")),
        P(("dom", "sub")),
        P(None, ("dom", "sub")),
        P(None, ("dom", "sub")),
        P(("dom", "sub")),
        P(),
        P(),
        P(),
        P(),
        P(),
        P(),
        P(),
        P(),
    )
    return jax.shard_map(
        functools.partial(body, mesh.shape["dom"], mesh.shape["sub"]),
        mesh=mesh,
        in_specs=placed,
        out_specs=P(None, None, ("dom", "sub")),
        check_vma=False,
    )
```

```python
import collections
import functools

import jax
import jax.numpy as jnp
from jax import lax
from jax.experimental import pallas as pl
from jax.experimental.pallas import tpu as pltpu
from jax.sharding import PartitionSpec as P

ORDER = 6
CAP_DOM = 64
HALF = 0.5
PAD = 24
SEC = 64
OSEC = 32
GROUP = 3

F32 = jnp.float32
BF16 = jnp.bfloat16
I32 = jnp.int32

Sizes = collections.namedtuple(
    "Sizes", ["variables", "basis", "sub_count", "cap_sub", "rows", "half_rows"]
)


def split(x):
    high = x.astype(BF16)
    low = (x - high.astype(F32)).astype(BF16)
    return high, low


def dot(a, b):
    return lax.dot_general(a, b, (((1,), (0,)), ((), ())), preferred_element_type=F32)


def dot_nt(a, b):
    return lax.dot_general(a, b, (((1,), (1,)), ((), ())), preferred_element_type=F32)


def pad_to(x, rows, lanes):
    m, k = x.shape
    if lanes > k:
        x = jnp.concatenate([x, jnp.zeros((m, lanes - k), x.dtype)], axis=1)
    if rows > m:
        x = jnp.concatenate([x, jnp.zeros((rows - m, lanes), x.dtype)], axis=0)
    return x


def stack_left(matrix):
    m = -(-matrix.shape[0] // 16) * 16
    wide = pad_to(matrix, m, 128)
    high = wide.astype(BF16).astype(F32)
    low = wide - high
    both = high + pltpu.roll(high, SEC, 1)
    return jnp.concatenate([both.astype(BF16), low.astype(BF16)], axis=1)[:, : 3 * SEC]


def stack_right(blocks):
    out = []
    for x in blocks:
        high, low = split(pad_to(x, SEC, x.shape[1]))
        out.append(jnp.concatenate([high, low, high], axis=0))
    return jnp.concatenate(out, axis=1) if len(out) > 1 else out[0]


def mix_group(moved_ref, star_ref, sizes, g):
    basis, variables = sizes.basis, sizes.variables
    acc = [None] * GROUP
    for q in range(variables):
        for d in range(3):
            block = moved_ref[d * basis : (d + 1) * basis, q * 128 : (q + 1) * 128]
            for i in range(GROUP):
                row = (q * variables + g * GROUP + i) * 4 + d
                term = block * star_ref[row : row + 1, :]
                acc[i] = term if acc[i] is None else acc[i] + term
    return acc


def lookup(table_ref, stage_ref, class_row, out_ref):
    nq, np_, parts, classes = table_ref.shape
    for q in range(nq):
        for p in range(np_):
            row = (q * np_ + p) * 4
            stage_ref[row : row + parts, :classes] = table_ref[q, p]
    rows = stage_ref.shape[0]
    high, low = split(stage_ref[:, :classes])
    onehot = (lax.broadcasted_iota(I32, (classes, 128), 0) == class_row).astype(F32).astype(BF16)
    out_ref[0:rows, :] = dot(high, onehot) + dot(low, onehot)


def groups(sizes):
    return range(sizes.variables // GROUP)


def group_lanes(g):
    return slice(g * GROUP * 128, (g + 1) * GROUP * 128)


def advance(src_ref, dst_ref, star_ref, left, sizes, emit, between):
    for g in groups(sizes):
        acc = mix_group(src_ref, star_ref, sizes, g)
        for i in range(GROUP):
            emit(g * GROUP + i, acc[i])
        dst_ref[:, group_lanes(g)] = dot(left, stack_right(acc))[: dst_ref.shape[0]]
        between()


def predictor(moved_ref, other_ref, star_ref, left, first_ref, late_ref, sizes, finish, extra=()):
    extra = list(extra)

    def between():
        if extra:
            extra.pop(0)()

    def weigh(weights, degree):
        w_half, w_full = weights
        scale = -1.0 / (degree + 1)
        return w_half * (scale * HALF), w_full * scale

    def emitter(weights):
        w_half, w_full = weights

        def emit(p, value):
            first_ref[p] += w_half * value
            if late_ref is not None:
                late_ref[p] += (w_full - w_half) * value

        return emit

    def two(i, weights):
        weights = weigh(weights, 2 * i + 1)
        advance(moved_ref, other_ref, star_ref, left, sizes, emitter(weights), between)
        weights = weigh(weights, 2 * i + 2)
        advance(other_ref, moved_ref, star_ref, left, sizes, emitter(weights), between)
        return weights

    steps = ORDER - 1
    weights = (HALF, 1.0)
    for i in range(steps // 2):
        weights = two(i, weights)
    w_half, w_full = weigh(weights, steps)
    for g in groups(sizes):
        acc = mix_group(moved_ref, star_ref, sizes, g)
        values = []
        for i in range(GROUP):
            p = g * GROUP + i
            first = first_ref[p] + w_half * acc[i]
            if late_ref is not None:
                late_ref[p] += (w_full - w_half) * acc[i]
            values.append(finish(p, first))
        yield g, values


def project(g, values, left, proj_ref):
    proj_ref[:, group_lanes(g)] = dot(left, stack_right(values))


def by_face(proj_ref, faces_ref, sizes):
    rows = sizes.rows
    for f in range(4):
        pieces = [
            proj_ref[f * PAD : (f + 1) * PAD, q * 128 : (q + 1) * 128] for q in range(sizes.variables)
        ]
        high, low = split(pad_to(jnp.concatenate(pieces, axis=0), rows, 128))
        faces_ref[0:rows, f * 128 : (f + 1) * 128] = high
        faces_ref[rows : 2 * rows, f * 128 : (f + 1) * 128] = low


def is_even():
    return lax.rem(lax.axis_index("dom"), 2) == 0


def low_lanes(shape):
    return lax.broadcasted_iota(I32, shape, 1) < CAP_DOM


def picks_of_sends(send_ref, pick_ref, pick_sub_ref):
    ghosts = send_ref.shape[1]
    row = send_ref[...].astype(F32)
    dom_row = row[:, 0:128]
    dom_row = jnp.where(is_even(), pltpu.roll(dom_row, CAP_DOM, 1), dom_row)
    place = lax.broadcasted_iota(I32, (128, 128), 0).astype(F32)
    for f in range(4):
        pick_ref[f * 128 : (f + 1) * 128, :] = (place + f * 128 == dom_row).astype(F32).astype(BF16)
    subs = ghosts - 128
    sub_row = pad_to(row[:, 128:], 1, 128)
    column = jnp.transpose(jnp.broadcast_to(sub_row, (128, 128)), (1, 0))[:subs]
    lane = lax.broadcasted_iota(I32, (subs, 128), 1).astype(F32)
    for f in range(4):
        pick_sub_ref[:, f * 128 : (f + 1) * 128] = (column == lane + f * 128).astype(F32).astype(BF16)


def payloads(faces_ref, pick_ref, pick_sub_ref, slot_ref, outs, sizes):
    pa_ref, pb_ref, p1_ref, pk_refs = outs
    rows, half = sizes.rows, sizes.half_rows
    sub = dot_nt(pick_sub_ref[...], faces_ref[0:rows, :]) + dot_nt(pick_sub_ref[...], faces_ref[rows : 2 * rows, :])
    slot_ref[...] = pad_to(sub, sub.shape[0], slot_ref.shape[1])
    both = dot(faces_ref[...], pick_ref[...])
    both = both[0:rows] + both[rows : 2 * rows]
    top, bottom = both[0:half], both[half:]
    low = low_lanes((half, 128))
    pa_ref[...] = jnp.where(low, top, pltpu.roll(bottom, CAP_DOM, 1))
    pb_ref[...] = jnp.where(low, pltpu.roll(top, CAP_DOM, 1), bottom)
    me = lax.axis_index("sub")
    cap = sizes.cap_sub

    def block(k):
        return slot_ref[pl.ds(pl.multiple_of(jnp.bitwise_xor(me, k) * cap, 8), cap), :]

    p1_ref[0:cap, :] = block(1)
    for i, k in enumerate(range(2, sizes.sub_count, 2)):
        p1_ref[(i + 1) * cap : (i + 2) * cap, :] = block(k + 1)
        pk_refs[i][...] = block(k)


def unpack(ins, slot_ref, sizes):
    ra_ref, rb_ref, r1_ref, rk_refs = ins
    ra, rb = ra_ref[...], rb_ref[...]
    low = low_lanes(ra.shape)
    top = jnp.where(low, ra, pltpu.roll(rb, CAP_DOM, 1))
    bottom = jnp.where(low, pltpu.roll(ra, CAP_DOM, 1), rb)
    dom = jnp.concatenate([top, bottom], axis=0)
    me = lax.axis_index("sub")
    cap = sizes.cap_sub
    slot_ref[...] = jnp.zeros_like(slot_ref)

    def put(k, value):
        slot_ref[pl.ds(pl.multiple_of(jnp.bitwise_xor(me, k) * cap, 8), cap), :] = value

    put(1, r1_ref[0:cap, :])
    for i, k in enumerate(range(2, sizes.sub_count, 2)):
        put(k, rk_refs[i][0:cap, :])
        put(k + 1, rk_refs[i][cap : 2 * cap, :])
    sub = jnp.transpose(slot_ref[...], (1, 0))[: dom.shape[0]]
    return jnp.concatenate([dom, sub], axis=1)


def turn_blocks(values, left, turns):
    stacks = []
    for value in values:
        high, low = split(pad_to(value, OSEC, value.shape[1]))
        stacks.append(jnp.concatenate([high, low, high], axis=0))
    width = values[0].shape[1]
    whole = dot(left, jnp.concatenate(stacks, axis=1))
    out = []
    for q in range(len(values)):
        turned = whole[:, q * width : (q + 1) * width]
        out.append(
            jnp.where(
                turns == 0,
                turned[0:PAD],
                jnp.where(turns == 1, turned[PAD : 2 * PAD], turned[2 * PAD : 3 * PAD]),
            )
        )
    return out


def orient_left(orient_ref):
    blocks = [pad_to(orient_ref[h], PAD, 128) for h in range(3)]
    wide = pad_to(jnp.concatenate(blocks, axis=0), 80, 128)
    high = wide.astype(BF16).astype(F32)
    low = wide - high
    stacked = high + pltpu.roll(high, OSEC, 1) + pltpu.roll(low, 2 * OSEC, 1)
    return stacked.astype(BF16)[:, : 3 * OSEC]


def face_of(flux):
    return (flux >= 3).astype(I32) + (flux >= 6).astype(I32) + (flux >= 9).astype(I32)


def kernel_predict(sizes, *refs):
    xs = sizes.sub_count // 2 - 1
    (state_hbm, class_hbm, table_hbm, deriv_hbm, restrict_hbm, send_hbm, *later_hbm) = refs[:14]
    refs = refs[14:]
    class_ref, refs = refs[0], refs[1:]
    later_refs, refs = refs[:8], refs[8:]
    (state_ref, first_ref, late_ref, proj_ref, faces_ref, star_ref, dleft_ref, rleft_ref, pick_ref, pick_sub_ref,
     pa_ref, pb_ref, p1_ref, *rest) = refs
    pk_refs, rest = rest[:xs], rest[xs:]
    (table_ref, deriv_ref, restrict_ref, send_ref, moved_ref, other_ref, stage_ref, rstage_ref, slot_ref,
     sems) = rest
    sources = [class_hbm, table_hbm, deriv_hbm, state_hbm, send_hbm, restrict_hbm, *later_hbm]
    targets = [class_ref, table_ref, deriv_ref, state_ref, send_ref, restrict_ref, *later_refs]
    copies = [pltpu.make_async_copy(s, t, sems.at[i]) for i, (s, t) in enumerate(zip(sources, targets))]
    for copy in copies:
        copy.start()
    variables, basis = sizes.variables, sizes.basis
    copies[0].wait()
    copies[1].wait()
    lookup(table_ref, stage_ref, class_ref[...], star_ref)
    copies[2].wait()
    dleft_ref[...] = stack_left(jnp.reshape(deriv_ref[...], (3 * basis, basis)))
    left = dleft_ref[...]
    copies[3].wait()
    for g in groups(sizes):
        values = [state_ref[g * GROUP + i] for i in range(GROUP)]
        moved_ref[:, group_lanes(g)] = dot(left, stack_right(values))[: moved_ref.shape[0]]
        for i in range(GROUP):
            first_ref[g * GROUP + i] = values[i] * HALF
            late_ref[g * GROUP + i] = values[i] * (1.0 - HALF)
    for copy in copies[4:6]:
        copy.wait()
    def send_picks():
        picks_of_sends(send_ref, pick_ref, pick_sub_ref)

    def restrict_left():
        rstage_ref[...] = jnp.zeros_like(rstage_ref)
        for f in range(4):
            rstage_ref[f * PAD : f * PAD + restrict_ref.shape[0], :basis] = restrict_ref[:, f, :]
        rleft_ref[...] = stack_left(rstage_ref[:, :basis])

    send_picks()
    restrict_left()

    def finish(p, first):
        first_ref[p] = first
        return first

    for g, values in predictor(moved_ref, other_ref, star_ref, left, first_ref, late_ref, sizes, finish,
                               []):
        project(g, values, rleft_ref[...], proj_ref)
    by_face(proj_ref, faces_ref, sizes)
    payloads(faces_ref, pick_ref, pick_sub_ref, slot_ref, (pa_ref, pb_ref, p1_ref, pk_refs), sizes)
    for copy in copies[6:]:
        copy.wait()


def volume_part(values_ref, base_ref, star_ref, kleft, moved_ref, partial_ref, sizes):
    for g in groups(sizes):
        values = [values_ref[g * GROUP + i] for i in range(GROUP)]
        moved_ref[:, group_lanes(g)] = dot(kleft, stack_right(values))[: moved_ref.shape[0]]
    for g in groups(sizes):
        acc = mix_group(moved_ref, star_ref, sizes, g)
        for i in range(GROUP):
            partial_ref[g * GROUP + i] = base_ref[g * GROUP + i] + acc[i]


def interior_part(faces_ref, pick_ref, oleft, turn, gath_ref, sizes):
    rows = sizes.rows
    both = dot(faces_ref[...], pick_ref[...])
    both = both[0:rows] + both[rows : 2 * rows]
    blocks = [both[q * PAD : (q + 1) * PAD] for q in range(sizes.variables)]
    for q, block in enumerate(turn_blocks(blocks, oleft, turn)):
        gath_ref[q * PAD : (q + 1) * PAD, :] = block


def own_part(proj_ref, minus_ref, comb_ref, sizes):
    variables = sizes.variables
    for f in range(4):
        rows = slice(f * PAD, (f + 1) * PAD)
        acc = [None] * variables
        for q in range(variables):
            block = proj_ref[rows, q * 128 : (q + 1) * 128]
            for p in range(variables):
                row = (q * variables + p) * 4 + f
                term = block * minus_ref[row : row + 1, :]
                acc[p] = term if acc[p] is None else acc[p] + term
        for p in range(variables):
            comb_ref[rows, p * 128 : (p + 1) * 128] = acc[p]


def kernel_local_first(sizes, *refs):
    (class_ref, minus_table, plus_table, code_ref, flux_ref, stiff_ref, lift_ref, orient_ref,
     first_ref, state_ref, star_ref, proj_ref, faces_ref,
     partial_ref, gath_ref, comb_ref, minus_ref, plus_ref, kleft_ref, oleft_ref, lleft_ref, llow_ref,
     pick_ref, ghost_pick_ref, turn_ref, ghost_turn_ref, moved_ref, stage_ref, lstage_ref) = refs
    basis = sizes.basis
    kleft_ref[...] = stack_left(jnp.reshape(stiff_ref[...], (3 * basis, basis)))
    volume_part(first_ref, state_ref, star_ref, kleft_ref[...], moved_ref, partial_ref, sizes)
    lookup(minus_table, stage_ref, class_ref[...], minus_ref)
    oleft_ref[...] = orient_left(orient_ref)
    code = code_ref[...]
    flux = flux_ref[...]
    face = face_of(flux)
    turn = flux - 3 * face
    turn_row = jnp.concatenate([turn[f : f + 1, :] for f in range(4)], axis=1)
    turn_ref[...] = turn_row
    place = lax.broadcasted_iota(I32, (128, 128), 0)
    target = jnp.where(code < 128, face * 128 + code, -1)
    for f in range(4):
        for j in range(4):
            pick_ref[j * 128 : (j + 1) * 128, f * 128 : (f + 1) * 128] = (
                (place + j * 128 == target[f : f + 1, :]).astype(F32).astype(BF16)
            )
    slot = code - 128
    swapped = jnp.where(slot < CAP_DOM, slot + CAP_DOM, jnp.where(slot < 2 * CAP_DOM, slot - CAP_DOM, slot))
    slot = jnp.where(is_even(), swapped, slot)
    slot = jnp.where(code < 128, -1, slot)
    for f in range(4):
        for j in range(2):
            ghost_pick_ref[j * 128 : (j + 1) * 128, f * 128 : (f + 1) * 128] = (
                (place + j * 128 == slot[f : f + 1, :]).astype(F32).astype(BF16)
            )
    rows = jnp.broadcast_to(turn_row.astype(F32), (16, 512)).astype(BF16)
    ghost_turn_ref[...] = dot_nt(rows, ghost_pick_ref[...])[0:1].astype(I32)
    interior_part(faces_ref, pick_ref, oleft_ref[...], turn_row, gath_ref, sizes)
    own_part(proj_ref, minus_ref, comb_ref, sizes)
    lookup(plus_table, stage_ref, class_ref[...], plus_ref)
    lstage_ref[...] = jnp.zeros_like(lstage_ref)
    for f in range(4):
        lstage_ref[f * PAD : f * PAD + lift_ref.shape[0], :basis] = lift_ref[:, f, :]
    wide = jnp.transpose(lstage_ref[...], (1, 0))[:64]
    high = wide.astype(BF16).astype(F32)
    low = wide - high
    rolled = pltpu.roll(high, 4 * PAD, 1)
    lane = lax.broadcasted_iota(I32, (64, 128), 1)
    lleft_ref[:, 0:128] = jnp.where(lane < 4 * PAD, high, rolled).astype(BF16)
    lleft_ref[:, 128:256] = jnp.where(lane < 8 * PAD - 128, rolled, 0.0).astype(BF16)
    llow_ref[...] = low.astype(BF16)


def kernel_local_second(sizes, *refs):
    (second_ref, middle_ref, star_ref, kleft_ref, proj_ref, faces_ref, minus_ref, oleft_ref, pick_ref, turn_ref,
     partial_ref, gath_ref, comb_ref, moved_ref) = refs
    volume_part(second_ref, middle_ref, star_ref, kleft_ref[...], moved_ref, partial_ref, sizes)
    interior_part(faces_ref, pick_ref, oleft_ref[...], turn_ref[...], gath_ref, sizes)
    own_part(proj_ref, minus_ref, comb_ref, sizes)


def neighbour_part(ins, oleft_ref, ghost_turn_ref, ghost_pick_ref, gath_ref, comb_ref, plus_ref, lleft_ref, llow_ref,
                   partial_ref, slot_ref, ghost_ref, gsum_ref, sizes):
    variables, basis, rows = sizes.variables, sizes.basis, sizes.rows
    received = unpack(ins, slot_ref, sizes)
    blocks = [received[q * PAD : (q + 1) * PAD] for q in range(variables)]
    turned = turn_blocks(blocks, oleft_ref[...], ghost_turn_ref[...])
    high, low = split(pad_to(jnp.concatenate(turned, axis=0), rows, turned[0].shape[1]))
    ghost_ref[0:rows, :] = high
    ghost_ref[rows : 2 * rows, :] = low
    both = dot(ghost_ref[...], ghost_pick_ref[...])
    used = variables * PAD
    gsum_ref[...] = gath_ref[...] + (both[0:used] + both[rows : rows + used])
    highs, stacks = [], []
    for g in groups(sizes):
        faces = [[], [], []]
        for f in range(4):
            frows = slice(f * PAD, (f + 1) * PAD)
            acc = []
            for i in range(GROUP):
                p = g * GROUP + i
                acc.append(comb_ref[frows, p * 128 : (p + 1) * 128])
            for q in range(variables):
                block = gsum_ref[q * PAD : (q + 1) * PAD, f * 128 : (f + 1) * 128]
                for i in range(GROUP):
                    row = (q * variables + g * GROUP + i) * 4 + f
                    acc[i] = acc[i] + block * plus_ref[row : row + 1, :]
            for i in range(GROUP):
                faces[i].append(acc[i])
        for i in range(GROUP):
            high, low = split(jnp.concatenate(faces[i], axis=0))
            highs.append(high)
            stacks.append(jnp.concatenate([high, low], axis=0))
    lifted = dot(lleft_ref[:, : 8 * PAD], jnp.concatenate(stacks, axis=1)) + dot(
        llow_ref[:, : 4 * PAD], jnp.concatenate(highs, axis=1)
    )
    for g in groups(sizes):
        yield g, [
            partial_ref[p] + lifted[:basis, p * 128 : (p + 1) * 128] for p in range(g * GROUP, (g + 1) * GROUP)
        ]


def kernel_second(sizes, *refs):
    xs = sizes.sub_count // 2 - 1
    ra_ref, rb_ref, r1_ref, *refs = refs
    rk_refs, refs = refs[:xs], refs[xs:]
    (oleft_ref, ghost_turn_ref, ghost_pick_ref, gath_ref, comb_ref, plus_ref, lleft_ref, llow_ref, partial_ref,
     star_ref, late_ref, cluster_ref, dleft_ref, rleft_ref, pick_ref, pick_sub_ref,
     middle_ref, second_ref, proj_ref, faces_ref, pa_ref, pb_ref, p1_ref, *rest) = refs
    pk_refs, rest = rest[:xs], rest[xs:]
    moved_ref, other_ref, slot_ref, pslot_ref, ghost_ref, gsum_ref = rest
    left = dleft_ref[...]
    for g, values in neighbour_part((ra_ref, rb_ref, r1_ref, rk_refs), oleft_ref, ghost_turn_ref, ghost_pick_ref,
                                    gath_ref, comb_ref, plus_ref, lleft_ref, llow_ref, partial_ref, slot_ref,
                                    ghost_ref, gsum_ref, sizes):
        moved_ref[:, group_lanes(g)] = dot(left, stack_right(values))[: moved_ref.shape[0]]
        for i in range(GROUP):
            middle_ref[g * GROUP + i] = values[i]
            second_ref[g * GROUP + i] = values[i] * HALF
    fine = cluster_ref[...] == 1

    def finish(p, first):
        value = jnp.where(fine, first, late_ref[p])
        second_ref[p] = value
        return value

    for g, values in predictor(moved_ref, other_ref, star_ref, left, second_ref, None, sizes, finish):
        project(g, values, rleft_ref[...], proj_ref)
    by_face(proj_ref, faces_ref, sizes)
    payloads(faces_ref, pick_ref, pick_sub_ref, pslot_ref, (pa_ref, pb_ref, p1_ref, pk_refs), sizes)


def kernel_last(sizes, *refs):
    xs = sizes.sub_count // 2 - 1
    ra_ref, rb_ref, r1_ref, *refs = refs
    rk_refs, refs = refs[:xs], refs[xs:]
    (oleft_ref, ghost_turn_ref, ghost_pick_ref, gath_ref, comb_ref, plus_ref, lleft_ref, llow_ref, partial_ref,
     out_hbm, slot_ref, ghost_ref, gsum_ref, out_ref, sems) = refs
    copies = []
    for g, values in neighbour_part((ra_ref, rb_ref, r1_ref, rk_refs), oleft_ref, ghost_turn_ref, ghost_pick_ref,
                                    gath_ref, comb_ref, plus_ref, lleft_ref, llow_ref, partial_ref, slot_ref,
                                    ghost_ref, gsum_ref, sizes):
        for i in range(GROUP):
            out_ref[g * GROUP + i] = values[i]
        part = pl.ds(g * GROUP, GROUP)
        copies.append(pltpu.make_async_copy(out_ref.at[part], out_hbm.at[part], sems.at[g]))
        copies[-1].start()
    for copy in copies:
        copy.wait()


def body(
    dom_count,
    sub_count,
    modal_state,
    cluster_id,
    jacobian_id,
    face_neighbour,
    flux_index,
    send_list,
    derivative,
    stiffness,
    restriction,
    lifting,
    orientation,
    star_matrix,
    flux_minus,
    flux_plus,
):
    basis, variables, elements = modal_state.shape
    ghosts = send_list.shape[0]
    cap_sub = (ghosts - 2 * CAP_DOM) // sub_count
    lanes = variables * elements
    half_rows = -(-variables * PAD // 32) * 16
    rows = 2 * half_rows
    sizes = Sizes(variables, basis, sub_count, cap_sub, rows, half_rows)
    sub_lanes = -(-rows // 128) * 128
    mat_rows = variables * variables * 4 + 4
    xs = sub_count // 2 - 1

    state = jnp.transpose(modal_state, (1, 0, 2))
    star_table = jnp.transpose(star_matrix, (2, 3, 1, 0))
    minus_table = jnp.transpose(flux_minus, (2, 3, 1, 0))
    plus_table = jnp.transpose(flux_plus, (2, 3, 1, 0))
    restrict = jnp.transpose(restriction, (1, 0, 2))
    lift = jnp.transpose(lifting, (2, 0, 1))
    classes = jacobian_id.reshape(1, elements)
    clusters = cluster_id.reshape(1, elements)
    sends = send_list.reshape(1, ghosts)

    def sds(*shape, dtype=F32):
        return jax.ShapeDtypeStruct(shape, dtype)

    def like(x):
        return sds(*x.shape, dtype=x.dtype)

    whole = sds(variables, basis, elements)
    face_t = sds(4 * PAD, lanes)
    faces_t = sds(2 * rows, 4 * elements, dtype=BF16)
    mat_t = sds(mat_rows, 128)
    gath_t = sds(variables * PAD, 4 * elements)
    left_t = sds(-(-3 * basis // 16) * 16, 3 * SEC, dtype=BF16)
    pay_t = [sds(half_rows, 128)] * 2 + [sds(cap_sub * (xs + 1), sub_lanes)] + [sds(cap_sub, sub_lanes)] * xs

    def scratch(t):
        return pltpu.VMEM(t.shape, t.dtype)

    moved_s = pltpu.VMEM((3 * basis, lanes), F32)
    stage_s = pltpu.VMEM((mat_rows, 128), F32)
    slot_s = pltpu.VMEM((128, sub_lanes), F32)
    pslot_s = pltpu.VMEM((ghosts - 2 * CAP_DOM, sub_lanes), F32)
    ghost_s = pltpu.VMEM((2 * rows, 256), BF16)

    def call(fn, outs, scratches, operands, flops, space=pltpu.VMEM, out_space=pltpu.VMEM):
        vmem = pl.BlockSpec(memory_space=out_space)
        if space is pltpu.HBM:
            operands = [pltpu.with_memory_space_constraint(x, pltpu.HBM) for x in operands]
        return pl.pallas_call(
            functools.partial(fn, sizes),
            out_shape=outs,
            in_specs=[pl.BlockSpec(memory_space=space)] * len(operands),
            out_specs=jax.tree.map(lambda _: vmem, outs),
            scratch_shapes=scratches,
            cost_estimate=pl.CostEstimate(flops=flops, bytes_accessed=2_000_000, transcendentals=0),
            compiler_params=pltpu.CompilerParams(vmem_limit_bytes=24 * 1024 * 1024),
        )(*operands)

    combined = ("dom", "sub")

    def device(d, s):
        return d * sub_count + s

    def pairs(target):
        return [(device(d, s), device(*target(d, s))) for d in range(dom_count) for s in range(sub_count)]

    even_pairs = pairs(lambda d, s: (d ^ 1, s))
    odd_pairs = pairs(lambda d, s: (((d + 1) ^ 1) - 1, s) if 0 < d < dom_count - 1 else (d, s ^ 1))

    def sub_pairs(k):
        return pairs(lambda d, s: (d, s ^ k))

    def trade(payload):
        pa, pb, p1, *pk = payload
        r1 = lax.ppermute(p1, combined, sub_pairs(1))
        rb = lax.ppermute(pb, combined, odd_pairs)
        ra = lax.ppermute(pa, combined, even_pairs)
        rk = []
        for i, part in enumerate(pk):
            passed = r1[(i + 1) * cap_sub : (i + 2) * cap_sub]
            rk.append(lax.ppermute(jnp.concatenate([part, passed], axis=0), combined, sub_pairs(2 * i + 2)))
        return [ra, rb, r1, *rk]

    later = [clusters, minus_table, plus_table, face_neighbour, flux_index, stiffness, lift, orientation]
    outs = call(
        kernel_predict,
        [like(x) for x in [classes, *later]]
        + [whole, whole, whole, face_t, faces_t, mat_t, left_t, sds(4 * PAD, 3 * SEC, dtype=BF16)]
        + [sds(4 * elements, 128, dtype=BF16), sds(ghosts - 2 * CAP_DOM, 4 * elements, dtype=BF16)]
        + pay_t,
        [
            scratch(star_table), scratch(derivative), scratch(restrict), scratch(sends),
            moved_s, moved_s, stage_s, pltpu.VMEM((4 * PAD, 128), F32), pslot_s, pltpu.SemaphoreType.DMA((14,)),
        ],
        [state, classes, star_table, derivative, restrict, sends, *later],
        60_000_000,
        pltpu.HBM,
    )
    clusters, minus_table, plus_table, code, flux, stiff, lift, orient = outs[1:9]
    classes = outs[0]
    state, first, late, proj, faces, star, dleft, rleft, pick_send, pick_sub, *payload = outs[9:]
    received = trade(payload)
    (partial, gath, comb, minus, plus, kleft, oleft, lleft, llow, pick, ghost_pick, turn, ghost_turn) = call(
        kernel_local_first,
        [whole, gath_t, face_t, mat_t, mat_t, left_t, sds(80, 3 * OSEC, dtype=BF16)]
        + [sds(64, 256, dtype=BF16), sds(64, 128, dtype=BF16)]
        + [sds(4 * elements, 4 * elements, dtype=BF16), sds(256, 4 * elements, dtype=BF16)]
        + [sds(1, 4 * elements, dtype=I32), sds(1, 256, dtype=I32)],
        [moved_s, stage_s, pltpu.VMEM((128, 128), F32)],
        [classes, minus_table, plus_table, code, flux, stiff, lift, orient, first, state, star, proj, faces],
        30_000_000,
    )
    common = [oleft, ghost_turn, ghost_pick]
    middle, second, proj, faces, *payload = call(
        kernel_second,
        [whole, whole, face_t, faces_t] + pay_t,
        [moved_s, moved_s, slot_s, pslot_s, ghost_s, scratch(gath_t)],
        received
        + common
        + [gath, comb, plus, lleft, llow, partial, star, late, clusters, dleft, rleft, pick_send, pick_sub],
        70_000_000,
    )
    received = trade(payload)
    partial, gath, comb = call(
        kernel_local_second,
        [whole, gath_t, face_t],
        [moved_s],
        [second, middle, star, kleft, proj, faces, minus, oleft, pick, turn],
        30_000_000,
    )
    result = call(
        kernel_last,
        whole,
        [slot_s, ghost_s, scratch(gath_t), scratch(whole), pltpu.SemaphoreType.DMA((variables // GROUP,))],
        received + common + [gath, comb, plus, lleft, llow, partial],
        10_000_000,
        out_space=pltpu.HBM,
    )
    return jnp.transpose(result, (1, 0, 2))


def solution(mesh):
    placed = (
        P(None, None, ("dom", "sub")),
        P(("dom", "sub")),
        P(("dom", "sub")),
        P(None, ("dom", "sub")),
        P(None, ("dom", "sub")),
        P(("dom", "sub")),
        P(),
        P(),
        P(),
        P(),
        P(),
        P(),
        P(),
        P(),
    )
    return jax.shard_map(
        functools.partial(body, mesh.shape["dom"], mesh.shape["sub"]),
        mesh=mesh,
        in_specs=placed,
        out_specs=P(None, None, ("dom", "sub")),
        check_vma=False,
    )
```

```python
import collections
import functools

import jax
import jax.numpy as jnp
from jax import lax
from jax.experimental import pallas as pl
from jax.experimental.pallas import tpu as pltpu
from jax.sharding import PartitionSpec as P

ORDER = 6
CAP_DOM = 64
HALF = 0.5
PAD = 24
SEC = 64
OSEC = 32
GROUP = 3

F32 = jnp.float32
BF16 = jnp.bfloat16
I32 = jnp.int32

Sizes = collections.namedtuple(
    "Sizes", ["variables", "basis", "sub_count", "cap_sub", "rows", "half_rows", "ghosts"]
)


def split(x):
    high = x.astype(BF16)
    low = (x - high.astype(F32)).astype(BF16)
    return high, low


def dot(a, b):
    return lax.dot_general(a, b, (((1,), (0,)), ((), ())), preferred_element_type=F32)


def dot_nt(a, b):
    return lax.dot_general(a, b, (((1,), (1,)), ((), ())), preferred_element_type=F32)


def pad_to(x, rows, lanes):
    m, k = x.shape
    if lanes > k:
        x = jnp.concatenate([x, jnp.zeros((m, lanes - k), x.dtype)], axis=1)
    if rows > m:
        x = jnp.concatenate([x, jnp.zeros((rows - m, lanes), x.dtype)], axis=0)
    return x


def stack_left(matrix):
    m = -(-matrix.shape[0] // 16) * 16
    wide = pad_to(matrix, m, 128)
    high = wide.astype(BF16).astype(F32)
    low = wide - high
    both = high + pltpu.roll(high, SEC, 1)
    return jnp.concatenate([both.astype(BF16), low.astype(BF16)], axis=1)[:, : 3 * SEC]


def stack_right(blocks):
    out = []
    for x in blocks:
        high, low = split(pad_to(x, SEC, x.shape[1]))
        out.append(jnp.concatenate([high, low, high], axis=0))
    return jnp.concatenate(out, axis=1) if len(out) > 1 else out[0]


def order_after(x):
    return split(x)[1].astype(F32) * 0.0


def mix_group(moved_ref, star_ref, sizes, g, zero=None):
    basis, variables = sizes.basis, sizes.variables
    acc = [zero] * GROUP
    for q in range(variables):
        for d in range(3):
            block = moved_ref[d * basis : (d + 1) * basis, q * 128 : (q + 1) * 128]
            for i in range(GROUP):
                row = (q * variables + g * GROUP + i) * 4 + d
                term = block * star_ref[row : row + 1, :]
                acc[i] = term if acc[i] is None else acc[i] + term
    return acc


def lookup(table_ref, stage_ref, class_row, out_ref):
    nq, np_, parts, classes = table_ref.shape
    for q in range(nq):
        for p in range(np_):
            row = (q * np_ + p) * 4
            stage_ref[row : row + parts, :classes] = table_ref[q, p]
    rows = stage_ref.shape[0]
    high, low = split(stage_ref[:, :classes])
    onehot = (lax.broadcasted_iota(I32, (classes, 128), 0) == class_row).astype(F32).astype(BF16)
    out_ref[0:rows, :] = dot(high, onehot) + dot(low, onehot)


def groups(sizes):
    return range(sizes.variables // GROUP)


def group_lanes(g):
    return slice(g * GROUP * 128, (g + 1) * GROUP * 128)


def advance(src_ref, dst_ref, star_ref, left, sizes, emit, between):
    zero = None
    for g in groups(sizes):
        acc = mix_group(src_ref, star_ref, sizes, g, zero)
        zero = order_after(acc[-1])
        for i in range(GROUP):
            emit(g * GROUP + i, acc[i])
        dst_ref[:, group_lanes(g)] = dot(left, stack_right(acc))[: dst_ref.shape[0]]
        between()


def predictor(moved_ref, other_ref, star_ref, left, first_ref, late_ref, sizes, finish, extra=()):
    extra = list(extra)

    def between():
        if extra:
            extra.pop(0)()

    def weigh(weights, degree):
        w_half, w_full = weights
        scale = -1.0 / (degree + 1)
        return w_half * (scale * HALF), w_full * scale

    def emitter(weights):
        w_half, w_full = weights

        def emit(p, value):
            first_ref[p] += w_half * value
            if late_ref is not None:
                late_ref[p] += (w_full - w_half) * value

        return emit

    def two(i, weights):
        weights = weigh(weights, 2 * i + 1)
        advance(moved_ref, other_ref, star_ref, left, sizes, emitter(weights), between)
        weights = weigh(weights, 2 * i + 2)
        advance(other_ref, moved_ref, star_ref, left, sizes, emitter(weights), between)
        return weights

    steps = ORDER - 1
    weights = (HALF, 1.0)
    for i in range(steps // 2):
        weights = two(i, weights)
    w_half, w_full = weigh(weights, steps)
    for g in groups(sizes):
        acc = mix_group(moved_ref, star_ref, sizes, g)
        values = []
        for i in range(GROUP):
            p = g * GROUP + i
            first = first_ref[p] + w_half * acc[i]
            if late_ref is not None:
                late_ref[p] += (w_full - w_half) * acc[i]
            values.append(finish(p, first))
        yield g, values


def project(g, values, left, proj_ref):
    proj_ref[:, group_lanes(g)] = dot(left, stack_right(values))


def by_face(proj_ref, faces_ref, sizes):
    rows = sizes.rows
    for f in range(4):
        pieces = [
            proj_ref[f * PAD : (f + 1) * PAD, q * 128 : (q + 1) * 128] for q in range(sizes.variables)
        ]
        high, low = split(pad_to(jnp.concatenate(pieces, axis=0), rows, 128))
        faces_ref[0:rows, f * 128 : (f + 1) * 128] = high
        faces_ref[rows : 2 * rows, f * 128 : (f + 1) * 128] = low


def is_even():
    return lax.rem(lax.axis_index("dom"), 2) == 0


def low_lanes(shape):
    return lax.broadcasted_iota(I32, shape, 1) < CAP_DOM


def picks_of_sends(send_ref, pick_ref, pick_sub_ref):
    ghosts = send_ref.shape[1]
    row = send_ref[...].astype(F32)
    dom_row = row[:, 0:128]
    dom_row = jnp.where(is_even(), pltpu.roll(dom_row, CAP_DOM, 1), dom_row)
    place = lax.broadcasted_iota(I32, (128, 128), 0).astype(F32)
    for f in range(4):
        pick_ref[f * 128 : (f + 1) * 128, :] = (place + f * 128 == dom_row).astype(F32).astype(BF16)
    subs = ghosts - 128
    sub_row = pad_to(row[:, 128:], 1, 128)
    column = jnp.transpose(jnp.broadcast_to(sub_row, (128, 128)), (1, 0))[:subs]
    lane = lax.broadcasted_iota(I32, (subs, 128), 1).astype(F32)
    for f in range(4):
        pick_sub_ref[:, f * 128 : (f + 1) * 128] = (column == lane + f * 128).astype(F32).astype(BF16)


def payloads(faces_ref, pick_ref, pick_sub_ref, slot_ref, outs, sizes):
    pa_ref, pb_ref, p1_ref, pk_refs = outs
    rows, half = sizes.rows, sizes.half_rows
    sub = dot_nt(pick_sub_ref[...], faces_ref[0:rows, :]) + dot_nt(pick_sub_ref[...], faces_ref[rows : 2 * rows, :])
    slot_ref[...] = pad_to(sub, sub.shape[0], slot_ref.shape[1])
    both = dot(faces_ref[...], pick_ref[...])
    both = both[0:rows] + both[rows : 2 * rows]
    top, bottom = both[0:half], both[half:]
    low = low_lanes((half, 128))
    pa_ref[...] = jnp.where(low, top, pltpu.roll(bottom, CAP_DOM, 1))
    pb_ref[...] = jnp.where(low, pltpu.roll(top, CAP_DOM, 1), bottom)
    me = lax.axis_index("sub")
    cap = sizes.cap_sub

    def block(k):
        return slot_ref[pl.ds(pl.multiple_of(jnp.bitwise_xor(me, k) * cap, 8), cap), :]

    p1_ref[0:cap, :] = block(1)
    for i, k in enumerate(range(2, sizes.sub_count, 2)):
        p1_ref[(i + 1) * cap : (i + 2) * cap, :] = block(k + 1)
        pk_refs[i][...] = block(k)


def by_rows(received):
    return jnp.concatenate([received, pltpu.roll(received, CAP_DOM, 1)], axis=0)


def with_subs(dom, r1_ref, rk_refs, slot_ref, sizes):
    me = lax.axis_index("sub")
    cap = sizes.cap_sub
    slot_ref[...] = jnp.zeros_like(slot_ref)

    def put(k, value):
        start = pl.multiple_of(CAP_DOM + jnp.bitwise_xor(me, k) * cap, 8)
        slot_ref[pl.ds(start, cap), :] = value

    put(1, r1_ref[0:cap, :])
    for i, k in enumerate(range(2, sizes.sub_count, 2)):
        put(k, rk_refs[i][0:cap, :])
        put(k + 1, rk_refs[i][cap : 2 * cap, :])
    sub = jnp.transpose(slot_ref[...], (1, 0))[: dom.shape[0]]
    return jnp.where(low_lanes(dom.shape), dom, sub)


def turn_blocks(values, left, turns):
    stacks = []
    for value in values:
        high, low = split(pad_to(value, OSEC, value.shape[1]))
        stacks.append(jnp.concatenate([high, low, high], axis=0))
    width = values[0].shape[1]
    whole = dot(left, jnp.concatenate(stacks, axis=1))
    out = []
    for q in range(len(values)):
        turned = whole[:, q * width : (q + 1) * width]
        out.append(
            jnp.where(
                turns == 0,
                turned[0:PAD],
                jnp.where(turns == 1, turned[PAD : 2 * PAD], turned[2 * PAD : 3 * PAD]),
            )
        )
    return out


def orient_left(orient_ref):
    blocks = [pad_to(orient_ref[h], PAD, 128) for h in range(3)]
    wide = pad_to(jnp.concatenate(blocks, axis=0), 80, 128)
    high = wide.astype(BF16).astype(F32)
    low = wide - high
    stacked = high + pltpu.roll(high, OSEC, 1) + pltpu.roll(low, 2 * OSEC, 1)
    return stacked.astype(BF16)[:, : 3 * OSEC]


def face_of(flux):
    return (flux >= 3).astype(I32) + (flux >= 6).astype(I32) + (flux >= 9).astype(I32)


def kernel_predict(sizes, *refs):
    xs = sizes.sub_count // 2 - 1
    (state_hbm, class_hbm, table_hbm, deriv_hbm, restrict_hbm, send_hbm, *later_hbm) = refs[:14]
    refs = refs[14:]
    class_ref, refs = refs[0], refs[1:]
    later_refs, refs = refs[:8], refs[8:]
    (state_ref, first_ref, late_ref, proj_ref, faces_ref, star_ref, dleft_ref, rleft_ref, pick_ref, pick_sub_ref,
     pa_ref, pb_ref, p1_ref, *rest) = refs
    pk_refs, rest = rest[:xs], rest[xs:]
    (table_ref, deriv_ref, restrict_ref, send_ref, moved_ref, other_ref, stage_ref, rstage_ref, slot_ref,
     sems) = rest
    sources = [class_hbm, table_hbm, deriv_hbm, state_hbm, send_hbm, restrict_hbm, *later_hbm]
    targets = [class_ref, table_ref, deriv_ref, state_ref, send_ref, restrict_ref, *later_refs]
    copies = [pltpu.make_async_copy(s, t, sems.at[i]) for i, (s, t) in enumerate(zip(sources, targets))]
    for copy in copies:
        copy.start()
    variables, basis = sizes.variables, sizes.basis
    copies[0].wait()
    copies[1].wait()
    lookup(table_ref, stage_ref, class_ref[...], star_ref)
    copies[2].wait()
    dleft_ref[...] = stack_left(jnp.reshape(deriv_ref[...], (3 * basis, basis)))
    left = dleft_ref[...]
    copies[3].wait()
    for g in groups(sizes):
        values = [state_ref[g * GROUP + i] for i in range(GROUP)]
        moved_ref[:, group_lanes(g)] = dot(left, stack_right(values))[: moved_ref.shape[0]]
        for i in range(GROUP):
            first_ref[g * GROUP + i] = values[i] * HALF
            late_ref[g * GROUP + i] = values[i] * (1.0 - HALF)
    for copy in copies[4:6]:
        copy.wait()
    def send_picks():
        picks_of_sends(send_ref, pick_ref, pick_sub_ref)

    def restrict_left():
        rstage_ref[...] = jnp.zeros_like(rstage_ref)
        for f in range(4):
            rstage_ref[f * PAD : f * PAD + restrict_ref.shape[0], :basis] = restrict_ref[:, f, :]
        rleft_ref[...] = stack_left(rstage_ref[:, :basis])

    send_picks()
    restrict_left()

    def finish(p, first):
        first_ref[p] = first
        return first

    for g, values in predictor(moved_ref, other_ref, star_ref, left, first_ref, late_ref, sizes, finish,
                               []):
        project(g, values, rleft_ref[...], proj_ref)
    by_face(proj_ref, faces_ref, sizes)
    payloads(faces_ref, pick_ref, pick_sub_ref, slot_ref, (pa_ref, pb_ref, p1_ref, pk_refs), sizes)
    for copy in copies[6:]:
        copy.wait()


def volume_part(values_ref, base_ref, star_ref, kleft, moved_ref, partial_ref, sizes):
    for g in groups(sizes):
        values = [values_ref[g * GROUP + i] for i in range(GROUP)]
        moved_ref[:, group_lanes(g)] = dot(kleft, stack_right(values))[: moved_ref.shape[0]]
    for g in groups(sizes):
        acc = mix_group(moved_ref, star_ref, sizes, g)
        for i in range(GROUP):
            partial_ref[g * GROUP + i] = base_ref[g * GROUP + i] + acc[i]


def interior_part(faces_ref, pick_ref, oleft, turn, gath_ref, sizes):
    rows = sizes.rows
    both = dot(faces_ref[...], pick_ref[...])
    both = both[0:rows] + both[rows : 2 * rows]
    blocks = [both[q * PAD : (q + 1) * PAD] for q in range(sizes.variables)]
    for q, block in enumerate(turn_blocks(blocks, oleft, turn)):
        gath_ref[q * PAD : (q + 1) * PAD, :] = block


def own_part(proj_ref, minus_ref, comb_ref, sizes):
    variables = sizes.variables
    for f in range(4):
        rows = slice(f * PAD, (f + 1) * PAD)
        acc = [None] * variables
        for q in range(variables):
            block = proj_ref[rows, q * 128 : (q + 1) * 128]
            for p in range(variables):
                row = (q * variables + p) * 4 + f
                term = block * minus_ref[row : row + 1, :]
                acc[p] = term if acc[p] is None else acc[p] + term
        for p in range(variables):
            comb_ref[rows, p * 128 : (p + 1) * 128] = acc[p]


def near_part(proj_ref, minus_ref, gath_ref, plus_ref, comb_ref, sizes):
    variables = sizes.variables
    for f in range(4):
        rows = slice(f * PAD, (f + 1) * PAD)
        acc = [None] * variables
        for q in range(variables):
            own = proj_ref[rows, q * 128 : (q + 1) * 128]
            other = gath_ref[q * PAD : (q + 1) * PAD, f * 128 : (f + 1) * 128]
            for p in range(variables):
                row = (q * variables + p) * 4 + f
                term = own * minus_ref[row : row + 1, :]
                acc[p] = term if acc[p] is None else acc[p] + term
                acc[p] = acc[p] + other * plus_ref[row : row + 1, :]
        for p in range(variables):
            comb_ref[rows, p * 128 : (p + 1) * 128] = acc[p]


def plus_by_slot(plus_ref, ghost_pick_ref, out_ref, sizes):
    mats = sizes.variables**2
    pieces = [pad_to(plus_ref[pl.ds(f, mats, stride=4), :], out_ref.shape[0], 128) for f in range(4)]
    high, low = split(jnp.concatenate(pieces, axis=1))
    pick = ghost_pick_ref[...]
    out_ref[...] = dot_nt(high, pick) + dot_nt(low, pick)


def kernel_local_first(sizes, *refs):
    (class_ref, minus_table, plus_table, code_ref, flux_ref, stiff_ref, lift_ref, orient_ref,
     first_ref, state_ref, star_ref, proj_ref, faces_ref,
     partial_ref, gath_ref, comb_ref, minus_ref, plus_ref, kleft_ref, oleft_ref, lleft_ref, llow_ref,
     pick_ref, ghost_pick_ref, turn_ref, ghost_turn_ref, moved_ref, stage_ref, lstage_ref) = refs
    basis = sizes.basis
    kleft_ref[...] = stack_left(jnp.reshape(stiff_ref[...], (3 * basis, basis)))
    volume_part(first_ref, state_ref, star_ref, kleft_ref[...], moved_ref, partial_ref, sizes)
    lookup(minus_table, stage_ref, class_ref[...], minus_ref)
    oleft_ref[...] = orient_left(orient_ref)
    code = code_ref[...]
    flux = flux_ref[...]
    face = face_of(flux)
    turn = flux - 3 * face
    turn_row = jnp.concatenate([turn[f : f + 1, :] for f in range(4)], axis=1)
    turn_ref[...] = turn_row
    place = lax.broadcasted_iota(I32, (128, 128), 0)
    target = jnp.where(code < 128, face * 128 + code, -1)
    for f in range(4):
        for j in range(4):
            pick_ref[j * 128 : (j + 1) * 128, f * 128 : (f + 1) * 128] = (
                (place + j * 128 == target[f : f + 1, :]).astype(F32).astype(BF16)
            )
    slot = code - 128
    swapped = jnp.where(slot < CAP_DOM, slot + CAP_DOM, slot - CAP_DOM)
    dom_slot = jnp.where(is_even(), swapped, slot)
    dom_slot = jnp.where(dom_slot < CAP_DOM, dom_slot, dom_slot + CAP_DOM)
    slot = jnp.where(slot < 2 * CAP_DOM, dom_slot, slot + CAP_DOM)
    slot = jnp.where(jnp.logical_or(code < 128, code >= 128 + sizes.ghosts), -1, slot)
    for f in range(4):
        for j in range(2):
            ghost_pick_ref[j * 128 : (j + 1) * 128, f * 128 : (f + 1) * 128] = (
                (place + j * 128 == slot[f : f + 1, :]).astype(F32).astype(BF16)
            )
    rows = jnp.broadcast_to(turn_row.astype(F32), (16, 512)).astype(BF16)
    ghost_turn_ref[...] = dot_nt(rows, ghost_pick_ref[...])[0:1].astype(I32)
    interior_part(faces_ref, pick_ref, oleft_ref[...], turn_row, gath_ref, sizes)
    lookup(plus_table, stage_ref, class_ref[...], plus_ref)
    own_part(proj_ref, minus_ref, comb_ref, sizes)
    lstage_ref[...] = jnp.zeros_like(lstage_ref)
    for f in range(4):
        lstage_ref[f * PAD : f * PAD + lift_ref.shape[0], :basis] = lift_ref[:, f, :]
    wide = jnp.transpose(lstage_ref[...], (1, 0))[:64]
    high = wide.astype(BF16).astype(F32)
    low = wide - high
    rolled = pltpu.roll(high, 4 * PAD, 1)
    lane = lax.broadcasted_iota(I32, (64, 128), 1)
    lleft_ref[:, 0:128] = jnp.where(lane < 4 * PAD, high, rolled).astype(BF16)
    lleft_ref[:, 128:256] = jnp.where(lane < 8 * PAD - 128, rolled, 0.0).astype(BF16)
    llow_ref[...] = low.astype(BF16)


def kernel_local_second(sizes, *refs):
    (second_ref, middle_ref, star_ref, kleft_ref, proj_ref, faces_ref, minus_ref, plus_ref, oleft_ref, pick_ref,
     turn_ref, ghost_pick_ref, partial_ref, comb_ref, slot_plus_ref, moved_ref, gath_ref) = refs
    volume_part(second_ref, middle_ref, star_ref, kleft_ref[...], moved_ref, partial_ref, sizes)
    interior_part(faces_ref, pick_ref, oleft_ref[...], turn_ref[...], gath_ref, sizes)
    near_part(proj_ref, minus_ref, gath_ref, plus_ref, comb_ref, sizes)
    plus_by_slot(plus_ref, ghost_pick_ref, slot_plus_ref, sizes)


def ghost_side(received, tile, oleft_ref, ghost_turn_ref, ghost_pick_ref, slot_plus_ref, ghost_ref, comb_ref, sizes):
    variables, rows = sizes.variables, sizes.rows
    lanes = slice(tile * 128, (tile + 1) * 128)
    blocks = [received[q * PAD : (q + 1) * PAD] for q in range(variables)]
    turned = turn_blocks(blocks, oleft_ref[...], ghost_turn_ref[:, lanes])
    acc = [None] * variables
    for q in range(variables):
        for p in range(variables):
            row = q * variables + p
            term = turned[q] * slot_plus_ref[row : row + 1, lanes]
            acc[p] = term if acc[p] is None else acc[p] + term
    high, low = split(pad_to(jnp.concatenate(acc, axis=0), rows, 128))
    ghost_ref[0:rows, :] = high
    ghost_ref[rows : 2 * rows, :] = low
    both = dot(ghost_ref[...], ghost_pick_ref[lanes, :])
    out = []
    for p in range(variables):
        pieces = []
        for f in range(4):
            cols = slice(f * 128, (f + 1) * 128)
            spread = both[p * PAD : (p + 1) * PAD, cols] + both[rows + p * PAD : rows + (p + 1) * PAD, cols]
            pieces.append(comb_ref[f * PAD : (f + 1) * PAD, p * 128 : (p + 1) * 128] + spread)
        out.append(jnp.concatenate(pieces, axis=0))
    return out


def kernel_even(sizes, *refs):
    (ra_ref, oleft_ref, ghost_turn_ref, ghost_pick_ref, slot_plus_ref, comb_ref, out_ref, ghost_ref) = refs
    values = ghost_side(by_rows(ra_ref[...]), 0, oleft_ref, ghost_turn_ref, ghost_pick_ref, slot_plus_ref,
                        ghost_ref, comb_ref, sizes)
    for p in range(sizes.variables):
        out_ref[:, p * 128 : (p + 1) * 128] = values[p]


def neighbour_part(ins, oleft_ref, ghost_turn_ref, ghost_pick_ref, slot_plus_ref, comb_ref, lleft_ref, llow_ref,
                   partial_ref, slot_ref, ghost_ref, sizes):
    basis = sizes.basis
    rb_ref, r1_ref, rk_refs = ins
    received = with_subs(by_rows(rb_ref[...]), r1_ref, rk_refs, slot_ref, sizes)
    faces = ghost_side(received, 1, oleft_ref, ghost_turn_ref, ghost_pick_ref, slot_plus_ref, ghost_ref, comb_ref, sizes)
    highs, stacks = [], []
    for value in faces:
        high, low = split(value)
        highs.append(high)
        stacks.append(jnp.concatenate([high, low], axis=0))
    lifted = dot(lleft_ref[:, : 8 * PAD], jnp.concatenate(stacks, axis=1)) + dot(
        llow_ref[:, : 4 * PAD], jnp.concatenate(highs, axis=1)
    )
    for g in groups(sizes):
        yield g, [
            partial_ref[p] + lifted[:basis, p * 128 : (p + 1) * 128] for p in range(g * GROUP, (g + 1) * GROUP)
        ]


def neighbour_all(ins, oleft_ref, ghost_turn_ref, ghost_pick_ref, gath_ref, comb_ref, plus_ref, lleft_ref, llow_ref,
                   partial_ref, slot_ref, ghost_ref, gsum_ref, sizes):
    variables, basis, rows = sizes.variables, sizes.basis, sizes.rows
    ra_ref, rb_ref, r1_ref, rk_refs = ins
    received = [by_rows(ra_ref[...]), with_subs(by_rows(rb_ref[...]), r1_ref, rk_refs, slot_ref, sizes)]
    received = jnp.concatenate(received, axis=1)
    blocks = [received[q * PAD : (q + 1) * PAD] for q in range(variables)]
    turned = turn_blocks(blocks, oleft_ref[...], ghost_turn_ref[...])
    high, low = split(pad_to(jnp.concatenate(turned, axis=0), rows, turned[0].shape[1]))
    ghost_ref[0:rows, :] = high
    ghost_ref[rows : 2 * rows, :] = low
    both = dot(ghost_ref[...], ghost_pick_ref[...])
    used = variables * PAD
    gsum_ref[...] = gath_ref[...] + (both[0:used] + both[rows : rows + used])
    highs, stacks = [], []
    for g in groups(sizes):
        faces = [[], [], []]
        for f in range(4):
            frows = slice(f * PAD, (f + 1) * PAD)
            acc = []
            for i in range(GROUP):
                p = g * GROUP + i
                acc.append(comb_ref[frows, p * 128 : (p + 1) * 128])
            for q in range(variables):
                block = gsum_ref[q * PAD : (q + 1) * PAD, f * 128 : (f + 1) * 128]
                for i in range(GROUP):
                    row = (q * variables + g * GROUP + i) * 4 + f
                    acc[i] = acc[i] + block * plus_ref[row : row + 1, :]
            for i in range(GROUP):
                faces[i].append(acc[i])
        for i in range(GROUP):
            high, low = split(jnp.concatenate(faces[i], axis=0))
            highs.append(high)
            stacks.append(jnp.concatenate([high, low], axis=0))
    lifted = dot(lleft_ref[:, : 8 * PAD], jnp.concatenate(stacks, axis=1)) + dot(
        llow_ref[:, : 4 * PAD], jnp.concatenate(highs, axis=1)
    )
    for g in groups(sizes):
        yield g, [
            partial_ref[p] + lifted[:basis, p * 128 : (p + 1) * 128] for p in range(g * GROUP, (g + 1) * GROUP)
        ]


def kernel_second(sizes, *refs):
    xs = sizes.sub_count // 2 - 1
    ra_ref, rb_ref, r1_ref, *refs = refs
    rk_refs, refs = refs[:xs], refs[xs:]
    (oleft_ref, ghost_turn_ref, ghost_pick_ref, gath_ref, comb_ref, plus_ref, lleft_ref, llow_ref, partial_ref,
     star_ref, late_ref, cluster_ref, dleft_ref, rleft_ref, pick_ref, pick_sub_ref,
     middle_ref, second_ref, proj_ref, faces_ref, pa_ref, pb_ref, p1_ref, *rest) = refs
    pk_refs, rest = rest[:xs], rest[xs:]
    moved_ref, other_ref, slot_ref, pslot_ref, ghost_ref, gsum_ref = rest
    left = dleft_ref[...]
    for g, values in neighbour_all((ra_ref, rb_ref, r1_ref, rk_refs), oleft_ref, ghost_turn_ref, ghost_pick_ref,
                                    gath_ref, comb_ref, plus_ref, lleft_ref, llow_ref, partial_ref, slot_ref,
                                    ghost_ref, gsum_ref, sizes):
        moved_ref[:, group_lanes(g)] = dot(left, stack_right(values))[: moved_ref.shape[0]]
        for i in range(GROUP):
            middle_ref[g * GROUP + i] = values[i]
            second_ref[g * GROUP + i] = values[i] * HALF
    fine = cluster_ref[...] == 1

    def finish(p, first):
        value = jnp.where(fine, first, late_ref[p])
        second_ref[p] = value
        return value

    for g, values in predictor(moved_ref, other_ref, star_ref, left, second_ref, None, sizes, finish):
        project(g, values, rleft_ref[...], proj_ref)
    by_face(proj_ref, faces_ref, sizes)
    payloads(faces_ref, pick_ref, pick_sub_ref, pslot_ref, (pa_ref, pb_ref, p1_ref, pk_refs), sizes)


def kernel_last(sizes, *refs):
    xs = sizes.sub_count // 2 - 1
    rb_ref, r1_ref, *refs = refs
    rk_refs, refs = refs[:xs], refs[xs:]
    (oleft_ref, ghost_turn_ref, ghost_pick_ref, slot_plus_ref, comb_ref, lleft_ref, llow_ref, partial_ref,
     out_hbm, slot_ref, ghost_ref, out_ref, sems) = refs
    copies = []
    for g, values in neighbour_part((rb_ref, r1_ref, rk_refs), oleft_ref, ghost_turn_ref, ghost_pick_ref,
                                    slot_plus_ref, comb_ref, lleft_ref, llow_ref, partial_ref, slot_ref,
                                    ghost_ref, sizes):
        for i in range(GROUP):
            out_ref[g * GROUP + i] = values[i]
        part = pl.ds(g * GROUP, GROUP)
        copies.append(pltpu.make_async_copy(out_ref.at[part], out_hbm.at[part], sems.at[g]))
        copies[-1].start()
    for copy in copies:
        copy.wait()


def body(
    dom_count,
    sub_count,
    modal_state,
    cluster_id,
    jacobian_id,
    face_neighbour,
    flux_index,
    send_list,
    derivative,
    stiffness,
    restriction,
    lifting,
    orientation,
    star_matrix,
    flux_minus,
    flux_plus,
):
    basis, variables, elements = modal_state.shape
    ghosts = send_list.shape[0]
    cap_sub = (ghosts - 2 * CAP_DOM) // sub_count
    lanes = variables * elements
    half_rows = -(-variables * PAD // 32) * 16
    rows = 2 * half_rows
    sizes = Sizes(variables, basis, sub_count, cap_sub, rows, half_rows, ghosts)
    sub_lanes = -(-rows // 128) * 128
    mat_rows = variables * variables * 4 + 4
    xs = sub_count // 2 - 1

    state = jnp.transpose(modal_state, (1, 0, 2))
    star_table = jnp.transpose(star_matrix, (2, 3, 1, 0))
    minus_table = jnp.transpose(flux_minus, (2, 3, 1, 0))
    plus_table = jnp.transpose(flux_plus, (2, 3, 1, 0))
    restrict = jnp.transpose(restriction, (1, 0, 2))
    lift = jnp.transpose(lifting, (2, 0, 1))
    classes = jacobian_id.reshape(1, elements)
    clusters = cluster_id.reshape(1, elements)
    sends = send_list.reshape(1, ghosts)

    def sds(*shape, dtype=F32):
        return jax.ShapeDtypeStruct(shape, dtype)

    def like(x):
        return sds(*x.shape, dtype=x.dtype)

    whole = sds(variables, basis, elements)
    face_t = sds(4 * PAD, lanes)
    faces_t = sds(2 * rows, 4 * elements, dtype=BF16)
    mat_t = sds(mat_rows, 128)
    gath_t = sds(variables * PAD, 4 * elements)
    left_t = sds(-(-3 * basis // 16) * 16, 3 * SEC, dtype=BF16)
    pay_t = [sds(half_rows, 128)] * 2 + [sds(cap_sub * (xs + 1), sub_lanes)] + [sds(cap_sub, sub_lanes)] * xs

    def scratch(t):
        return pltpu.VMEM(t.shape, t.dtype)

    moved_s = pltpu.VMEM((3 * basis, lanes), F32)
    stage_s = pltpu.VMEM((mat_rows, 128), F32)
    slot_s = pltpu.VMEM((128, sub_lanes), F32)
    pslot_s = pltpu.VMEM((ghosts - 2 * CAP_DOM, sub_lanes), F32)
    ghost_s = pltpu.VMEM((2 * rows, 128), BF16)
    ghost_all_s = pltpu.VMEM((2 * rows, 256), BF16)
    slot_mat_t = sds(-(-variables * variables // 16) * 16, 256)

    def call(fn, outs, scratches, operands, flops, space=pltpu.VMEM, out_space=pltpu.VMEM):
        vmem = pl.BlockSpec(memory_space=out_space)
        if space is pltpu.HBM:
            operands = [pltpu.with_memory_space_constraint(x, pltpu.HBM) for x in operands]
        return pl.pallas_call(
            functools.partial(fn, sizes),
            out_shape=outs,
            in_specs=[pl.BlockSpec(memory_space=space)] * len(operands),
            out_specs=jax.tree.map(lambda _: vmem, outs),
            scratch_shapes=scratches,
            cost_estimate=pl.CostEstimate(flops=flops, bytes_accessed=2_000_000, transcendentals=0),
            compiler_params=pltpu.CompilerParams(vmem_limit_bytes=24 * 1024 * 1024),
        )(*operands)

    combined = ("dom", "sub")

    def device(d, s):
        return d * sub_count + s

    def pairs(target):
        return [(device(d, s), device(*target(d, s))) for d in range(dom_count) for s in range(sub_count)]

    even_pairs = pairs(lambda d, s: (d ^ 1, s))
    odd_pairs = pairs(lambda d, s: (((d + 1) ^ 1) - 1, s) if 0 < d < dom_count - 1 else (d, s ^ 1))

    def sub_pairs(k):
        return pairs(lambda d, s: (d, s ^ k))

    def trade(payload):
        pa, pb, p1, *pk = payload
        r1 = lax.ppermute(p1, combined, sub_pairs(1))
        rb = lax.ppermute(pb, combined, odd_pairs)
        ra = lax.ppermute(pa, combined, even_pairs)
        rk = []
        for i, part in enumerate(pk):
            passed = r1[(i + 1) * cap_sub : (i + 2) * cap_sub]
            rk.append(lax.ppermute(jnp.concatenate([part, passed], axis=0), combined, sub_pairs(2 * i + 2)))
        return [ra, rb, r1, *rk]

    later = [clusters, minus_table, plus_table, face_neighbour, flux_index, stiffness, lift, orientation]
    outs = call(
        kernel_predict,
        [like(x) for x in [classes, *later]]
        + [whole, whole, whole, face_t, faces_t, mat_t, left_t, sds(4 * PAD, 3 * SEC, dtype=BF16)]
        + [sds(4 * elements, 128, dtype=BF16), sds(ghosts - 2 * CAP_DOM, 4 * elements, dtype=BF16)]
        + pay_t,
        [
            scratch(star_table), scratch(derivative), scratch(restrict), scratch(sends),
            moved_s, moved_s, stage_s, pltpu.VMEM((4 * PAD, 128), F32), pslot_s, pltpu.SemaphoreType.DMA((14,)),
        ],
        [state, classes, star_table, derivative, restrict, sends, *later],
        60_000_000,
        pltpu.HBM,
    )
    clusters, minus_table, plus_table, code, flux, stiff, lift, orient = outs[1:9]
    classes = outs[0]
    state, first, late, proj, faces, star, dleft, rleft, pick_send, pick_sub, *payload = outs[9:]
    received = trade(payload)
    partial, gath, comb, minus, plus, kleft, oleft, lleft, llow, pick, ghost_pick, turn, ghost_turn = call(
        kernel_local_first,
        [whole, gath_t, face_t, mat_t, mat_t, left_t, sds(80, 3 * OSEC, dtype=BF16)]
        + [sds(64, 256, dtype=BF16), sds(64, 128, dtype=BF16)]
        + [sds(4 * elements, 4 * elements, dtype=BF16), sds(256, 4 * elements, dtype=BF16)]
        + [sds(1, 4 * elements, dtype=I32), sds(1, 256, dtype=I32)],
        [moved_s, stage_s, pltpu.VMEM((128, 128), F32)],
        [classes, minus_table, plus_table, code, flux, stiff, lift, orient, first, state, star, proj, faces],
        30_000_000,
    )
    common = [oleft, ghost_turn, ghost_pick]
    middle, second, proj, faces, *payload = call(
        kernel_second,
        [whole, whole, face_t, faces_t] + pay_t,
        [moved_s, moved_s, slot_s, pslot_s, ghost_all_s, scratch(gath_t)],
        received
        + common
        + [gath, comb, plus, lleft, llow, partial, star, late, clusters, dleft, rleft, pick_send, pick_sub],
        70_000_000,
    )
    received = trade(payload)
    partial, comb, slot_plus = call(
        kernel_local_second,
        [whole, face_t, slot_mat_t],
        [moved_s, scratch(gath_t)],
        [second, middle, star, kleft, proj, faces, minus, plus, oleft, pick, turn, ghost_pick],
        30_000_000,
    )
    common = [*common, slot_plus]
    comb = call(kernel_even, face_t, [ghost_s], [received[0], *common, comb], 3_000_000)
    result = call(
        kernel_last,
        whole,
        [slot_s, ghost_s, scratch(whole), pltpu.SemaphoreType.DMA((variables // GROUP,))],
        received[1:] + common + [comb, lleft, llow, partial],
        10_000_000,
        out_space=pltpu.HBM,
    )
    return jnp.transpose(result, (1, 0, 2))


def solution(mesh):
    placed = (
        P(None, None, ("dom", "sub")),
        P(("dom", "sub")),
        P(("dom", "sub")),
        P(None, ("dom", "sub")),
        P(None, ("dom", "sub")),
        P(("dom", "sub")),
        P(),
        P(),
        P(),
        P(),
        P(),
        P(),
        P(),
        P(),
    )
    return jax.shard_map(
        functools.partial(body, mesh.shape["dom"], mesh.shape["sub"]),
        mesh=mesh,
        in_specs=placed,
        out_specs=P(None, None, ("dom", "sub")),
        check_vma=False,
    )
```

```python
import collections
import functools

import jax
import jax.numpy as jnp
from jax import lax
from jax.experimental import pallas as pl
from jax.experimental.pallas import tpu as pltpu
from jax.sharding import PartitionSpec as P

ORDER = 6
CAP_DOM = 64
HALF = 0.5
PAD = 24
SEC = 64
OSEC = 32
GROUP = 3

F32 = jnp.float32
BF16 = jnp.bfloat16
I32 = jnp.int32

Sizes = collections.namedtuple(
    "Sizes", ["variables", "basis", "sub_count", "cap_sub", "rows", "half_rows", "ghosts"]
)


def split(x):
    high = x.astype(BF16)
    low = (x - high.astype(F32)).astype(BF16)
    return high, low


def dot(a, b):
    return lax.dot_general(a, b, (((1,), (0,)), ((), ())), preferred_element_type=F32)


def dot_nt(a, b):
    return lax.dot_general(a, b, (((1,), (1,)), ((), ())), preferred_element_type=F32)


def pad_to(x, rows, lanes):
    m, k = x.shape
    if lanes > k:
        x = jnp.concatenate([x, jnp.zeros((m, lanes - k), x.dtype)], axis=1)
    if rows > m:
        x = jnp.concatenate([x, jnp.zeros((rows - m, lanes), x.dtype)], axis=0)
    return x


def stack_left(matrix):
    m = -(-matrix.shape[0] // 16) * 16
    wide = pad_to(matrix, m, 128)
    high = wide.astype(BF16).astype(F32)
    low = wide - high
    both = high + pltpu.roll(high, SEC, 1)
    return jnp.concatenate([both.astype(BF16), low.astype(BF16)], axis=1)[:, : 3 * SEC]


def stack_right(blocks):
    out = []
    for x in blocks:
        high, low = split(pad_to(x, SEC, x.shape[1]))
        out.append(jnp.concatenate([high, low, high], axis=0))
    return jnp.concatenate(out, axis=1) if len(out) > 1 else out[0]


def order_after(x):
    return split(x)[1].astype(F32) * 0.0


def mix_group(moved_ref, star_ref, sizes, g, zero=None):
    basis, variables = sizes.basis, sizes.variables
    acc = [zero] * GROUP
    for q in range(variables):
        for d in range(3):
            block = moved_ref[d * basis : (d + 1) * basis, q * 128 : (q + 1) * 128]
            for i in range(GROUP):
                row = (q * variables + g * GROUP + i) * 4 + d
                term = block * star_ref[row : row + 1, :]
                acc[i] = term if acc[i] is None else acc[i] + term
    return acc


def lookup(table_ref, stage_ref, class_row, out_ref):
    nq, np_, parts, classes = table_ref.shape
    for q in range(nq):
        for p in range(np_):
            row = (q * np_ + p) * 4
            stage_ref[row : row + parts, :classes] = table_ref[q, p]
    rows = stage_ref.shape[0]
    high, low = split(stage_ref[:, :classes])
    onehot = (lax.broadcasted_iota(I32, (classes, 128), 0) == class_row).astype(F32).astype(BF16)
    out_ref[0:rows, :] = dot(high, onehot) + dot(low, onehot)


def groups(sizes):
    return range(sizes.variables // GROUP)


def group_lanes(g):
    return slice(g * GROUP * 128, (g + 1) * GROUP * 128)


def advance(src_ref, dst_ref, star_ref, left, sizes, emit, between):
    zero = None
    for g in groups(sizes):
        acc = mix_group(src_ref, star_ref, sizes, g, zero)
        zero = order_after(acc[-1])
        for i in range(GROUP):
            emit(g * GROUP + i, acc[i])
        dst_ref[:, group_lanes(g)] = dot(left, stack_right(acc))[: dst_ref.shape[0]]
        between()


def predictor(moved_ref, other_ref, star_ref, left, first_ref, late_ref, sizes, finish, extra=()):
    extra = list(extra)

    def between():
        if extra:
            extra.pop(0)()

    def weigh(weights, degree):
        w_half, w_full = weights
        scale = -1.0 / (degree + 1)
        return w_half * (scale * HALF), w_full * scale

    def emitter(weights):
        w_half, w_full = weights

        def emit(p, value):
            first_ref[p] += w_half * value
            if late_ref is not None:
                late_ref[p] += (w_full - w_half) * value

        return emit

    def two(i, weights):
        weights = weigh(weights, 2 * i + 1)
        advance(moved_ref, other_ref, star_ref, left, sizes, emitter(weights), between)
        weights = weigh(weights, 2 * i + 2)
        advance(other_ref, moved_ref, star_ref, left, sizes, emitter(weights), between)
        return weights

    steps = ORDER - 1
    weights = (HALF, 1.0)
    for i in range(steps // 2):
        weights = two(i, weights)
    w_half, w_full = weigh(weights, steps)
    for g in groups(sizes):
        acc = mix_group(moved_ref, star_ref, sizes, g)
        values = []
        for i in range(GROUP):
            p = g * GROUP + i
            first = first_ref[p] + w_half * acc[i]
            if late_ref is not None:
                late_ref[p] += (w_full - w_half) * acc[i]
            values.append(finish(p, first))
        yield g, values


def project(g, values, left, proj_ref):
    proj_ref[:, group_lanes(g)] = dot(left, stack_right(values))


def by_face(proj_ref, faces_ref, sizes):
    rows = sizes.rows
    for f in range(4):
        pieces = [
            proj_ref[f * PAD : (f + 1) * PAD, q * 128 : (q + 1) * 128] for q in range(sizes.variables)
        ]
        high, low = split(pad_to(jnp.concatenate(pieces, axis=0), rows, 128))
        faces_ref[0:rows, f * 128 : (f + 1) * 128] = high
        faces_ref[rows : 2 * rows, f * 128 : (f + 1) * 128] = low


def is_even():
    return lax.rem(lax.axis_index("dom"), 2) == 0


def low_lanes(shape):
    return lax.broadcasted_iota(I32, shape, 1) < CAP_DOM


def picks_of_sends(send_ref, pick_ref, pick_sub_ref):
    ghosts = send_ref.shape[1]
    row = send_ref[...].astype(F32)
    dom_row = row[:, 0:128]
    dom_row = jnp.where(is_even(), pltpu.roll(dom_row, CAP_DOM, 1), dom_row)
    place = lax.broadcasted_iota(I32, (128, 128), 0).astype(F32)
    for f in range(4):
        pick_ref[f * 128 : (f + 1) * 128, :] = (place + f * 128 == dom_row).astype(F32).astype(BF16)
    subs = ghosts - 128
    sub_row = pad_to(row[:, 128:], 1, 128)
    column = jnp.transpose(jnp.broadcast_to(sub_row, (128, 128)), (1, 0))[:subs]
    lane = lax.broadcasted_iota(I32, (subs, 128), 1).astype(F32)
    for f in range(4):
        pick_sub_ref[:, f * 128 : (f + 1) * 128] = (column == lane + f * 128).astype(F32).astype(BF16)


def payloads(faces_ref, pick_ref, pick_sub_ref, slot_ref, outs, sizes):
    pa_ref, pb_ref, p1_ref, pk_refs = outs
    rows, half = sizes.rows, sizes.half_rows
    sub = dot_nt(pick_sub_ref[...], faces_ref[0:rows, :]) + dot_nt(pick_sub_ref[...], faces_ref[rows : 2 * rows, :])
    slot_ref[...] = pad_to(sub, sub.shape[0], slot_ref.shape[1])
    both = dot(faces_ref[...], pick_ref[...])
    both = both[0:rows] + both[rows : 2 * rows]
    top, bottom = both[0:half], both[half:]
    low = low_lanes((half, 128))
    pa_ref[...] = jnp.where(low, top, pltpu.roll(bottom, CAP_DOM, 1))
    pb_ref[...] = jnp.where(low, pltpu.roll(top, CAP_DOM, 1), bottom)
    me = lax.axis_index("sub")
    cap = sizes.cap_sub

    def block(k):
        return slot_ref[pl.ds(pl.multiple_of(jnp.bitwise_xor(me, k) * cap, 8), cap), :]

    p1_ref[0:cap, :] = block(1)
    for i, k in enumerate(range(2, sizes.sub_count, 2)):
        p1_ref[(i + 1) * cap : (i + 2) * cap, :] = block(k + 1)
        pk_refs[i][...] = block(k)


def by_rows(received):
    return jnp.concatenate([received, pltpu.roll(received, CAP_DOM, 1)], axis=0)


def with_subs(dom, r1_ref, rk_refs, slot_ref, sizes):
    me = lax.axis_index("sub")
    cap = sizes.cap_sub
    slot_ref[...] = jnp.zeros_like(slot_ref)

    def put(k, value):
        start = pl.multiple_of(CAP_DOM + jnp.bitwise_xor(me, k) * cap, 8)
        slot_ref[pl.ds(start, cap), :] = value

    put(1, r1_ref[0:cap, :])
    for i, k in enumerate(range(2, sizes.sub_count, 2)):
        put(k, rk_refs[i][0:cap, :])
        put(k + 1, rk_refs[i][cap : 2 * cap, :])
    sub = jnp.transpose(slot_ref[...], (1, 0))[: dom.shape[0]]
    return jnp.where(low_lanes(dom.shape), dom, sub)


def turn_blocks(values, left, turns):
    stacks = []
    for value in values:
        high, low = split(pad_to(value, OSEC, value.shape[1]))
        stacks.append(jnp.concatenate([high, low, high], axis=0))
    width = values[0].shape[1]
    whole = dot(left, jnp.concatenate(stacks, axis=1))
    out = []
    for q in range(len(values)):
        turned = whole[:, q * width : (q + 1) * width]
        out.append(
            jnp.where(
                turns == 0,
                turned[0:PAD],
                jnp.where(turns == 1, turned[PAD : 2 * PAD], turned[2 * PAD : 3 * PAD]),
            )
        )
    return out


def orient_left(orient_ref):
    blocks = [pad_to(orient_ref[h], PAD, 128) for h in range(3)]
    wide = pad_to(jnp.concatenate(blocks, axis=0), 80, 128)
    high = wide.astype(BF16).astype(F32)
    low = wide - high
    stacked = high + pltpu.roll(high, OSEC, 1) + pltpu.roll(low, 2 * OSEC, 1)
    return stacked.astype(BF16)[:, : 3 * OSEC]


def face_of(flux):
    return (flux >= 3).astype(I32) + (flux >= 6).astype(I32) + (flux >= 9).astype(I32)


def kernel_predict(sizes, *refs):
    xs = sizes.sub_count // 2 - 1
    (state_hbm, class_hbm, table_hbm, deriv_hbm, restrict_hbm, send_hbm, *later_hbm) = refs[:14]
    refs = refs[14:]
    class_ref, refs = refs[0], refs[1:]
    later_refs, refs = refs[:8], refs[8:]
    (state_ref, first_ref, late_ref, proj_ref, faces_ref, star_ref, dleft_ref, rleft_ref, pick_ref, pick_sub_ref,
     pa_ref, pb_ref, p1_ref, *rest) = refs
    pk_refs, rest = rest[:xs], rest[xs:]
    (table_ref, deriv_ref, restrict_ref, send_ref, moved_ref, other_ref, stage_ref, rstage_ref, slot_ref,
     sems) = rest
    sources = [class_hbm, table_hbm, deriv_hbm, state_hbm, send_hbm, restrict_hbm, *later_hbm]
    targets = [class_ref, table_ref, deriv_ref, state_ref, send_ref, restrict_ref, *later_refs]
    copies = [pltpu.make_async_copy(s, t, sems.at[i]) for i, (s, t) in enumerate(zip(sources, targets))]
    for copy in copies:
        copy.start()
    variables, basis = sizes.variables, sizes.basis
    copies[0].wait()
    copies[1].wait()
    lookup(table_ref, stage_ref, class_ref[...], star_ref)
    copies[2].wait()
    dleft_ref[...] = stack_left(jnp.reshape(deriv_ref[...], (3 * basis, basis)))
    left = dleft_ref[...]
    copies[3].wait()
    for g in groups(sizes):
        values = [state_ref[g * GROUP + i] for i in range(GROUP)]
        moved_ref[:, group_lanes(g)] = dot(left, stack_right(values))[: moved_ref.shape[0]]
        for i in range(GROUP):
            first_ref[g * GROUP + i] = values[i] * HALF
            late_ref[g * GROUP + i] = values[i] * (1.0 - HALF)
    for copy in copies[4:6]:
        copy.wait()
    def send_picks():
        picks_of_sends(send_ref, pick_ref, pick_sub_ref)

    def restrict_left():
        rstage_ref[...] = jnp.zeros_like(rstage_ref)
        for f in range(4):
            rstage_ref[f * PAD : f * PAD + restrict_ref.shape[0], :basis] = restrict_ref[:, f, :]
        rleft_ref[...] = stack_left(rstage_ref[:, :basis])

    send_picks()
    restrict_left()

    def finish(p, first):
        first_ref[p] = first
        return first

    for g, values in predictor(moved_ref, other_ref, star_ref, left, first_ref, late_ref, sizes, finish,
                               []):
        project(g, values, rleft_ref[...], proj_ref)
    by_face(proj_ref, faces_ref, sizes)
    payloads(faces_ref, pick_ref, pick_sub_ref, slot_ref, (pa_ref, pb_ref, p1_ref, pk_refs), sizes)
    for copy in copies[6:]:
        copy.wait()


def volume_part(values_ref, base_ref, star_ref, kleft, moved_ref, partial_ref, sizes):
    for g in groups(sizes):
        values = [values_ref[g * GROUP + i] for i in range(GROUP)]
        moved_ref[:, group_lanes(g)] = dot(kleft, stack_right(values))[: moved_ref.shape[0]]
    for g in groups(sizes):
        acc = mix_group(moved_ref, star_ref, sizes, g)
        for i in range(GROUP):
            partial_ref[g * GROUP + i] = base_ref[g * GROUP + i] + acc[i]


def interior_part(faces_ref, pick_ref, oleft, turn, gath_ref, sizes):
    rows = sizes.rows
    both = dot(faces_ref[...], pick_ref[...])
    both = both[0:rows] + both[rows : 2 * rows]
    blocks = [both[q * PAD : (q + 1) * PAD] for q in range(sizes.variables)]
    for q, block in enumerate(turn_blocks(blocks, oleft, turn)):
        gath_ref[q * PAD : (q + 1) * PAD, :] = block


def own_part(proj_ref, minus_ref, comb_ref, sizes):
    variables = sizes.variables
    for f in range(4):
        rows = slice(f * PAD, (f + 1) * PAD)
        acc = [None] * variables
        for q in range(variables):
            block = proj_ref[rows, q * 128 : (q + 1) * 128]
            for p in range(variables):
                row = (q * variables + p) * 4 + f
                term = block * minus_ref[row : row + 1, :]
                acc[p] = term if acc[p] is None else acc[p] + term
        for p in range(variables):
            comb_ref[rows, p * 128 : (p + 1) * 128] = acc[p]


def near_part(proj_ref, minus_ref, gath_ref, plus_ref, comb_ref, sizes):
    variables = sizes.variables
    for f in range(4):
        rows = slice(f * PAD, (f + 1) * PAD)
        acc = [None] * variables
        for q in range(variables):
            own = proj_ref[rows, q * 128 : (q + 1) * 128]
            other = gath_ref[q * PAD : (q + 1) * PAD, f * 128 : (f + 1) * 128]
            for p in range(variables):
                row = (q * variables + p) * 4 + f
                term = own * minus_ref[row : row + 1, :]
                acc[p] = term if acc[p] is None else acc[p] + term
                acc[p] = acc[p] + other * plus_ref[row : row + 1, :]
        for p in range(variables):
            comb_ref[rows, p * 128 : (p + 1) * 128] = acc[p]


def plus_by_slot(plus_ref, ghost_pick_ref, out_ref, sizes):
    mats = sizes.variables**2
    pieces = [pad_to(plus_ref[pl.ds(f, mats, stride=4), :], out_ref.shape[0], 128) for f in range(4)]
    high, low = split(jnp.concatenate(pieces, axis=1))
    pick = ghost_pick_ref[...]
    out_ref[...] = dot_nt(high, pick) + dot_nt(low, pick)


def kernel_local_first(sizes, *refs):
    (class_ref, minus_table, plus_table, code_ref, flux_ref, stiff_ref, lift_ref, orient_ref,
     first_ref, state_ref, star_ref, proj_ref, faces_ref,
     partial_ref, gath_ref, comb_ref, minus_ref, plus_ref, kleft_ref, oleft_ref, lleft_ref, llow_ref,
     pick_ref, ghost_pick_ref, turn_ref, ghost_turn_ref, moved_ref, stage_ref, lstage_ref) = refs
    basis = sizes.basis
    kleft_ref[...] = stack_left(jnp.reshape(stiff_ref[...], (3 * basis, basis)))
    volume_part(first_ref, state_ref, star_ref, kleft_ref[...], moved_ref, partial_ref, sizes)
    lookup(minus_table, stage_ref, class_ref[...], minus_ref)
    oleft_ref[...] = orient_left(orient_ref)
    code = code_ref[...]
    flux = flux_ref[...]
    face = face_of(flux)
    turn = flux - 3 * face
    turn_row = jnp.concatenate([turn[f : f + 1, :] for f in range(4)], axis=1)
    turn_ref[...] = turn_row
    place = lax.broadcasted_iota(I32, (128, 128), 0)
    target = jnp.where(code < 128, face * 128 + code, -1)
    for f in range(4):
        for j in range(4):
            pick_ref[j * 128 : (j + 1) * 128, f * 128 : (f + 1) * 128] = (
                (place + j * 128 == target[f : f + 1, :]).astype(F32).astype(BF16)
            )
    slot = code - 128
    swapped = jnp.where(slot < CAP_DOM, slot + CAP_DOM, slot - CAP_DOM)
    dom_slot = jnp.where(is_even(), swapped, slot)
    dom_slot = jnp.where(dom_slot < CAP_DOM, dom_slot, dom_slot + CAP_DOM)
    slot = jnp.where(slot < 2 * CAP_DOM, dom_slot, slot + CAP_DOM)
    slot = jnp.where(jnp.logical_or(code < 128, code >= 128 + sizes.ghosts), -1, slot)
    for f in range(4):
        for j in range(2):
            ghost_pick_ref[j * 128 : (j + 1) * 128, f * 128 : (f + 1) * 128] = (
                (place + j * 128 == slot[f : f + 1, :]).astype(F32).astype(BF16)
            )
    rows = jnp.broadcast_to(turn_row.astype(F32), (16, 512)).astype(BF16)
    ghost_turn_ref[...] = dot_nt(rows, ghost_pick_ref[...])[0:1].astype(I32)
    interior_part(faces_ref, pick_ref, oleft_ref[...], turn_row, gath_ref, sizes)
    lookup(plus_table, stage_ref, class_ref[...], plus_ref)
    own_part(proj_ref, minus_ref, comb_ref, sizes)
    lstage_ref[...] = jnp.zeros_like(lstage_ref)
    for f in range(4):
        lstage_ref[f * PAD : f * PAD + lift_ref.shape[0], :basis] = lift_ref[:, f, :]
    wide = jnp.transpose(lstage_ref[...], (1, 0))[:64]
    high = wide.astype(BF16).astype(F32)
    low = wide - high
    rolled = pltpu.roll(high, 4 * PAD, 1)
    lane = lax.broadcasted_iota(I32, (64, 128), 1)
    lleft_ref[:, 0:128] = jnp.where(lane < 4 * PAD, high, rolled).astype(BF16)
    lleft_ref[:, 128:256] = jnp.where(lane < 8 * PAD - 128, rolled, 0.0).astype(BF16)
    llow_ref[...] = low.astype(BF16)


def kernel_local_second(sizes, *refs):
    (second_ref, middle_ref, star_ref, kleft_ref, proj_ref, faces_ref, minus_ref, plus_ref, oleft_ref, pick_ref,
     turn_ref, ghost_pick_ref, partial_ref, comb_ref, slot_plus_ref, moved_ref, gath_ref) = refs
    volume_part(second_ref, middle_ref, star_ref, kleft_ref[...], moved_ref, partial_ref, sizes)
    interior_part(faces_ref, pick_ref, oleft_ref[...], turn_ref[...], gath_ref, sizes)
    near_part(proj_ref, minus_ref, gath_ref, plus_ref, comb_ref, sizes)
    plus_by_slot(plus_ref, ghost_pick_ref, slot_plus_ref, sizes)


def ghost_side(received, tile, oleft_ref, ghost_turn_ref, ghost_pick_ref, slot_plus_ref, ghost_ref, comb_ref, sizes):
    variables, rows = sizes.variables, sizes.rows
    lanes = slice(tile * 128, (tile + 1) * 128)
    blocks = [received[q * PAD : (q + 1) * PAD] for q in range(variables)]
    turned = turn_blocks(blocks, oleft_ref[...], ghost_turn_ref[:, lanes])
    acc = [None] * variables
    for q in range(variables):
        for p in range(variables):
            row = q * variables + p
            term = turned[q] * slot_plus_ref[row : row + 1, lanes]
            acc[p] = term if acc[p] is None else acc[p] + term
    high, low = split(pad_to(jnp.concatenate(acc, axis=0), rows, 128))
    ghost_ref[0:rows, :] = high
    ghost_ref[rows : 2 * rows, :] = low
    both = dot(ghost_ref[...], ghost_pick_ref[lanes, :])
    out = []
    for p in range(variables):
        pieces = []
        for f in range(4):
            cols = slice(f * 128, (f + 1) * 128)
            spread = both[p * PAD : (p + 1) * PAD, cols] + both[rows + p * PAD : rows + (p + 1) * PAD, cols]
            pieces.append(comb_ref[f * PAD : (f + 1) * PAD, p * 128 : (p + 1) * 128] + spread)
        out.append(jnp.concatenate(pieces, axis=0))
    return out


def kernel_even(sizes, *refs):
    (ra_ref, oleft_ref, ghost_turn_ref, ghost_pick_ref, slot_plus_ref, comb_ref, out_ref, ghost_ref) = refs
    values = ghost_side(by_rows(ra_ref[...]), 0, oleft_ref, ghost_turn_ref, ghost_pick_ref, slot_plus_ref,
                        ghost_ref, comb_ref, sizes)
    for p in range(sizes.variables):
        out_ref[:, p * 128 : (p + 1) * 128] = values[p]


def neighbour_part(ins, oleft_ref, ghost_turn_ref, ghost_pick_ref, slot_plus_ref, comb_ref, lleft_ref, llow_ref,
                   partial_ref, slot_ref, ghost_ref, sizes):
    basis = sizes.basis
    rb_ref, r1_ref, rk_refs = ins
    received = with_subs(by_rows(rb_ref[...]), r1_ref, rk_refs, slot_ref, sizes)
    faces = ghost_side(received, 1, oleft_ref, ghost_turn_ref, ghost_pick_ref, slot_plus_ref, ghost_ref, comb_ref, sizes)
    highs, stacks = [], []
    for value in faces:
        high, low = split(value)
        highs.append(high)
        stacks.append(jnp.concatenate([high, low], axis=0))
    lifted = dot(lleft_ref[:, : 8 * PAD], jnp.concatenate(stacks, axis=1)) + dot(
        llow_ref[:, : 4 * PAD], jnp.concatenate(highs, axis=1)
    )
    for g in groups(sizes):
        yield g, [
            partial_ref[p] + lifted[:basis, p * 128 : (p + 1) * 128] for p in range(g * GROUP, (g + 1) * GROUP)
        ]


def neighbour_all(ins, oleft_ref, ghost_turn_ref, ghost_pick_ref, gath_ref, comb_ref, plus_ref, lleft_ref, llow_ref,
                   partial_ref, slot_ref, ghost_ref, gsum_ref, sizes):
    variables, basis, rows = sizes.variables, sizes.basis, sizes.rows
    ra_ref, rb_ref, r1_ref, rk_refs = ins
    received = [by_rows(ra_ref[...]), with_subs(by_rows(rb_ref[...]), r1_ref, rk_refs, slot_ref, sizes)]
    received = jnp.concatenate(received, axis=1)
    blocks = [received[q * PAD : (q + 1) * PAD] for q in range(variables)]
    turned = turn_blocks(blocks, oleft_ref[...], ghost_turn_ref[...])
    high, low = split(pad_to(jnp.concatenate(turned, axis=0), rows, turned[0].shape[1]))
    ghost_ref[0:rows, :] = high
    ghost_ref[rows : 2 * rows, :] = low
    both = dot(ghost_ref[...], ghost_pick_ref[...])
    used = variables * PAD
    gsum_ref[...] = gath_ref[...] + (both[0:used] + both[rows : rows + used])
    faces = [[] for _ in range(variables)]
    for f in range(4):
        frows = slice(f * PAD, (f + 1) * PAD)
        acc = [comb_ref[frows, p * 128 : (p + 1) * 128] for p in range(variables)]
        for q in range(variables):
            block = gsum_ref[q * PAD : (q + 1) * PAD, f * 128 : (f + 1) * 128]
            for p in range(variables):
                row = (q * variables + p) * 4 + f
                acc[p] = acc[p] + block * plus_ref[row : row + 1, :]
        for p in range(variables):
            faces[p].append(acc[p])
    highs, stacks = [], []
    for pieces in faces:
        high, low = split(jnp.concatenate(pieces, axis=0))
        highs.append(high)
        stacks.append(jnp.concatenate([high, low], axis=0))
    lifted = dot(lleft_ref[:, : 8 * PAD], jnp.concatenate(stacks, axis=1)) + dot(
        llow_ref[:, : 4 * PAD], jnp.concatenate(highs, axis=1)
    )
    for g in groups(sizes):
        yield g, [
            partial_ref[p] + lifted[:basis, p * 128 : (p + 1) * 128] for p in range(g * GROUP, (g + 1) * GROUP)
        ]


def kernel_second(sizes, *refs):
    xs = sizes.sub_count // 2 - 1
    ra_ref, rb_ref, r1_ref, *refs = refs
    rk_refs, refs = refs[:xs], refs[xs:]
    (oleft_ref, ghost_turn_ref, ghost_pick_ref, gath_ref, comb_ref, plus_ref, lleft_ref, llow_ref, partial_ref,
     star_ref, late_ref, cluster_ref, dleft_ref, rleft_ref, pick_ref, pick_sub_ref,
     middle_ref, second_ref, proj_ref, faces_ref, pa_ref, pb_ref, p1_ref, *rest) = refs
    pk_refs, rest = rest[:xs], rest[xs:]
    moved_ref, other_ref, slot_ref, pslot_ref, ghost_ref, gsum_ref = rest
    left = dleft_ref[...]
    for g, values in neighbour_all((ra_ref, rb_ref, r1_ref, rk_refs), oleft_ref, ghost_turn_ref, ghost_pick_ref,
                                    gath_ref, comb_ref, plus_ref, lleft_ref, llow_ref, partial_ref, slot_ref,
                                    ghost_ref, gsum_ref, sizes):
        moved_ref[:, group_lanes(g)] = dot(left, stack_right(values))[: moved_ref.shape[0]]
        for i in range(GROUP):
            middle_ref[g * GROUP + i] = values[i]
            second_ref[g * GROUP + i] = values[i] * HALF
    fine = cluster_ref[...] == 1

    def finish(p, first):
        value = jnp.where(fine, first, late_ref[p])
        second_ref[p] = value
        return value

    for g, values in predictor(moved_ref, other_ref, star_ref, left, second_ref, None, sizes, finish):
        project(g, values, rleft_ref[...], proj_ref)
    by_face(proj_ref, faces_ref, sizes)
    payloads(faces_ref, pick_ref, pick_sub_ref, pslot_ref, (pa_ref, pb_ref, p1_ref, pk_refs), sizes)


def kernel_last(sizes, *refs):
    xs = sizes.sub_count // 2 - 1
    rb_ref, r1_ref, *refs = refs
    rk_refs, refs = refs[:xs], refs[xs:]
    (oleft_ref, ghost_turn_ref, ghost_pick_ref, slot_plus_ref, comb_ref, lleft_ref, llow_ref, partial_ref,
     out_hbm, slot_ref, ghost_ref, out_ref, sems) = refs
    copies = []
    for g, values in neighbour_part((rb_ref, r1_ref, rk_refs), oleft_ref, ghost_turn_ref, ghost_pick_ref,
                                    slot_plus_ref, comb_ref, lleft_ref, llow_ref, partial_ref, slot_ref,
                                    ghost_ref, sizes):
        for i in range(GROUP):
            out_ref[g * GROUP + i] = values[i]
        part = pl.ds(g * GROUP, GROUP)
        copies.append(pltpu.make_async_copy(out_ref.at[part], out_hbm.at[part], sems.at[g]))
        copies[-1].start()
    for copy in copies:
        copy.wait()


def body(
    dom_count,
    sub_count,
    modal_state,
    cluster_id,
    jacobian_id,
    face_neighbour,
    flux_index,
    send_list,
    derivative,
    stiffness,
    restriction,
    lifting,
    orientation,
    star_matrix,
    flux_minus,
    flux_plus,
):
    basis, variables, elements = modal_state.shape
    ghosts = send_list.shape[0]
    cap_sub = (ghosts - 2 * CAP_DOM) // sub_count
    lanes = variables * elements
    half_rows = -(-variables * PAD // 32) * 16
    rows = 2 * half_rows
    sizes = Sizes(variables, basis, sub_count, cap_sub, rows, half_rows, ghosts)
    sub_lanes = -(-rows // 128) * 128
    mat_rows = variables * variables * 4 + 4
    xs = sub_count // 2 - 1

    state = jnp.transpose(modal_state, (1, 0, 2))
    star_table = jnp.transpose(star_matrix, (2, 3, 1, 0))
    minus_table = jnp.transpose(flux_minus, (2, 3, 1, 0))
    plus_table = jnp.transpose(flux_plus, (2, 3, 1, 0))
    restrict = jnp.transpose(restriction, (1, 0, 2))
    lift = jnp.transpose(lifting, (2, 0, 1))
    classes = jacobian_id.reshape(1, elements)
    clusters = cluster_id.reshape(1, elements)
    sends = send_list.reshape(1, ghosts)

    def sds(*shape, dtype=F32):
        return jax.ShapeDtypeStruct(shape, dtype)

    def like(x):
        return sds(*x.shape, dtype=x.dtype)

    whole = sds(variables, basis, elements)
    face_t = sds(4 * PAD, lanes)
    faces_t = sds(2 * rows, 4 * elements, dtype=BF16)
    mat_t = sds(mat_rows, 128)
    gath_t = sds(variables * PAD, 4 * elements)
    left_t = sds(-(-3 * basis // 16) * 16, 3 * SEC, dtype=BF16)
    pay_t = [sds(half_rows, 128)] * 2 + [sds(cap_sub * (xs + 1), sub_lanes)] + [sds(cap_sub, sub_lanes)] * xs

    def scratch(t):
        return pltpu.VMEM(t.shape, t.dtype)

    moved_s = pltpu.VMEM((3 * basis, lanes), F32)
    stage_s = pltpu.VMEM((mat_rows, 128), F32)
    slot_s = pltpu.VMEM((128, sub_lanes), F32)
    pslot_s = pltpu.VMEM((ghosts - 2 * CAP_DOM, sub_lanes), F32)
    ghost_s = pltpu.VMEM((2 * rows, 128), BF16)
    ghost_all_s = pltpu.VMEM((2 * rows, 256), BF16)
    slot_mat_t = sds(-(-variables * variables // 16) * 16, 256)

    def call(fn, outs, scratches, operands, flops, space=pltpu.VMEM, out_space=pltpu.VMEM):
        vmem = pl.BlockSpec(memory_space=out_space)
        if space is pltpu.HBM:
            operands = [pltpu.with_memory_space_constraint(x, pltpu.HBM) for x in operands]
        return pl.pallas_call(
            functools.partial(fn, sizes),
            out_shape=outs,
            in_specs=[pl.BlockSpec(memory_space=space)] * len(operands),
            out_specs=jax.tree.map(lambda _: vmem, outs),
            scratch_shapes=scratches,
            cost_estimate=pl.CostEstimate(flops=flops, bytes_accessed=2_000_000, transcendentals=0),
            compiler_params=pltpu.CompilerParams(vmem_limit_bytes=24 * 1024 * 1024),
        )(*operands)

    combined = ("dom", "sub")

    def device(d, s):
        return d * sub_count + s

    def pairs(target):
        return [(device(d, s), device(*target(d, s))) for d in range(dom_count) for s in range(sub_count)]

    even_pairs = pairs(lambda d, s: (d ^ 1, s))
    odd_pairs = pairs(lambda d, s: (((d + 1) ^ 1) - 1, s) if 0 < d < dom_count - 1 else (d, s ^ 1))

    def sub_pairs(k):
        return pairs(lambda d, s: (d, s ^ k))

    def trade(payload):
        pa, pb, p1, *pk = payload
        r1 = lax.ppermute(p1, combined, sub_pairs(1))
        ra = lax.ppermute(pa, combined, even_pairs)
        rk = []
        pb, r1 = lax.optimization_barrier((pb, r1))
        for i, part in enumerate(pk):
            passed = r1[(i + 1) * cap_sub : (i + 2) * cap_sub]
            rk.append(lax.ppermute(jnp.concatenate([part, passed], axis=0), combined, sub_pairs(2 * i + 2)))
        rb = lax.ppermute(pb, combined, odd_pairs)
        return [ra, rb, r1, *rk]

    later = [clusters, minus_table, plus_table, face_neighbour, flux_index, stiffness, lift, orientation]
    outs = call(
        kernel_predict,
        [like(x) for x in [classes, *later]]
        + [whole, whole, whole, face_t, faces_t, mat_t, left_t, sds(4 * PAD, 3 * SEC, dtype=BF16)]
        + [sds(4 * elements, 128, dtype=BF16), sds(ghosts - 2 * CAP_DOM, 4 * elements, dtype=BF16)]
        + pay_t,
        [
            scratch(star_table), scratch(derivative), scratch(restrict), scratch(sends),
            moved_s, moved_s, stage_s, pltpu.VMEM((4 * PAD, 128), F32), pslot_s, pltpu.SemaphoreType.DMA((14,)),
        ],
        [state, classes, star_table, derivative, restrict, sends, *later],
        60_000_000,
        pltpu.HBM,
    )
    clusters, minus_table, plus_table, code, flux, stiff, lift, orient = outs[1:9]
    classes = outs[0]
    state, first, late, proj, faces, star, dleft, rleft, pick_send, pick_sub, *payload = outs[9:]
    received = trade(payload)
    partial, gath, comb, minus, plus, kleft, oleft, lleft, llow, pick, ghost_pick, turn, ghost_turn = call(
        kernel_local_first,
        [whole, gath_t, face_t, mat_t, mat_t, left_t, sds(80, 3 * OSEC, dtype=BF16)]
        + [sds(64, 256, dtype=BF16), sds(64, 128, dtype=BF16)]
        + [sds(4 * elements, 4 * elements, dtype=BF16), sds(256, 4 * elements, dtype=BF16)]
        + [sds(1, 4 * elements, dtype=I32), sds(1, 256, dtype=I32)],
        [moved_s, stage_s, pltpu.VMEM((128, 128), F32)],
        [classes, minus_table, plus_table, code, flux, stiff, lift, orient, first, state, star, proj, faces],
        30_000_000,
    )
    common = [oleft, ghost_turn, ghost_pick]
    middle, second, proj, faces, *payload = call(
        kernel_second,
        [whole, whole, face_t, faces_t] + pay_t,
        [moved_s, moved_s, slot_s, pslot_s, ghost_all_s, scratch(gath_t)],
        received
        + common
        + [gath, comb, plus, lleft, llow, partial, star, late, clusters, dleft, rleft, pick_send, pick_sub],
        70_000_000,
    )
    received = trade(payload)
    partial, comb, slot_plus = call(
        kernel_local_second,
        [whole, face_t, slot_mat_t],
        [moved_s, scratch(gath_t)],
        [second, middle, star, kleft, proj, faces, minus, plus, oleft, pick, turn, ghost_pick],
        30_000_000,
    )
    common = [*common, slot_plus]
    comb = call(kernel_even, face_t, [ghost_s], [received[0], *common, comb], 3_000_000)
    result = call(
        kernel_last,
        whole,
        [slot_s, ghost_s, scratch(whole), pltpu.SemaphoreType.DMA((variables // GROUP,))],
        received[1:] + common + [comb, lleft, llow, partial],
        10_000_000,
        out_space=pltpu.HBM,
    )
    return jnp.transpose(result, (1, 0, 2))


def solution(mesh):
    placed = (
        P(None, None, ("dom", "sub")),
        P(("dom", "sub")),
        P(("dom", "sub")),
        P(None, ("dom", "sub")),
        P(None, ("dom", "sub")),
        P(("dom", "sub")),
        P(),
        P(),
        P(),
        P(),
        P(),
        P(),
        P(),
        P(),
    )
    return jax.shard_map(
        functools.partial(body, mesh.shape["dom"], mesh.shape["sub"]),
        mesh=mesh,
        in_specs=placed,
        out_specs=P(None, None, ("dom", "sub")),
        check_vma=False,
    )
```

```python
import collections
import functools

import jax
import jax.numpy as jnp
from jax import lax
from jax.experimental import pallas as pl
from jax.experimental.pallas import tpu as pltpu
from jax.sharding import PartitionSpec as P

ORDER = 6
CAP_DOM = 64
HALF = 0.5
PAD = 24
SEC = 64
OSEC = 32
GROUP = 3

F32 = jnp.float32
BF16 = jnp.bfloat16
I32 = jnp.int32

Sizes = collections.namedtuple(
    "Sizes", ["variables", "basis", "sub_count", "cap_sub", "rows", "half_rows", "ghosts"]
)


def split(x):
    high = x.astype(BF16)
    low = (x - high.astype(F32)).astype(BF16)
    return high, low


def dot(a, b):
    return lax.dot_general(a, b, (((1,), (0,)), ((), ())), preferred_element_type=F32)


def dot_nt(a, b):
    return lax.dot_general(a, b, (((1,), (1,)), ((), ())), preferred_element_type=F32)


def pad_to(x, rows, lanes):
    m, k = x.shape
    if lanes > k:
        x = jnp.concatenate([x, jnp.zeros((m, lanes - k), x.dtype)], axis=1)
    if rows > m:
        x = jnp.concatenate([x, jnp.zeros((rows - m, lanes), x.dtype)], axis=0)
    return x


def stack_left(matrix):
    m = -(-matrix.shape[0] // 16) * 16
    wide = pad_to(matrix, m, 128)
    high = wide.astype(BF16).astype(F32)
    low = wide - high
    both = high + pltpu.roll(high, SEC, 1)
    return jnp.concatenate([both.astype(BF16), low.astype(BF16)], axis=1)[:, : 3 * SEC]


def stack_right(blocks):
    out = []
    for x in blocks:
        high, low = split(pad_to(x, SEC, x.shape[1]))
        out.append(jnp.concatenate([high, low, high], axis=0))
    return jnp.concatenate(out, axis=1) if len(out) > 1 else out[0]


def order_after(x):
    return split(x)[1].astype(F32) * 0.0


def mix_group(moved_ref, star_ref, sizes, g, zero=None):
    basis, variables = sizes.basis, sizes.variables
    acc = [zero] * GROUP
    for q in range(variables):
        for d in range(3):
            block = moved_ref[d * basis : (d + 1) * basis, q * 128 : (q + 1) * 128]
            for i in range(GROUP):
                row = (q * variables + g * GROUP + i) * 4 + d
                term = block * star_ref[row : row + 1, :]
                acc[i] = term if acc[i] is None else acc[i] + term
    return acc


def lookup(table_ref, stage_ref, class_row, out_ref):
    nq, np_, parts, classes = table_ref.shape
    for q in range(nq):
        for p in range(np_):
            row = (q * np_ + p) * 4
            stage_ref[row : row + parts, :classes] = table_ref[q, p]
    rows = stage_ref.shape[0]
    high, low = split(stage_ref[:, :classes])
    onehot = (lax.broadcasted_iota(I32, (classes, 128), 0) == class_row).astype(F32).astype(BF16)
    out_ref[0:rows, :] = dot(high, onehot) + dot(low, onehot)


def groups(sizes):
    return range(sizes.variables // GROUP)


def group_lanes(g):
    return slice(g * GROUP * 128, (g + 1) * GROUP * 128)


def advance(src_ref, dst_ref, star_ref, left, sizes, emit, between):
    zero = None
    for g in groups(sizes):
        acc = mix_group(src_ref, star_ref, sizes, g, zero)
        zero = order_after(acc[-1])
        for i in range(GROUP):
            emit(g * GROUP + i, acc[i])
        dst_ref[:, group_lanes(g)] = dot(left, stack_right(acc))[: dst_ref.shape[0]]
        between()


def predictor(moved_ref, other_ref, star_ref, left, first_ref, late_ref, sizes, finish, extra=()):
    extra = list(extra)

    def between():
        if extra:
            extra.pop(0)()

    def weigh(weights, degree):
        w_half, w_full = weights
        scale = -1.0 / (degree + 1)
        return w_half * (scale * HALF), w_full * scale

    def emitter(weights):
        w_half, w_full = weights

        def emit(p, value):
            first_ref[p] += w_half * value
            if late_ref is not None:
                late_ref[p] += (w_full - w_half) * value

        return emit

    def two(i, weights):
        weights = weigh(weights, 2 * i + 1)
        advance(moved_ref, other_ref, star_ref, left, sizes, emitter(weights), between)
        weights = weigh(weights, 2 * i + 2)
        advance(other_ref, moved_ref, star_ref, left, sizes, emitter(weights), between)
        return weights

    steps = ORDER - 1
    weights = (HALF, 1.0)
    for i in range(steps // 2):
        weights = two(i, weights)
    w_half, w_full = weigh(weights, steps)
    for g in groups(sizes):
        acc = mix_group(moved_ref, star_ref, sizes, g)
        values = []
        for i in range(GROUP):
            p = g * GROUP + i
            first = first_ref[p] + w_half * acc[i]
            if late_ref is not None:
                late_ref[p] += (w_full - w_half) * acc[i]
            values.append(finish(p, first))
        yield g, values


def project(g, values, left, proj_ref):
    proj_ref[:, group_lanes(g)] = dot(left, stack_right(values))


def by_face(proj_ref, faces_ref, sizes):
    rows = sizes.rows
    for f in range(4):
        pieces = [
            proj_ref[f * PAD : (f + 1) * PAD, q * 128 : (q + 1) * 128] for q in range(sizes.variables)
        ]
        high, low = split(pad_to(jnp.concatenate(pieces, axis=0), rows, 128))
        faces_ref[0:rows, f * 128 : (f + 1) * 128] = high
        faces_ref[rows : 2 * rows, f * 128 : (f + 1) * 128] = low


def is_even():
    return lax.rem(lax.axis_index("dom"), 2) == 0


def low_lanes(shape):
    return lax.broadcasted_iota(I32, shape, 1) < CAP_DOM


def picks_of_sends(send_ref, pick_ref, pick_sub_ref):
    ghosts = send_ref.shape[1]
    row = send_ref[...].astype(F32)
    dom_row = row[:, 0:128]
    dom_row = jnp.where(is_even(), pltpu.roll(dom_row, CAP_DOM, 1), dom_row)
    place = lax.broadcasted_iota(I32, (128, 128), 0).astype(F32)
    for f in range(4):
        pick_ref[f * 128 : (f + 1) * 128, :] = (place + f * 128 == dom_row).astype(F32).astype(BF16)
    subs = ghosts - 128
    sub_row = pad_to(row[:, 128:], 1, 128)
    column = jnp.transpose(jnp.broadcast_to(sub_row, (128, 128)), (1, 0))[:subs]
    lane = lax.broadcasted_iota(I32, (subs, 128), 1).astype(F32)
    for f in range(4):
        pick_sub_ref[:, f * 128 : (f + 1) * 128] = (column == lane + f * 128).astype(F32).astype(BF16)


def payloads(faces_ref, pick_ref, pick_sub_ref, slot_ref, outs, sizes):
    pa_ref, pb_ref, p1_ref, pk_refs = outs
    rows, half = sizes.rows, sizes.half_rows
    sub = dot_nt(pick_sub_ref[...], faces_ref[0:rows, :]) + dot_nt(pick_sub_ref[...], faces_ref[rows : 2 * rows, :])
    slot_ref[...] = pad_to(sub, sub.shape[0], slot_ref.shape[1])
    both = dot(faces_ref[...], pick_ref[...])
    both = both[0:rows] + both[rows : 2 * rows]
    top, bottom = both[0:half], both[half:]
    low = low_lanes((half, 128))
    pa_ref[...] = jnp.where(low, top, pltpu.roll(bottom, CAP_DOM, 1))
    pb_ref[...] = jnp.where(low, pltpu.roll(top, CAP_DOM, 1), bottom)
    me = lax.axis_index("sub")
    cap = sizes.cap_sub

    def block(k):
        return slot_ref[pl.ds(pl.multiple_of(jnp.bitwise_xor(me, k) * cap, 8), cap), :]

    p1_ref[0:cap, :] = block(1)
    for i, k in enumerate(range(2, sizes.sub_count, 2)):
        p1_ref[(i + 1) * cap : (i + 2) * cap, :] = block(k + 1)
        pk_refs[i][...] = block(k)


def by_rows(received):
    return jnp.concatenate([received, pltpu.roll(received, CAP_DOM, 1)], axis=0)


def with_subs(dom, r1_ref, rk_refs, slot_ref, sizes):
    me = lax.axis_index("sub")
    cap = sizes.cap_sub
    slot_ref[...] = jnp.zeros_like(slot_ref)

    def put(k, value):
        start = pl.multiple_of(CAP_DOM + jnp.bitwise_xor(me, k) * cap, 8)
        slot_ref[pl.ds(start, cap), :] = value

    put(1, r1_ref[0:cap, :])
    for i, k in enumerate(range(2, sizes.sub_count, 2)):
        put(k, rk_refs[i][0:cap, :])
        put(k + 1, rk_refs[i][cap : 2 * cap, :])
    sub = jnp.transpose(slot_ref[...], (1, 0))[: dom.shape[0]]
    return jnp.where(low_lanes(dom.shape), dom, sub)


def turn_blocks(values, left, turns):
    stacks = []
    for value in values:
        high, low = split(pad_to(value, OSEC, value.shape[1]))
        stacks.append(jnp.concatenate([high, low, high], axis=0))
    width = values[0].shape[1]
    whole = dot(left, jnp.concatenate(stacks, axis=1))
    out = []
    for q in range(len(values)):
        turned = whole[:, q * width : (q + 1) * width]
        out.append(
            jnp.where(
                turns == 0,
                turned[0:PAD],
                jnp.where(turns == 1, turned[PAD : 2 * PAD], turned[2 * PAD : 3 * PAD]),
            )
        )
    return out


def orient_left(orient_ref):
    blocks = [pad_to(orient_ref[h], PAD, 128) for h in range(3)]
    wide = pad_to(jnp.concatenate(blocks, axis=0), 80, 128)
    high = wide.astype(BF16).astype(F32)
    low = wide - high
    stacked = high + pltpu.roll(high, OSEC, 1) + pltpu.roll(low, 2 * OSEC, 1)
    return stacked.astype(BF16)[:, : 3 * OSEC]


def face_of(flux):
    return (flux >= 3).astype(I32) + (flux >= 6).astype(I32) + (flux >= 9).astype(I32)


def kernel_predict(sizes, *refs):
    xs = sizes.sub_count // 2 - 1
    (state_hbm, class_hbm, table_hbm, deriv_hbm, restrict_hbm, send_hbm, *later_hbm) = refs[:14]
    refs = refs[14:]
    class_ref, refs = refs[0], refs[1:]
    later_refs, refs = refs[:8], refs[8:]
    (state_ref, first_ref, late_ref, proj_ref, faces_ref, star_ref, dleft_ref, rleft_ref, pick_ref, pick_sub_ref,
     pa_ref, pb_ref, p1_ref, *rest) = refs
    pk_refs, rest = rest[:xs], rest[xs:]
    (table_ref, deriv_ref, restrict_ref, send_ref, moved_ref, other_ref, stage_ref, rstage_ref, slot_ref,
     sems) = rest
    sources = [class_hbm, table_hbm, deriv_hbm, state_hbm, send_hbm, restrict_hbm, *later_hbm]
    targets = [class_ref, table_ref, deriv_ref, state_ref, send_ref, restrict_ref, *later_refs]
    copies = [pltpu.make_async_copy(s, t, sems.at[i]) for i, (s, t) in enumerate(zip(sources, targets))]
    for copy in copies:
        copy.start()
    variables, basis = sizes.variables, sizes.basis
    copies[0].wait()
    copies[1].wait()
    lookup(table_ref, stage_ref, class_ref[...], star_ref)
    copies[2].wait()
    dleft_ref[...] = stack_left(jnp.reshape(deriv_ref[...], (3 * basis, basis)))
    left = dleft_ref[...]
    copies[3].wait()
    for g in groups(sizes):
        values = [state_ref[g * GROUP + i] for i in range(GROUP)]
        moved_ref[:, group_lanes(g)] = dot(left, stack_right(values))[: moved_ref.shape[0]]
        for i in range(GROUP):
            first_ref[g * GROUP + i] = values[i] * HALF
            late_ref[g * GROUP + i] = values[i] * (1.0 - HALF)
    def send_picks():
        copies[4].wait()
        picks_of_sends(send_ref, pick_ref, pick_sub_ref)

    def restrict_left():
        copies[5].wait()
        rstage_ref[...] = jnp.zeros_like(rstage_ref)
        for f in range(4):
            rstage_ref[f * PAD : f * PAD + restrict_ref.shape[0], :basis] = restrict_ref[:, f, :]
        rleft_ref[...] = stack_left(rstage_ref[:, :basis])


    def finish(p, first):
        first_ref[p] = first
        return first

    for g, values in predictor(moved_ref, other_ref, star_ref, left, first_ref, late_ref, sizes, finish,
                               [send_picks, restrict_left]):
        project(g, values, rleft_ref[...], proj_ref)
    by_face(proj_ref, faces_ref, sizes)
    payloads(faces_ref, pick_ref, pick_sub_ref, slot_ref, (pa_ref, pb_ref, p1_ref, pk_refs), sizes)
    for copy in copies[6:]:
        copy.wait()


def volume_part(values_ref, base_ref, star_ref, kleft, moved_ref, partial_ref, sizes):
    for g in groups(sizes):
        values = [values_ref[g * GROUP + i] for i in range(GROUP)]
        moved_ref[:, group_lanes(g)] = dot(kleft, stack_right(values))[: moved_ref.shape[0]]
    for g in groups(sizes):
        acc = mix_group(moved_ref, star_ref, sizes, g)
        for i in range(GROUP):
            partial_ref[g * GROUP + i] = base_ref[g * GROUP + i] + acc[i]


def interior_part(faces_ref, pick_ref, oleft, turn, gath_ref, sizes):
    rows = sizes.rows
    both = dot(faces_ref[...], pick_ref[...])
    both = both[0:rows] + both[rows : 2 * rows]
    blocks = [both[q * PAD : (q + 1) * PAD] for q in range(sizes.variables)]
    for q, block in enumerate(turn_blocks(blocks, oleft, turn)):
        gath_ref[q * PAD : (q + 1) * PAD, :] = block


def own_part(proj_ref, minus_ref, comb_ref, sizes):
    variables = sizes.variables
    for f in range(4):
        rows = slice(f * PAD, (f + 1) * PAD)
        acc = [None] * variables
        for q in range(variables):
            block = proj_ref[rows, q * 128 : (q + 1) * 128]
            for p in range(variables):
                row = (q * variables + p) * 4 + f
                term = block * minus_ref[row : row + 1, :]
                acc[p] = term if acc[p] is None else acc[p] + term
        for p in range(variables):
            comb_ref[rows, p * 128 : (p + 1) * 128] = acc[p]


def near_part(proj_ref, minus_ref, gath_ref, plus_ref, comb_ref, sizes):
    variables = sizes.variables
    for f in range(4):
        rows = slice(f * PAD, (f + 1) * PAD)
        acc = [None] * variables
        for q in range(variables):
            own = proj_ref[rows, q * 128 : (q + 1) * 128]
            other = gath_ref[q * PAD : (q + 1) * PAD, f * 128 : (f + 1) * 128]
            for p in range(variables):
                row = (q * variables + p) * 4 + f
                term = own * minus_ref[row : row + 1, :]
                acc[p] = term if acc[p] is None else acc[p] + term
                acc[p] = acc[p] + other * plus_ref[row : row + 1, :]
        for p in range(variables):
            comb_ref[rows, p * 128 : (p + 1) * 128] = acc[p]


def plus_by_slot(plus_ref, ghost_pick_ref, out_ref, sizes):
    mats = sizes.variables**2
    pieces = [pad_to(plus_ref[pl.ds(f, mats, stride=4), :], out_ref.shape[0], 128) for f in range(4)]
    high, low = split(jnp.concatenate(pieces, axis=1))
    pick = ghost_pick_ref[...]
    out_ref[...] = dot_nt(high, pick) + dot_nt(low, pick)


def kernel_local_first(sizes, *refs):
    (class_ref, minus_table, plus_table, code_ref, flux_ref, stiff_ref, lift_ref, orient_ref,
     first_ref, state_ref, star_ref, proj_ref, faces_ref,
     partial_ref, gath_ref, comb_ref, minus_ref, plus_ref, kleft_ref, oleft_ref, lleft_ref, llow_ref,
     pick_ref, ghost_pick_ref, turn_ref, ghost_turn_ref, moved_ref, stage_ref, lstage_ref) = refs
    basis = sizes.basis
    kleft_ref[...] = stack_left(jnp.reshape(stiff_ref[...], (3 * basis, basis)))
    volume_part(first_ref, state_ref, star_ref, kleft_ref[...], moved_ref, partial_ref, sizes)
    lookup(minus_table, stage_ref, class_ref[...], minus_ref)
    oleft_ref[...] = orient_left(orient_ref)
    code = code_ref[...]
    flux = flux_ref[...]
    face = face_of(flux)
    turn = flux - 3 * face
    turn_row = jnp.concatenate([turn[f : f + 1, :] for f in range(4)], axis=1)
    turn_ref[...] = turn_row
    place = lax.broadcasted_iota(I32, (128, 128), 0)
    target = jnp.where(code < 128, face * 128 + code, -1)
    for f in range(4):
        for j in range(4):
            pick_ref[j * 128 : (j + 1) * 128, f * 128 : (f + 1) * 128] = (
                (place + j * 128 == target[f : f + 1, :]).astype(F32).astype(BF16)
            )
    slot = code - 128
    swapped = jnp.where(slot < CAP_DOM, slot + CAP_DOM, slot - CAP_DOM)
    dom_slot = jnp.where(is_even(), swapped, slot)
    dom_slot = jnp.where(dom_slot < CAP_DOM, dom_slot, dom_slot + CAP_DOM)
    slot = jnp.where(slot < 2 * CAP_DOM, dom_slot, slot + CAP_DOM)
    slot = jnp.where(jnp.logical_or(code < 128, code >= 128 + sizes.ghosts), -1, slot)
    for f in range(4):
        for j in range(2):
            ghost_pick_ref[j * 128 : (j + 1) * 128, f * 128 : (f + 1) * 128] = (
                (place + j * 128 == slot[f : f + 1, :]).astype(F32).astype(BF16)
            )
    rows = jnp.broadcast_to(turn_row.astype(F32), (16, 512)).astype(BF16)
    ghost_turn_ref[...] = dot_nt(rows, ghost_pick_ref[...])[0:1].astype(I32)
    interior_part(faces_ref, pick_ref, oleft_ref[...], turn_row, gath_ref, sizes)
    lookup(plus_table, stage_ref, class_ref[...], plus_ref)
    own_part(proj_ref, minus_ref, comb_ref, sizes)
    lstage_ref[...] = jnp.zeros_like(lstage_ref)
    for f in range(4):
        lstage_ref[f * PAD : f * PAD + lift_ref.shape[0], :basis] = lift_ref[:, f, :]
    wide = jnp.transpose(lstage_ref[...], (1, 0))[:64]
    high = wide.astype(BF16).astype(F32)
    low = wide - high
    rolled = pltpu.roll(high, 4 * PAD, 1)
    lane = lax.broadcasted_iota(I32, (64, 128), 1)
    lleft_ref[:, 0:128] = jnp.where(lane < 4 * PAD, high, rolled).astype(BF16)
    lleft_ref[:, 128:256] = jnp.where(lane < 8 * PAD - 128, rolled, 0.0).astype(BF16)
    llow_ref[...] = low.astype(BF16)


def kernel_local_second(sizes, *refs):
    (second_ref, middle_ref, star_ref, kleft_ref, proj_ref, faces_ref, minus_ref, plus_ref, oleft_ref, pick_ref,
     turn_ref, ghost_pick_ref, partial_ref, comb_ref, slot_plus_ref, moved_ref, gath_ref) = refs
    volume_part(second_ref, middle_ref, star_ref, kleft_ref[...], moved_ref, partial_ref, sizes)
    interior_part(faces_ref, pick_ref, oleft_ref[...], turn_ref[...], gath_ref, sizes)
    near_part(proj_ref, minus_ref, gath_ref, plus_ref, comb_ref, sizes)
    plus_by_slot(plus_ref, ghost_pick_ref, slot_plus_ref, sizes)


def ghost_side(received, tile, oleft_ref, ghost_turn_ref, ghost_pick_ref, slot_plus_ref, ghost_ref, comb_ref, sizes):
    variables, rows = sizes.variables, sizes.rows
    lanes = slice(tile * 128, (tile + 1) * 128)
    blocks = [received[q * PAD : (q + 1) * PAD] for q in range(variables)]
    turned = turn_blocks(blocks, oleft_ref[...], ghost_turn_ref[:, lanes])
    acc = [None] * variables
    for q in range(variables):
        for p in range(variables):
            row = q * variables + p
            term = turned[q] * slot_plus_ref[row : row + 1, lanes]
            acc[p] = term if acc[p] is None else acc[p] + term
    high, low = split(pad_to(jnp.concatenate(acc, axis=0), rows, 128))
    ghost_ref[0:rows, :] = high
    ghost_ref[rows : 2 * rows, :] = low
    both = dot(ghost_ref[...], ghost_pick_ref[lanes, :])
    out = []
    for p in range(variables):
        pieces = []
        for f in range(4):
            cols = slice(f * 128, (f + 1) * 128)
            spread = both[p * PAD : (p + 1) * PAD, cols] + both[rows + p * PAD : rows + (p + 1) * PAD, cols]
            pieces.append(comb_ref[f * PAD : (f + 1) * PAD, p * 128 : (p + 1) * 128] + spread)
        out.append(jnp.concatenate(pieces, axis=0))
    return out


def kernel_even(sizes, *refs):
    (ra_ref, oleft_ref, ghost_turn_ref, ghost_pick_ref, slot_plus_ref, comb_ref, out_ref, ghost_ref) = refs
    values = ghost_side(by_rows(ra_ref[...]), 0, oleft_ref, ghost_turn_ref, ghost_pick_ref, slot_plus_ref,
                        ghost_ref, comb_ref, sizes)
    for p in range(sizes.variables):
        out_ref[:, p * 128 : (p + 1) * 128] = values[p]


def neighbour_part(ins, oleft_ref, ghost_turn_ref, ghost_pick_ref, slot_plus_ref, comb_ref, lleft_ref, llow_ref,
                   partial_ref, slot_ref, ghost_ref, sizes):
    basis = sizes.basis
    rb_ref, r1_ref, rk_refs = ins
    received = with_subs(by_rows(rb_ref[...]), r1_ref, rk_refs, slot_ref, sizes)
    faces = ghost_side(received, 1, oleft_ref, ghost_turn_ref, ghost_pick_ref, slot_plus_ref, ghost_ref, comb_ref, sizes)
    highs, stacks = [], []
    for value in faces:
        high, low = split(value)
        highs.append(high)
        stacks.append(jnp.concatenate([high, low], axis=0))
    lifted = dot(lleft_ref[:, : 8 * PAD], jnp.concatenate(stacks, axis=1)) + dot(
        llow_ref[:, : 4 * PAD], jnp.concatenate(highs, axis=1)
    )
    for g in groups(sizes):
        yield g, [
            partial_ref[p] + lifted[:basis, p * 128 : (p + 1) * 128] for p in range(g * GROUP, (g + 1) * GROUP)
        ]


def neighbour_all(ins, oleft_ref, ghost_turn_ref, ghost_pick_ref, gath_ref, comb_ref, plus_ref, lleft_ref, llow_ref,
                   partial_ref, slot_ref, ghost_ref, gsum_ref, sizes):
    variables, basis, rows = sizes.variables, sizes.basis, sizes.rows
    ra_ref, rb_ref, r1_ref, rk_refs = ins
    received = [by_rows(ra_ref[...]), with_subs(by_rows(rb_ref[...]), r1_ref, rk_refs, slot_ref, sizes)]
    received = jnp.concatenate(received, axis=1)
    blocks = [received[q * PAD : (q + 1) * PAD] for q in range(variables)]
    turned = turn_blocks(blocks, oleft_ref[...], ghost_turn_ref[...])
    high, low = split(pad_to(jnp.concatenate(turned, axis=0), rows, turned[0].shape[1]))
    ghost_ref[0:rows, :] = high
    ghost_ref[rows : 2 * rows, :] = low
    both = dot(ghost_ref[...], ghost_pick_ref[...])
    used = variables * PAD
    gsum_ref[...] = gath_ref[...] + (both[0:used] + both[rows : rows + used])
    faces = [[] for _ in range(variables)]
    for f in range(4):
        frows = slice(f * PAD, (f + 1) * PAD)
        acc = [comb_ref[frows, p * 128 : (p + 1) * 128] for p in range(variables)]
        for q in range(variables):
            block = gsum_ref[q * PAD : (q + 1) * PAD, f * 128 : (f + 1) * 128]
            for p in range(variables):
                row = (q * variables + p) * 4 + f
                acc[p] = acc[p] + block * plus_ref[row : row + 1, :]
        for p in range(variables):
            faces[p].append(acc[p])
    highs, stacks = [], []
    for pieces in faces:
        high, low = split(jnp.concatenate(pieces, axis=0))
        highs.append(high)
        stacks.append(jnp.concatenate([high, low], axis=0))
    lifted = dot(lleft_ref[:, : 8 * PAD], jnp.concatenate(stacks, axis=1)) + dot(
        llow_ref[:, : 4 * PAD], jnp.concatenate(highs, axis=1)
    )
    for g in groups(sizes):
        yield g, [
            partial_ref[p] + lifted[:basis, p * 128 : (p + 1) * 128] for p in range(g * GROUP, (g + 1) * GROUP)
        ]


def kernel_second(sizes, *refs):
    xs = sizes.sub_count // 2 - 1
    ra_ref, rb_ref, r1_ref, *refs = refs
    rk_refs, refs = refs[:xs], refs[xs:]
    (oleft_ref, ghost_turn_ref, ghost_pick_ref, gath_ref, comb_ref, plus_ref, lleft_ref, llow_ref, partial_ref,
     star_ref, late_ref, cluster_ref, dleft_ref, rleft_ref, pick_ref, pick_sub_ref,
     middle_ref, second_ref, proj_ref, faces_ref, pa_ref, pb_ref, p1_ref, *rest) = refs
    pk_refs, rest = rest[:xs], rest[xs:]
    moved_ref, other_ref, slot_ref, pslot_ref, ghost_ref, gsum_ref = rest
    left = dleft_ref[...]
    for g, values in neighbour_all((ra_ref, rb_ref, r1_ref, rk_refs), oleft_ref, ghost_turn_ref, ghost_pick_ref,
                                    gath_ref, comb_ref, plus_ref, lleft_ref, llow_ref, partial_ref, slot_ref,
                                    ghost_ref, gsum_ref, sizes):
        moved_ref[:, group_lanes(g)] = dot(left, stack_right(values))[: moved_ref.shape[0]]
        for i in range(GROUP):
            middle_ref[g * GROUP + i] = values[i]
            second_ref[g * GROUP + i] = values[i] * HALF
    fine = cluster_ref[...] == 1

    def finish(p, first):
        value = jnp.where(fine, first, late_ref[p])
        second_ref[p] = value
        return value

    for g, values in predictor(moved_ref, other_ref, star_ref, left, second_ref, None, sizes, finish):
        project(g, values, rleft_ref[...], proj_ref)
    by_face(proj_ref, faces_ref, sizes)
    payloads(faces_ref, pick_ref, pick_sub_ref, pslot_ref, (pa_ref, pb_ref, p1_ref, pk_refs), sizes)


def kernel_last(sizes, *refs):
    xs = sizes.sub_count // 2 - 1
    rb_ref, r1_ref, *refs = refs
    rk_refs, refs = refs[:xs], refs[xs:]
    (oleft_ref, ghost_turn_ref, ghost_pick_ref, slot_plus_ref, comb_ref, lleft_ref, llow_ref, partial_ref,
     out_hbm, slot_ref, ghost_ref, out_ref, sems) = refs
    copies = []
    for g, values in neighbour_part((rb_ref, r1_ref, rk_refs), oleft_ref, ghost_turn_ref, ghost_pick_ref,
                                    slot_plus_ref, comb_ref, lleft_ref, llow_ref, partial_ref, slot_ref,
                                    ghost_ref, sizes):
        for i in range(GROUP):
            out_ref[g * GROUP + i] = values[i]
        part = pl.ds(g * GROUP, GROUP)
        copies.append(pltpu.make_async_copy(out_ref.at[part], out_hbm.at[part], sems.at[g]))
        copies[-1].start()
    for copy in copies:
        copy.wait()


def body(
    dom_count,
    sub_count,
    modal_state,
    cluster_id,
    jacobian_id,
    face_neighbour,
    flux_index,
    send_list,
    derivative,
    stiffness,
    restriction,
    lifting,
    orientation,
    star_matrix,
    flux_minus,
    flux_plus,
):
    basis, variables, elements = modal_state.shape
    ghosts = send_list.shape[0]
    cap_sub = (ghosts - 2 * CAP_DOM) // sub_count
    lanes = variables * elements
    half_rows = -(-variables * PAD // 32) * 16
    rows = 2 * half_rows
    sizes = Sizes(variables, basis, sub_count, cap_sub, rows, half_rows, ghosts)
    sub_lanes = -(-rows // 128) * 128
    mat_rows = variables * variables * 4 + 4
    xs = sub_count // 2 - 1

    state = jnp.transpose(modal_state, (1, 0, 2))
    star_table = jnp.transpose(star_matrix, (2, 3, 1, 0))
    minus_table = jnp.transpose(flux_minus, (2, 3, 1, 0))
    plus_table = jnp.transpose(flux_plus, (2, 3, 1, 0))
    restrict = jnp.transpose(restriction, (1, 0, 2))
    lift = jnp.transpose(lifting, (2, 0, 1))
    classes = jacobian_id.reshape(1, elements)
    clusters = cluster_id.reshape(1, elements)
    sends = send_list.reshape(1, ghosts)

    def sds(*shape, dtype=F32):
        return jax.ShapeDtypeStruct(shape, dtype)

    def like(x):
        return sds(*x.shape, dtype=x.dtype)

    whole = sds(variables, basis, elements)
    face_t = sds(4 * PAD, lanes)
    faces_t = sds(2 * rows, 4 * elements, dtype=BF16)
    mat_t = sds(mat_rows, 128)
    gath_t = sds(variables * PAD, 4 * elements)
    left_t = sds(-(-3 * basis // 16) * 16, 3 * SEC, dtype=BF16)
    pay_t = [sds(half_rows, 128)] * 2 + [sds(cap_sub * (xs + 1), sub_lanes)] + [sds(cap_sub, sub_lanes)] * xs

    def scratch(t):
        return pltpu.VMEM(t.shape, t.dtype)

    moved_s = pltpu.VMEM((3 * basis, lanes), F32)
    stage_s = pltpu.VMEM((mat_rows, 128), F32)
    slot_s = pltpu.VMEM((128, sub_lanes), F32)
    pslot_s = pltpu.VMEM((ghosts - 2 * CAP_DOM, sub_lanes), F32)
    ghost_s = pltpu.VMEM((2 * rows, 128), BF16)
    ghost_all_s = pltpu.VMEM((2 * rows, 256), BF16)
    slot_mat_t = sds(-(-variables * variables // 16) * 16, 256)

    def call(fn, outs, scratches, operands, flops, space=pltpu.VMEM, out_space=pltpu.VMEM):
        vmem = pl.BlockSpec(memory_space=out_space)
        if space is pltpu.HBM:
            operands = [pltpu.with_memory_space_constraint(x, pltpu.HBM) for x in operands]
        return pl.pallas_call(
            functools.partial(fn, sizes),
            out_shape=outs,
            in_specs=[pl.BlockSpec(memory_space=space)] * len(operands),
            out_specs=jax.tree.map(lambda _: vmem, outs),
            scratch_shapes=scratches,
            cost_estimate=pl.CostEstimate(flops=flops, bytes_accessed=2_000_000, transcendentals=0),
            compiler_params=pltpu.CompilerParams(vmem_limit_bytes=24 * 1024 * 1024),
        )(*operands)

    combined = ("dom", "sub")

    def device(d, s):
        return d * sub_count + s

    def pairs(target):
        return [(device(d, s), device(*target(d, s))) for d in range(dom_count) for s in range(sub_count)]

    even_pairs = pairs(lambda d, s: (d ^ 1, s))
    odd_pairs = pairs(lambda d, s: (((d + 1) ^ 1) - 1, s) if 0 < d < dom_count - 1 else (d, s ^ 1))

    def sub_pairs(k):
        return pairs(lambda d, s: (d, s ^ k))

    def trade(payload):
        pa, pb, p1, *pk = payload
        r1 = lax.ppermute(p1, combined, sub_pairs(1))
        ra = lax.ppermute(pa, combined, even_pairs)
        rk = []
        pb, r1 = lax.optimization_barrier((pb, r1))
        for i, part in enumerate(pk):
            passed = r1[(i + 1) * cap_sub : (i + 2) * cap_sub]
            rk.append(lax.ppermute(jnp.concatenate([part, passed], axis=0), combined, sub_pairs(2 * i + 2)))
        rb = lax.ppermute(pb, combined, odd_pairs)
        return [ra, rb, r1, *rk]

    later = [clusters, minus_table, plus_table, face_neighbour, flux_index, stiffness, lift, orientation]
    outs = call(
        kernel_predict,
        [like(x) for x in [classes, *later]]
        + [whole, whole, whole, face_t, faces_t, mat_t, left_t, sds(4 * PAD, 3 * SEC, dtype=BF16)]
        + [sds(4 * elements, 128, dtype=BF16), sds(ghosts - 2 * CAP_DOM, 4 * elements, dtype=BF16)]
        + pay_t,
        [
            scratch(star_table), scratch(derivative), scratch(restrict), scratch(sends),
            moved_s, moved_s, stage_s, pltpu.VMEM((4 * PAD, 128), F32), pslot_s, pltpu.SemaphoreType.DMA((14,)),
        ],
        [state, classes, star_table, derivative, restrict, sends, *later],
        60_000_000,
        pltpu.HBM,
    )
    clusters, minus_table, plus_table, code, flux, stiff, lift, orient = outs[1:9]
    classes = outs[0]
    state, first, late, proj, faces, star, dleft, rleft, pick_send, pick_sub, *payload = outs[9:]
    received = trade(payload)
    partial, gath, comb, minus, plus, kleft, oleft, lleft, llow, pick, ghost_pick, turn, ghost_turn = call(
        kernel_local_first,
        [whole, gath_t, face_t, mat_t, mat_t, left_t, sds(80, 3 * OSEC, dtype=BF16)]
        + [sds(64, 256, dtype=BF16), sds(64, 128, dtype=BF16)]
        + [sds(4 * elements, 4 * elements, dtype=BF16), sds(256, 4 * elements, dtype=BF16)]
        + [sds(1, 4 * elements, dtype=I32), sds(1, 256, dtype=I32)],
        [moved_s, stage_s, pltpu.VMEM((128, 128), F32)],
        [classes, minus_table, plus_table, code, flux, stiff, lift, orient, first, state, star, proj, faces],
        30_000_000,
    )
    common = [oleft, ghost_turn, ghost_pick]
    middle, second, proj, faces, *payload = call(
        kernel_second,
        [whole, whole, face_t, faces_t] + pay_t,
        [moved_s, moved_s, slot_s, pslot_s, ghost_all_s, scratch(gath_t)],
        received
        + common
        + [gath, comb, plus, lleft, llow, partial, star, late, clusters, dleft, rleft, pick_send, pick_sub],
        70_000_000,
    )
    received = trade(payload)
    partial, comb, slot_plus = call(
        kernel_local_second,
        [whole, face_t, slot_mat_t],
        [moved_s, scratch(gath_t)],
        [second, middle, star, kleft, proj, faces, minus, plus, oleft, pick, turn, ghost_pick],
        30_000_000,
    )
    common = [*common, slot_plus]
    comb = call(kernel_even, face_t, [ghost_s], [received[0], *common, comb], 3_000_000)
    result = call(
        kernel_last,
        whole,
        [slot_s, ghost_s, scratch(whole), pltpu.SemaphoreType.DMA((variables // GROUP,))],
        received[1:] + common + [comb, lleft, llow, partial],
        10_000_000,
        out_space=pltpu.HBM,
    )
    return jnp.transpose(result, (1, 0, 2))


def solution(mesh):
    placed = (
        P(None, None, ("dom", "sub")),
        P(("dom", "sub")),
        P(("dom", "sub")),
        P(None, ("dom", "sub")),
        P(None, ("dom", "sub")),
        P(("dom", "sub")),
        P(),
        P(),
        P(),
        P(),
        P(),
        P(),
        P(),
        P(),
    )
    return jax.shard_map(
        functools.partial(body, mesh.shape["dom"], mesh.shape["sub"]),
        mesh=mesh,
        in_specs=placed,
        out_specs=P(None, None, ("dom", "sub")),
        check_vma=False,
    )
```
